512 devices in a mesh: dp: 64 (over y_lo, z, core), graph: 8 (over x, y_hi).
Axes of the slice: x: 4, y: 8 (y_hi: 2, y_lo: 4; y = y_hi * 4 + y_lo), z: 8, core: 2. Of those that a mesh axis runs over, the one named last changes fastest.
Arguments:
- positions: float32 [64, 8, 3, 128], P('dp', 'graph'), as said below
- species: int32 [64, 8, 128], P('dp', 'graph'), may hold values from 0 to 99
- counts: int32 [64, 8], P('dp', 'graph'), may hold values from 64 to 128, as said below
- source: int32 [64, 8, 2048], P('dp', 'graph'), may hold values from 0 to 191, as said below
- target: int32 [64, 8, 2048], P('dp', 'graph'), may hold values from 0 to 127, as said below
- send_left: int32 [64, 8, 32], P('dp', 'graph'), may hold values from 0 to 31, as said below
- send_right: int32 [64, 8, 32], P('dp', 'graph'), may hold values from 32 to 127, as said below
- energy_ref: float32 [64], P('dp'), may hold values from -32 to 32
- force_ref: float32 [64, 8, 3, 128], P('dp', 'graph'), may hold values from -6 to 6
- stress_ref: float32 [64, 3, 3], P('dp'), may hold values from -3 to 3
- params: float32 [122880], P('dp')
- moment_one: float32 [122880], P('dp'), may hold values from -0.15625 to 0.15625
- moment_two: float32 [122880], P('dp'), may hold values from 1e-06 to 0.001
Outputs:
- new_params: float32 [122880], P('dp')
- new_moment_one: float32 [122880], P('dp')
- new_moment_two: float32 [122880], P('dp')
- forces: float32 [64, 8, 3, 128], P('dp', 'graph')
- energy: float32 [64], P('dp')
- stress: float32 [64, 3, 3], P('dp')
The draws below stay inside these ranges and needn't reach their ends.
Inputs may be any that keep to these rules, and one draw needn't show every extreme that they name: Slot i of a slab holds a live atom if i < counts. Some slab is full and some slab holds exactly half. Every slot is the target of exactly 16 edges; the edges of a live atom are distinct pairs with sources within 32 slots of it in the order of the cell's atoms along the first coordinate, through ghosts across slab bounds; the sources of edges to slots that are not live lie in the slab. `source`: indices into the extended list of the target's slab; a live edge never joins an atom to itself. `send_left`: A permutation of slots 0 to 31. `send_right`: A permutation of the last 32 live slots. `positions`: live atoms of a slab are ordered along the first coordinate with spacing at least half a mean spacing, slabs are 20 wide and adjacent, a cell is periodic with period 20 * 8 along it, and the other two coordinates lie in a 6 by 6 cross-section.
All inputs are finite; a program needn't handle non-finite values.
Results may differ from the reference program's by a relative error of at most 0.0003.
Values sent between devices are 32-bit elements; how exact they have to be, the bound alone decides.
No kernel may reach another device: no remote copies, remote signals or barrier semaphores. Data moves between devices by JAX's collectives and lax.ppermute only.
A program may use at most 64 MiB of HBM per device.

```python
import math
import jax
import jax.numpy as jnp
from jax import lax

C = 128
FF = 512
K = 64
NS = 100
A_DEV = 128
G = 32
R = 32
DEG = 16
STEP = 100
CELLS = 64
SLABS = 8
PARAMS = 122880


slab_width = 20.0


cross_side = 6.0


def permutations(key, length, number):
    keys = jax.random.split(key, number)
    return jax.vmap(lambda single: jax.random.permutation(single, length))(keys).astype(jnp.int32)


def edge_layout(key):
    key_count, key_left, key_right, key_offset, key_order = jax.random.split(key, 5)
    counts = jax.random.randint(key_count, (CELLS, SLABS), A_DEV // 2, A_DEV + 1).astype(jnp.int32)
    counts = counts.at[0, 0].set(A_DEV).at[0, SLABS - 1].set(A_DEV // 2)
    perm_left = permutations(key_left, G, CELLS * SLABS).reshape(CELLS, SLABS, G)
    perm_right = permutations(key_right, G, CELLS * SLABS).reshape(CELLS, SLABS, G)
    send_left = perm_left
    send_right = (counts[:, :, None] - G + perm_right).astype(jnp.int32)
    inverse_left = jnp.argsort(perm_left, axis=-1, stable=True).astype(jnp.int32)
    inverse_right = jnp.argsort(perm_right, axis=-1, stable=True).astype(jnp.int32)
    lower_inverse = jnp.roll(inverse_right, 1, axis=1)
    upper_inverse = jnp.roll(inverse_left, -1, axis=1)
    offset_table = jnp.concatenate([jnp.arange(-R, 0), jnp.arange(1, R + 1)]).astype(jnp.int32)
    picks = permutations(key_offset, 2 * R, CELLS * SLABS * A_DEV)[:, :DEG]
    offsets = offset_table[picks].reshape(CELLS, SLABS, A_DEV, DEG)
    slots = jnp.broadcast_to(jnp.arange(A_DEV, dtype=jnp.int32)[None, None, :, None], (CELLS, SLABS, A_DEV, DEG))
    near = (slots + offsets).reshape(CELLS, SLABS, A_DEV * DEG)
    slot_flat = slots.reshape(CELLS, SLABS, A_DEV * DEG)
    count_flat = counts[:, :, None]
    left_slot = jnp.take_along_axis(lower_inverse, jnp.clip(G + near, 0, G - 1), axis=2)
    right_slot = jnp.take_along_axis(upper_inverse, jnp.clip(near - count_flat, 0, G - 1), axis=2)
    source = jnp.where(near < 0, left_slot, jnp.where(near < count_flat, G + near, G + A_DEV + right_slot))
    source = jnp.where(slot_flat < count_flat, source, G + slot_flat - 1).astype(jnp.int32)
    order = permutations(key_order, A_DEV * DEG, CELLS * SLABS).reshape(CELLS, SLABS, A_DEV * DEG)
    source = jnp.take_along_axis(source, order, axis=2).astype(jnp.int32)
    target = jnp.take_along_axis(slot_flat, order, axis=2).astype(jnp.int32)
    return (counts, send_left, send_right, source, target)


def draw_counts(key, part):
    return edge_layout(key)[0]


def draw_send_left(key, part):
    return edge_layout(key)[1]


def draw_send_right(key, part):
    return edge_layout(key)[2]


def draw_source(key, part):
    return edge_layout(key)[3]


def draw_target(key, part):
    return edge_layout(key)[4]


def draw_positions(key, part):
    counts = edge_layout(key)[0]
    key = jax.random.fold_in(key, 7)
    key_x, key_yz = jax.random.split(key)
    spacing = slab_width / counts[:, :, None].astype(jnp.float32)
    slot = jnp.arange(A_DEV, dtype=jnp.float32)[None, None, :]
    start = jnp.arange(SLABS, dtype=jnp.float32)[None, :, None] * slab_width
    jitter = jax.random.uniform(key_x, (CELLS, SLABS, A_DEV), jnp.float32, -0.25, 0.25)
    first = start + (slot + 0.5 + jitter) * spacing
    others = jax.random.uniform(key_yz, (CELLS, SLABS, 2, A_DEV), jnp.float32, 0.0, cross_side)
    return jnp.concatenate([first[:, :, None, :], others], axis=2)


def draw_params(key, part):
    key = jax.random.fold_in(key, 11)
    position = jnp.arange(PARAMS, dtype=jnp.int32)
    per_shard = PARAMS // CELLS
    index = position % per_shard * CELLS + position // per_shard
    end_table = NS * C
    end_one = end_table + K * C
    end_message = end_one + 2 * C * C
    end_update = end_message + C * FF
    end_readout = end_update + FF
    scale = jnp.where(index < end_table, 1.0, jnp.where(index < end_one, 1.0, jnp.where(index < end_update, C ** (-0.5), jnp.where(index < end_readout, FF ** (-0.5), 0.02))))
    return jax.random.normal(key, (PARAMS,), jnp.float32) * scale


def with_ends(values, own_key, smallest, top_value):
    longest = values.shape.index(max(values.shape))
    spots = []
    for shift in (0, 1):
        where = [jax.random.randint(jax.random.fold_in(own_key, axis), (), 0, length) for axis, length in enumerate(values.shape)]
        where[longest] = (where[longest] + shift) % values.shape[longest]
        spots.append(tuple(where))
    return values.at[spots[0]].set(smallest).at[spots[1]].set(top_value)


def block_scale(rng, dims, shards, least, high):
    def one(dim, parts):
        draws = jax.random.uniform(jax.random.fold_in(jax.random.fold_in(rng, 6), dim), (parts,), jnp.float32, least / len(shards), high / len(shards))
        return jnp.repeat(jnp.exp(draws), dims[dim] // parts).reshape((-1,) + (1,) * (len(dims) - dim - 1))

    gain = one(*shards[0])
    for cut in shards[1:]:
        gain = gain * one(*cut)
    return gain


def noise(key, extent, scale, limit, cuts=(), kind=jnp.bfloat16):
    loudness = block_scale(key, extent, cuts, -0.22, 0.18) if cuts else 1.0
    result = jax.random.normal(key, extent, jnp.float32) * scale * loudness
    return jnp.minimum(jnp.maximum(result, -limit), limit).astype(kind)


def setup_inputs(seed: int = 0) -> dict:
    seeds = jax.random.split(jax.random.key(seed), 14)
    return {
        "positions": draw_positions(jax.random.fold_in(seeds[13], 71), 0),
        "species": with_ends(jax.random.randint(seeds[1], (CELLS, SLABS, A_DEV), 0, NS), jax.random.fold_in(seeds[1], 1), 0, NS - 1).astype(jnp.int32),
        "counts": draw_counts(jax.random.fold_in(seeds[13], 71), 0),
        "source": draw_source(jax.random.fold_in(seeds[13], 71), 0),
        "target": draw_target(jax.random.fold_in(seeds[13], 71), 0),
        "send_left": draw_send_left(jax.random.fold_in(seeds[13], 71), 0),
        "send_right": draw_send_right(jax.random.fold_in(seeds[13], 71), 0),
        "energy_ref": noise(seeds[7], (CELLS,), 5.0, 32.0, ((0, 64),), jnp.float32),
        "force_ref": noise(seeds[8], (CELLS, SLABS, 3, A_DEV), 1.0, 6.0, ((0, 64), (1, 8)), jnp.float32),
        "stress_ref": noise(seeds[9], (CELLS, 3, 3), 0.2, 3.0, ((0, 64),), jnp.float32),
        "params": draw_params(jax.random.fold_in(seeds[13], 71), 0),
        "moment_one": noise(seeds[11], (PARAMS,), 0.01, 0.15625, ((0, 64),), jnp.float32),
        "moment_two": jnp.clip(jnp.exp(math.log(0.001) - 6.9077553 * jax.random.uniform(seeds[12], (PARAMS,), jnp.float32) ** block_scale(seeds[12], (PARAMS,), ((0, 64),), -0.2, 0.2)), 9.999999974752427e-07, 0.001),
    }


highest = lax.Precision.HIGHEST
cutoff = 6.0
slab_width = 20.0
cross_area = 36.0
force_weight = 10.0
stress_weight = 100.0

def split_weights(flat):
    offset = 0
    table = flat[offset:offset + NS * C].reshape(NS, C)
    offset = offset + NS * C
    radial_one = flat[offset:offset + K * C].reshape(K, C)
    offset = offset + K * C
    radial_two = flat[offset:offset + C * C].reshape(C, C)
    offset = offset + C * C
    message_weight = flat[offset:offset + C * C].reshape(C, C)
    offset = offset + C * C
    update_weight = flat[offset:offset + C * FF].reshape(C, FF)
    offset = offset + C * FF
    readout_weight = flat[offset:offset + FF]
    return (table, radial_one, radial_two, message_weight, update_weight, readout_weight)

def to_model_order(blocked):
    return blocked.reshape(CELLS, PARAMS // CELLS).T.reshape(-1)

def to_shard_order(model_order):
    return model_order.reshape(PARAMS // CELLS, CELLS).T.reshape(-1)

def slab_energy(flat, vectors, ext_species, source, target, count):
    table, radial_one, radial_two, message_weight, update_weight, readout_weight = split_weights(flat)
    onehot = (ext_species[:, None] == jnp.arange(NS, dtype=jnp.int32)[None, :]).astype(jnp.float32)
    embedded = jnp.dot(onehot, table, precision=highest)
    dist = jnp.sqrt(lax.optimization_barrier(jnp.sum(vectors * vectors, axis=0)))
    centers = jnp.arange(K, dtype=jnp.float32) * (cutoff / (K - 1))
    spread = 0.5 * ((K - 1) / cutoff) ** 2
    basis = jnp.exp(-spread * (dist[:, None] - centers[None, :]) ** 2)
    ratio = jnp.minimum(dist / cutoff, 1.0)
    envelope = (1.0 - ratio * ratio) ** 2
    live_edge = (target < count).astype(jnp.float32)
    inner = jax.nn.silu(jnp.dot(basis, radial_one, precision=highest))
    filtered = jnp.dot(inner, radial_two, precision=highest) * (envelope * live_edge)[:, None]
    projected = jnp.dot(embedded, message_weight, precision=highest)
    messages = filtered * projected[source]
    summed = jax.ops.segment_sum(messages, target, num_segments=A_DEV)
    hidden = embedded[G:G + A_DEV] + summed * (1.0 / DEG)
    normed = hidden * lax.rsqrt(lax.optimization_barrier(jnp.mean(hidden * hidden, axis=-1, keepdims=True)) + 1e-05)
    activated = jax.nn.silu(jnp.dot(normed, update_weight, precision=highest))
    atom_energy = jnp.dot(activated, readout_weight, precision=highest)
    live_atom = (jnp.arange(A_DEV, dtype=jnp.int32) < count).astype(jnp.float32)
    return jnp.sum(atom_energy * live_atom)

def take_cols(data, index):
    return jnp.take_along_axis(data, index[:, None, :], axis=2)

def one_cell(flat, positions_c, species_c, counts_c, source_c, target_c, left_c, right_c, eref, fref, sref):
    slabs = positions_c.shape[0]
    box = slabs * slab_width
    volume = box * cross_area
    packed = jnp.concatenate([positions_c, species_c[:, None, :].astype(jnp.float32)], axis=1)
    outgoing = jnp.concatenate([take_cols(packed, left_c), take_cols(packed, right_c)], axis=2)
    from_left = jnp.roll(outgoing[:, :, G:], 1, axis=0)
    from_right = jnp.roll(outgoing[:, :, :G], -1, axis=0)
    ranks = jnp.arange(slabs)
    from_left = from_left.at[:, 0, :].add(jnp.where(ranks == 0, -box, 0.0)[:, None])
    from_right = from_right.at[:, 0, :].add(jnp.where(ranks == slabs - 1, box, 0.0)[:, None])
    ext_pos = jnp.concatenate([from_left[:, :3], positions_c, from_right[:, :3]], axis=2)
    ext_species = jnp.concatenate([from_left[:, 3], species_c.astype(jnp.float32), from_right[:, 3]], axis=1).astype(jnp.int32)
    vectors = take_cols(ext_pos, source_c) - take_cols(ext_pos, target_c + G)

    def slope_all(weights):
        return jax.vmap(jax.value_and_grad(slab_energy, argnums=1), in_axes=(None, 0, 0, 0, 0, 0))(weights, vectors, ext_species, source_c, target_c, counts_c)
    (energy_parts, slopes), pull = jax.vjp(slope_all, flat)
    energy = jnp.sum(energy_parts)
    stress = jnp.einsum('sie,sje->ij', slopes, vectors, precision=highest) / volume

    def spread_slopes(slope, src, dst):
        zero = jnp.zeros((3, A_DEV + 2 * G), jnp.float32)
        return zero.at[:, src].add(slope).at[:, dst + G].add(-slope)
    contrib = jax.vmap(spread_slopes)(slopes, source_c, target_c)
    back = jnp.concatenate([contrib[:, :, :G], contrib[:, :, G + A_DEV:]], axis=2)
    returned_left = jnp.roll(back[:, :, G:], 1, axis=0)
    returned_right = jnp.roll(back[:, :, :G], -1, axis=0)

    def collect(base, left_idx, right_idx, first, second):
        return base.at[:, left_idx].add(first).at[:, right_idx].add(second)
    grad_pos = jax.vmap(collect)(contrib[:, :, G:G + A_DEV], left_c, right_c, returned_left, returned_right)
    forces = -grad_pos
    scale = 2.0 / (slabs * A_DEV)
    live = jnp.arange(A_DEV, dtype=jnp.int32)[None, :] < counts_c[:, None]
    force_cot = jnp.where(live[:, None, :], force_weight * scale * (forces - fref), 0.0)
    sent_cot = jnp.concatenate([take_cols(force_cot, left_c), take_cols(force_cot, right_c)], axis=2)
    ext_cot = jnp.concatenate([jnp.roll(sent_cot[:, :, G:], 1, axis=0), force_cot, jnp.roll(sent_cot[:, :, :G], -1, axis=0)], axis=2)
    stress_cot = 2.0 * stress_weight * (stress - sref)
    slope_cot = -(take_cols(ext_cot, source_c) - take_cols(ext_cot, target_c + G))
    slope_cot = slope_cot + jnp.einsum('ij,sje->sie', stress_cot, vectors, precision=highest) / volume
    energy_cot = jnp.zeros((slabs,), jnp.float32) + (energy - eref) * scale
    grad = pull((energy_cot, slope_cot))[0]
    return (forces, energy, stress, grad)

def reference(positions, species, counts, source, target, send_left, send_right, energy_ref, force_ref, stress_ref, params, moment_one, moment_two):
    model_params = to_model_order(params)

    def step_cell(total, items):
        forces, energy, stress, grad = one_cell(model_params, *items)
        return (total + grad, (forces, energy, stress))
    start = jnp.zeros(params.shape, jnp.float32)
    grad_model, (forces, energy, stress) = lax.scan(step_cell, start, (positions, species, counts, source, target, send_left, send_right, energy_ref, force_ref, stress_ref))
    grad = to_shard_order(grad_model)
    new_moment_one = 0.9 * moment_one + 0.1 * grad
    new_moment_two = 0.999 * moment_two + 0.001 * grad * grad
    corrected_one = new_moment_one / (1.0 - 0.9 ** STEP)
    corrected_two = new_moment_two / (1.0 - 0.999 ** STEP)
    new_params = params - 0.001 * (corrected_one / (jnp.sqrt(corrected_two) + 1e-08) + 0.01 * params)
    return (new_params, new_moment_one, new_moment_two, forces, energy, stress)
```

```python
import jax
import jax.numpy as jnp
from jax import lax
from jax.sharding import PartitionSpec as P

C = 128
FF = 512
K = 64
NS = 100
A_DEV = 128
G = 32
DEG = 16
STEP = 100


highest = lax.Precision.HIGHEST
cutoff = 6.0
slab_width = 20.0
cross_area = 36.0
force_weight = 10.0
stress_weight = 100.0


def with_halo(cells, sides, width):
    for axis, dim in sides:
        count = lax.axis_size(axis)
        head = lax.slice_in_dim(cells, 0, width, axis=dim)
        tail = lax.slice_in_dim(cells, cells.shape[dim] - width, cells.shape[dim], axis=dim)
        cells = jnp.concatenate(
            [
                lax.ppermute(tail, axis, [(i, (i + 1) % count) for i in range(count)]),
                cells,
                lax.ppermute(head, axis, [((i + 1) % count, i) for i in range(count)]),
            ],
            axis=dim,
        )
    return cells


def split_weights(flat):
    offset = 0
    table = flat[offset : offset + NS * C].reshape(NS, C)
    offset = offset + NS * C
    radial_one = flat[offset : offset + K * C].reshape(K, C)
    offset = offset + K * C
    radial_two = flat[offset : offset + C * C].reshape(C, C)
    offset = offset + C * C
    message_weight = flat[offset : offset + C * C].reshape(C, C)
    offset = offset + C * C
    update_weight = flat[offset : offset + C * FF].reshape(C, FF)
    offset = offset + C * FF
    readout_weight = flat[offset : offset + FF]
    return (table, radial_one, radial_two, message_weight, update_weight, readout_weight)


def slab_energy(flat, vectors, ext_species, source, target, count):
    table, radial_one, radial_two, message_weight, update_weight, readout_weight = split_weights(
        flat
    )
    onehot = (ext_species[:, None] == jnp.arange(NS, dtype=jnp.int32)[None, :]).astype(jnp.float32)
    embedded = jnp.dot(onehot, table, precision=highest)
    dist = jnp.sqrt(jnp.sum(vectors * vectors, axis=0))
    centers = jnp.arange(K, dtype=jnp.float32) * (cutoff / (K - 1))
    spread = 0.5 * ((K - 1) / cutoff) ** 2
    basis = jnp.exp(-spread * (dist[:, None] - centers[None, :]) ** 2)
    ratio = jnp.minimum(dist / cutoff, 1.0)
    envelope = (1.0 - ratio * ratio) ** 2
    live_edge = (target < count).astype(jnp.float32)
    inner = jax.nn.silu(jnp.dot(basis, radial_one, precision=highest))
    filtered = jnp.dot(inner, radial_two, precision=highest) * (envelope * live_edge)[:, None]
    projected = jnp.dot(embedded, message_weight, precision=highest)
    messages = filtered * projected[source]
    summed = jax.ops.segment_sum(messages, target, num_segments=A_DEV)
    hidden = embedded[G : G + A_DEV] + summed * (1.0 / DEG)
    normed = hidden * lax.rsqrt(jnp.mean(hidden * hidden, axis=-1, keepdims=True) + 1e-05)
    activated = jax.nn.silu(jnp.dot(normed, update_weight, precision=highest))
    atom_energy = jnp.dot(activated, readout_weight, precision=highest)
    live_atom = (jnp.arange(A_DEV, dtype=jnp.int32) < count).astype(jnp.float32)
    return jnp.sum(atom_energy * live_atom)


def body(
    positions,
    species,
    counts,
    source,
    target,
    send_left,
    send_right,
    energy_ref,
    force_ref,
    stress_ref,
    params,
    moment_one,
    moment_two,
):
    shards = lax.axis_size("dp")
    spread = jnp.broadcast_to(params[None], (shards, params.shape[0]))
    gathered = lax.all_to_all(spread, "dp", 0, 0, tiled=True)
    flat = gathered.T.reshape(-1)
    place = positions[0, 0]
    kinds = species[0, 0]
    count = counts[0, 0]
    src = source[0, 0]
    dst = target[0, 0]
    left_list = send_left[0, 0]
    right_list = send_right[0, 0]
    ghosts = left_list.shape[0]
    slots = place.shape[1]
    rank = lax.axis_index("graph")
    slabs = lax.axis_size("graph")
    box = slabs * slab_width
    volume = box * cross_area
    packed = jnp.concatenate([place, kinds[None, :].astype(jnp.float32)], axis=0)
    outgoing = jnp.concatenate([packed[:, left_list], packed[:, right_list]], axis=1)
    extended = with_halo(outgoing, (("graph", 1),), ghosts)
    row_mask = (jnp.arange(4) == 0).astype(jnp.float32)[:, None]
    from_left = extended[:, :ghosts] + row_mask * jnp.where(rank == 0, -box, 0.0)
    from_right = extended[:, 3 * ghosts :] + row_mask * jnp.where(rank == slabs - 1, box, 0.0)
    ext_pos = jnp.concatenate([from_left[:3], place, from_right[:3]], axis=1)
    ext_species = jnp.concatenate([from_left[3], kinds.astype(jnp.float32), from_right[3]]).astype(
        jnp.int32
    )
    vectors = ext_pos[:, src] - ext_pos[:, dst + ghosts]

    def slope_fn(weights):
        return jax.value_and_grad(slab_energy, argnums=1)(
            weights, vectors, ext_species, src, dst, count
        )

    (energy_part, slopes), pull = jax.vjp(slope_fn, flat)
    stress_part = jnp.einsum("ie,je->ij", slopes, vectors, precision=highest)
    sums = jnp.concatenate([stress_part.reshape(-1), energy_part[None]])
    sums = jnp.sum(
        lax.all_to_all(jnp.broadcast_to(sums, (slabs, 10)), "graph", 0, 0, tiled=True), axis=0
    )
    energy = sums[9]
    stress_total = sums[:9].reshape(3, 3)
    stress = stress_total / volume
    contrib = (
        jnp.zeros((3, slots + 2 * ghosts), jnp.float32)
        .at[:, src]
        .add(slopes)
        .at[:, dst + ghosts]
        .add(-slopes)
    )
    back = jnp.concatenate([contrib[:, :ghosts], contrib[:, ghosts + slots :]], axis=1)
    returned = with_halo(back, (("graph", 1),), ghosts)
    grad_pos = contrib[:, ghosts : ghosts + slots].at[:, left_list].add(returned[:, :ghosts])
    grad_pos = grad_pos.at[:, right_list].add(returned[:, 3 * ghosts :])
    forces = -grad_pos
    scale = 2.0 / (slabs * slots)
    live = jnp.arange(slots, dtype=jnp.int32) < count
    force_cot = jnp.where(live[None, :], force_weight * scale * (forces - force_ref[0, 0]), 0.0)
    sent_cot = jnp.concatenate([force_cot[:, left_list], force_cot[:, right_list]], axis=1)
    beside_all = with_halo(sent_cot, (("graph", 1),), ghosts)
    ext_cot = jnp.concatenate(
        [beside_all[:, :ghosts], force_cot, beside_all[:, 3 * ghosts :]], axis=1
    )
    stress_cot = 2.0 * stress_weight * (stress - stress_ref[0])
    slope_cot = -(ext_cot[:, src] - ext_cot[:, dst + ghosts])
    slope_cot = slope_cot + jnp.dot(stress_cot, vectors, precision=highest) / volume
    energy_cot = (energy - energy_ref[0]) * scale
    grad_model = pull((energy_cot, slope_cot))[0]
    grad_rows = grad_model.reshape(-1, shards).T
    within = jnp.sum(lax.all_to_all(grad_rows, "dp", 0, 0, tiled=True), axis=0)
    spread = jnp.broadcast_to(within[None], (slabs, within.shape[0]))
    grad = jnp.sum(lax.all_to_all(spread, "graph", 0, 0, tiled=True), axis=0)
    new_moment_one = 0.9 * moment_one + 0.1 * grad
    new_moment_two = 0.999 * moment_two + 0.001 * grad * grad
    corrected_one = new_moment_one / (1.0 - 0.9**STEP)
    corrected_two = new_moment_two / (1.0 - 0.999**STEP)
    new_params = params - 0.001 * (
        corrected_one / (jnp.sqrt(corrected_two) + 1e-08) + 0.01 * params
    )
    return (
        new_params,
        new_moment_one,
        new_moment_two,
        forces[None, None],
        energy[None],
        stress[None],
    )


def solution(mesh):
    in_specs = (
        P("dp", "graph", None, None),
        P("dp", "graph", None),
        P("dp", "graph"),
        P("dp", "graph", None),
        P("dp", "graph", None),
        P("dp", "graph", None),
        P("dp", "graph", None),
        P("dp"),
        P("dp", "graph", None, None),
        P("dp", None, None),
        P("dp"),
        P("dp"),
        P("dp"),
    )
    out_specs = (
        P("dp"),
        P("dp"),
        P("dp"),
        P("dp", "graph", None, None),
        P("dp"),
        P("dp", None, None),
    )
    return jax.shard_map(body, mesh=mesh, in_specs=in_specs, out_specs=out_specs, check_vma=False)
```

```python
import functools
import jax
import jax.numpy as jnp
from jax import lax
from jax.experimental import pallas as pl
from jax.experimental.pallas import tpu as pltpu
from jax.sharding import PartitionSpec as P

C = 128
FF = 512
K = 64
NS = 100
A = 128
G = 32
DEG = 16
STEP = 100
E = A * DEG
N = A + 2 * G
EC = 512
CHUNKS = E // EC
BLOCKS = 16

highest = lax.Precision.HIGHEST
cutoff = 6.0
slab_width = 20.0
cross_area = 36.0
force_weight = 10.0
stress_weight = 100.0
spread = 0.5 * ((K - 1) / cutoff) ** 2

f32 = jnp.float32
bf16 = jnp.bfloat16
NN = ((1,), (0,))
NT = ((1,), (1,))


def split(x):
    high = x.astype(bf16)
    return high, (x - high.astype(f32)).astype(bf16)


def mm(a, b, dims):
    return lax.dot_general(a, b, (dims, ((), ())), preferred_element_type=f32)


def dot3(a, b, dims):
    return mm(a[0], b[0], dims) + mm(a[0], b[1], dims) + mm(a[1], b[0], dims)


def dot2(a, onehot, dims):
    return mm(a[0], onehot, dims) + mm(a[1], onehot, dims)


def exact(x):
    one = x.astype(bf16).astype(f32)
    two = (x - one).astype(bf16).astype(f32)
    return jnp.concatenate([one, two, x - one - two], axis=0).astype(bf16)


def whole(x):
    return x[0:8] + x[8:16] + x[16:24]


def full_dot(a, b, dims):
    return lax.dot_general(a, b, (dims, ((), ())), precision=highest, preferred_element_type=f32)


def iota(shape, dim):
    return lax.broadcasted_iota(jnp.int32, shape, dim)


def select_lists(lists):
    return (iota((A, 128), 0) == lists).astype(f32)


def send_kernel(own, lists, out):
    out[...] = full_dot(own[...], select_lists(lists[...]), NN)


def weight(wg, first):
    return jnp.concatenate([wg[:, first, :], wg[:, first + 1, :]], axis=0)


def update_weight_t(wg):
    return jnp.concatenate([wg[:, 7 + h, :] for h in range(8)], axis=0)


def readout_column(wg):
    block = wg[:, 15, :]
    return jnp.concatenate([block[:, h : h + 1] for h in range(8)], axis=0)


def radial_one_t(wg):
    block = wg[:, 2, :]
    return jnp.concatenate([block[:, :K], block[:, K:]], axis=0)


def silu_parts(a):
    sig = 1.0 / (1.0 + jnp.exp(-a))
    first = sig * (1.0 + a * (1.0 - sig))
    return sig, first


def silu_second(a, sig):
    return sig * (1.0 - sig) * (2.0 + a * (1.0 - 2.0 * sig))


def forward_kernel(
    scalars, wg, own, ghost, src, dst, lists,
    message, contrib_out, a_out, da_out, filt_out, dfilt_out, q_out, h_out, dn_out, dh_out,
    z_out, emb_out, vec_out, rows_out, src_hot, dst_hot, total, force_total,
):
    count = scalars[0]
    rank = scalars[1]
    slabs = scalars[2]
    box = slab_width * slabs.astype(f32)
    table_t = weight(wg, 0)
    one_t = split(radial_one_t(wg))
    two_t = split(weight(wg, 3))
    message_t = split(weight(wg, 5))
    update_f = update_weight_t(wg)
    update_t = split(update_f)
    update = split(update_f.T)
    readout = readout_column(wg)

    own_rows = own[...]
    ghost_rows = ghost[...]
    lane = iota((8, 128), 1)
    row = iota((8, 128), 0)
    shift = jnp.where(lane < G, jnp.where(rank == 0, -box, 0.0), 0.0)
    shift = shift + jnp.where((lane >= G) & (lane < 2 * G), jnp.where(rank == slabs - 1, box, 0.0), 0.0)
    ghost_pos = ghost_rows + jnp.where(row == 0, shift, 0.0)
    ext = jnp.concatenate([own_rows, ghost_pos], axis=1)
    pieces = exact(jnp.where(iota((8, 256), 0) < 3, ext, 0.0))
    kinds = ext[3:4, :].astype(jnp.int32)
    kind_hot = (iota((128, 256), 0) == kinds).astype(f32)
    table_hi, table_rest = split(table_t)
    table_lo = (table_t - table_hi.astype(f32) - table_rest.astype(f32)).astype(bf16)
    kind_bf = kind_hot.astype(bf16)
    emb = mm(table_hi, kind_bf, NN) + mm(table_rest, kind_bf, NN) + mm(table_lo, kind_bf, NN)
    emb_out[...] = emb
    projected = split(dot3(message_t, split(emb), NN))
    projected = (projected[0][:, :N], projected[1][:, :N])
    total[...] = jnp.zeros_like(total)
    centers = iota((K, EC), 0).astype(f32) * (cutoff / (K - 1))

    def first_pass(i, carry):
        at = pl.ds(pl.multiple_of(i * EC, EC), EC)
        s = src[:, at]
        t = dst[:, at]
        s = jnp.where(s < G, s + A, jnp.where(s < G + A, s - G, s))
        hot_s = (iota((N, EC), 0) == s).astype(f32).astype(bf16)
        hot_t = (iota((A, EC), 0) == t).astype(f32).astype(bf16)
        src_hot[:, at] = hot_s
        dst_hot[:, at] = hot_t
        vec = whole(mm(pieces[:, :N], hot_s, NN) - mm(pieces[:, :A], hot_t, NN))
        vec_out[:, at] = vec
        square = jnp.sum(vec * vec, axis=0, keepdims=True)
        dist = jnp.sqrt(square)
        inverse = jnp.where(square > 0.0, 1.0 / jnp.where(square > 0.0, dist, 1.0), 0.0)
        ratio = jnp.minimum(dist / cutoff, 1.0)
        live = (t < count).astype(f32)
        inside = 1.0 - ratio * ratio
        gate = inside * inside * live
        dgate = inside * ratio * (-4.0 / cutoff) * live
        rows_out[0:1, at] = dist
        rows_out[1:2, at] = inverse
        rows_out[2:3, at] = gate
        rows_out[3:4, at] = dgate
        delta = dist - centers
        basis = jnp.exp(-spread * delta * delta)
        dbasis = (-2.0 * spread) * delta * basis
        a = dot3(one_t, split(basis), NN)
        da = dot3(one_t, split(dbasis), NN)
        a_out[:, at] = a
        da_out[:, at] = da
        sig, slope = silu_parts(a)
        f = dot3(two_t, split(a * sig), NN)
        df = dot3(two_t, split(slope * da), NN)
        filt = f * gate
        dfilt = df * gate + f * dgate
        q = dot2(projected, hot_s, NN)
        filt_out[:, at] = filt
        dfilt_out[:, at] = dfilt
        q_out[:, at] = q
        total[...] += dot2(split(filt * q), hot_t, NT)
        return carry

    lax.fori_loop(0, CHUNKS, first_pass, 0)

    hidden = emb[:, :A] + total[...] * (1.0 / DEG)
    h_out[...] = hidden
    rms = lax.rsqrt(jnp.mean(hidden * hidden, axis=0, keepdims=True) + 1e-05)
    z = dot3(update_t, split(hidden * rms), NN)
    z_out[...] = z
    sig, slope = silu_parts(z)
    live_atom = (iota((1, A), 1) < count).astype(f32)
    weighted = readout * live_atom
    energy = jnp.sum(jnp.sum(weighted * (z * sig), axis=0, keepdims=True), axis=1, keepdims=True)
    dn = dot3(update, split(weighted * slope), NN)
    dn_out[...] = dn
    cube = rms * rms * rms * (1.0 / C)
    dh = rms * dn - hidden * (cube * jnp.sum(dn * hidden, axis=0, keepdims=True))
    dh_out[...] = dh
    dh_pieces = split(dh * (1.0 / DEG))
    force_total[...] = jnp.zeros_like(force_total)

    def second_pass(i, stress):
        at = pl.ds(pl.multiple_of(i * EC, EC), EC)
        hot_s = src_hot[:, at]
        hot_t = dst_hot[:, at]
        back = dot2(dh_pieces, hot_t, NN)
        along = jnp.sum(back * (dfilt_out[:, at] * q_out[:, at]), axis=0, keepdims=True)
        vec = vec_out[:, at]
        slopes = vec * (along * rows_out[1:2, at])
        three = exact(slopes)
        force_total[:, :N] += mm(three, hot_s, NT)
        force_total[:, :A] -= mm(three, hot_t, NT)
        return stress + full_dot(slopes, vec, NT)

    stress = lax.fori_loop(0, CHUNKS, second_pass, jnp.zeros((8, 8), f32))
    contrib = whole(force_total[...])
    contrib_out[...] = contrib
    lists_hot = select_lists(lists[...])
    outgoing = full_dot(contrib[:, :A], lists_hot, NN) + pltpu.roll(contrib[:, A:], 64, 1)
    to_right = (lane < G) | (lane >= 96)
    sums = jnp.zeros((8, 128), f32)
    for i in range(3):
        for j in range(3):
            sums = sums + jnp.where(lane == 3 * i + j, stress[i : i + 1, j : j + 1], 0.0)
    sums = sums + jnp.where(lane == 9, energy, 0.0)
    right = lax.rem(rank + 1, slabs)
    left = lax.rem(rank + slabs - 1, slabs)
    for d in range(8):
        keep = (to_right & (right == d)) | (jnp.logical_not(to_right) & (left == d))
        message[d] = jnp.where(row == 3, sums, jnp.where(keep, outgoing, 0.0))[:4]


def backward_kernel(
    scalars, refs, wg, own, ghost, lists, received, contrib_in, a_in, da_in, filt_in, dfilt_in,
    q_in, h_in, dn_in, dh_in, z_in, emb_in, vec_in, rows_in, src_hot, dst_hot,
    forces_out, sums_out, grad, step_row, total, source_total, one_total, two_total,
):
    count = scalars[0]
    slabs = scalars[2]
    volume = slab_width * cross_area * slabs.astype(f32)
    scale = 2.0 / (slabs.astype(f32) * A)
    two_f = weight(wg, 3)
    two = split(two_f.T)
    message_w = split(weight(wg, 5).T)
    update_f = update_weight_t(wg)
    update_t = split(update_f)
    update = split(update_f.T)
    readout = readout_column(wg)
    lists_hot = select_lists(lists[...])
    lane = iota((8, 128), 1)
    row = iota((8, 128), 0)

    got = jnp.sum(received[...], axis=0)
    got = jnp.concatenate([got, jnp.zeros_like(got)], axis=0)
    moved = jnp.where(row < 3, got, 0.0)
    energy = got[3:4, 9:10]
    inner = jnp.where(lane < 2 * G, pltpu.roll(moved, 64, 1), 0.0)
    contrib = contrib_in[...]
    force_own = -(contrib[:, :A] + full_dot(inner, lists_hot, NT))
    force_ghost = -(contrib[:, A:] + jnp.where(lane < 2 * G, moved, 0.0))
    forces_out[...] = force_own
    sums_out[...] = got
    own_ref = jnp.concatenate([own[4:8], jnp.zeros((4, 128), f32)], axis=0)
    ghost_ref = jnp.concatenate([ghost[4:8], jnp.zeros((4, 128), f32)], axis=0)
    factor = force_weight * scale
    cot_own = jnp.where((lane < count) & (row < 3), factor * (force_own - own_ref), 0.0)
    cot_ghost = jnp.where((lane < 2 * G) & (row < 3), factor * (force_ghost - ghost_ref), 0.0)
    cot = exact(jnp.concatenate([cot_own, cot_ghost], axis=1))
    stress_cot = [
        [
            (2.0 * stress_weight / volume) * (got[3:4, 3 * i + j : 3 * i + j + 1] / volume - refs[1 + 3 * i + j])
            for j in range(3)
        ]
        for i in range(3)
    ]
    energy_cot = (energy - refs[0]) * scale
    total[...] = jnp.zeros_like(total)

    def first_pass(i, carry):
        at = pl.ds(pl.multiple_of(i * EC, EC), EC)
        hot_t = dst_hot[:, at]
        vec = vec_in[:, at]
        delta = whole(mm(cot[:, :A], hot_t, NN) - mm(cot[:, :N], src_hot[:, at], NN))
        along = jnp.sum(vec * delta, axis=0, keepdims=True)
        for r in range(3):
            inner_row = sum(stress_cot[r][j] * vec[j : j + 1] for j in range(3))
            along = along + vec[r : r + 1] * inner_row
        step = along * rows_in[1:2, at]
        step_row[:, at] = step
        total[...] += dot2(split(dfilt_in[:, at] * q_in[:, at] * step), hot_t, NT)
        return carry

    lax.fori_loop(0, CHUNKS, first_pass, 0)

    hidden = h_in[...]
    dn = dn_in[...]
    dh = dh_in[...]
    z = z_in[...]
    moved_h = total[...] * (1.0 / DEG)
    rms = lax.rsqrt(jnp.mean(hidden * hidden, axis=0, keepdims=True) + 1e-05)
    cube = rms * rms * rms
    cross = jnp.mean(hidden * moved_h, axis=0, keepdims=True)
    normed = hidden * rms
    moved_n = rms * moved_h - (cube * cross) * hidden
    moved_z = dot3(update_t, split(moved_n), NN)
    sig, slope = silu_parts(z)
    live_atom = (iota((1, A), 1) < count).astype(f32)
    weighted = readout * live_atom
    z_bar = weighted * (energy_cot * slope + silu_second(z, sig) * moved_z)
    z_bar = split(z_bar)
    moved_z_bar = split(weighted * slope)
    update_grad = dot3(z_bar, split(normed), NT) + dot3(moved_z_bar, split(moved_n), NT)
    readout_grad = jnp.sum(live_atom * (energy_cot * (z * sig) + slope * moved_z), axis=1, keepdims=True)
    n_bar = dot3(update, z_bar, NN)
    dn_h = jnp.sum(dn * hidden, axis=0, keepdims=True) * (1.0 / C)
    mix = (jnp.sum(n_bar * hidden, axis=0, keepdims=True) + jnp.sum(dn * moved_h, axis=0, keepdims=True)) * (1.0 / C)
    h_bar = (
        rms * n_bar
        + hidden * (3.0 * cube * rms * rms * cross * dn_h - cube * mix)
        - moved_h * (cube * dn_h)
        - dn * (cube * cross)
    )
    for h in range(8):
        grad[:, 7 + h, :] = update_grad[64 * h : 64 * h + 64]
    lane64 = iota((64, 128), 1)
    block = jnp.zeros((64, 128), f32)
    for h in range(8):
        block = block + jnp.where(lane64 == h, readout_grad[64 * h : 64 * h + 64], 0.0)
    grad[:, 15, :] = block

    h_pieces = split(h_bar * (1.0 / DEG))
    dh_pieces = split(dh * (1.0 / DEG))
    source_total[...] = jnp.zeros_like(source_total)
    one_total[...] = jnp.zeros_like(one_total)
    two_total[...] = jnp.zeros_like(two_total)
    centers = iota((K, EC), 0).astype(f32) * (cutoff / (K - 1))

    def second_pass(i, carry):
        at = pl.ds(pl.multiple_of(i * EC, EC), EC)
        hot_s = src_hot[:, at]
        hot_t = dst_hot[:, at]
        step = step_row[:, at]
        gate = rows_in[2:3, at]
        dgate = rows_in[3:4, at]
        m_bar = dot2(h_pieces, hot_t, NN)
        dm_bar = dot2(dh_pieces, hot_t, NN)
        q = q_in[:, at]
        source_total[...] += dot2(
            split(m_bar * filt_in[:, at] + dm_bar * (dfilt_in[:, at] * step)), hot_s, NT
        )
        dq = dm_bar * q
        f_bar = split(m_bar * q * gate + dq * (dgate * step))
        df_bar = split(dq * gate)
        s_bar = dot3(two, f_bar, NN)
        ds_bar = dot3(two, df_bar, NN)
        a = a_in[:, at]
        moved_a = da_in[:, at] * step
        sig, slope = silu_parts(a)
        two_total[...] += dot3(f_bar, split(a * sig), NT) + dot3(df_bar, split(slope * moved_a), NT)
        a_bar = split(s_bar * slope + ds_bar * (silu_second(a, sig) * moved_a))
        da_bar = split(ds_bar * slope)
        delta = rows_in[0:1, at] - centers
        basis = jnp.exp(-spread * delta * delta)
        moved_basis = (-2.0 * spread) * delta * basis * step
        one_total[...] += dot3(a_bar, split(basis), NT) + dot3(da_bar, split(moved_basis), NT)
        return carry

    lax.fori_loop(0, CHUNKS, second_pass, 0)

    one_grad = one_total[...]
    grad[:, 2, :] = jnp.concatenate([one_grad[:64], one_grad[64:]], axis=1)
    two_grad = two_total[...]
    grad[:, 3, :] = two_grad[:64]
    grad[:, 4, :] = two_grad[64:]
    p_bar = source_total[...]
    p_bar = jnp.concatenate([p_bar, jnp.zeros((C, 256 - N), f32)], axis=1)
    p_pieces = split(p_bar)
    emb = emb_in[...]
    message_grad = dot3(p_pieces, split(emb), NT)
    grad[:, 5, :] = message_grad[:64]
    grad[:, 6, :] = message_grad[64:]
    emb_bar = dot3(message_w, p_pieces, NN)
    emb_bar = jnp.concatenate([emb_bar[:, :A] + h_bar, emb_bar[:, A:]], axis=1)
    kinds = jnp.concatenate([own[3:4], ghost[3:4]], axis=1).astype(jnp.int32)
    kind_hot = (iota((128, 256), 0) == kinds).astype(f32).astype(bf16)
    table_grad = dot2(split(emb_bar), kind_hot, NT)
    grad[:, 0, :] = table_grad[:64]
    grad[:, 1, :] = table_grad[64:]


vmem = pl.BlockSpec(memory_space=pltpu.VMEM)
smem = pl.BlockSpec(memory_space=pltpu.SMEM)
params_vmem = pltpu.CompilerParams(vmem_limit_bytes=56 * 1024 * 1024)


def shape(*dims, dtype=jnp.float32):
    return jax.ShapeDtypeStruct(dims, dtype)


def send(own, lists):
    return pl.pallas_call(
        send_kernel, out_shape=shape(8, 128), in_specs=[vmem] * 2, out_specs=vmem, name="halo_send"
    )(own, lists)


def forward(scalars, wg, own, ghost, src, dst, lists):
    outs = [
        shape(8, 4, 128), shape(8, 256), shape(C, E), shape(C, E), shape(C, E), shape(C, E),
        shape(C, E), shape(C, A), shape(C, A), shape(C, A), shape(FF, A), shape(C, 256),
        shape(8, E), shape(8, E), shape(N, E, dtype=bf16), shape(A, E, dtype=bf16),
    ]
    return pl.pallas_call(
        forward_kernel,
        out_shape=outs,
        in_specs=[smem] + [vmem] * 6,
        out_specs=[vmem] * len(outs),
        scratch_shapes=[pltpu.VMEM((C, A), f32), pltpu.VMEM((24, 256), f32)],
        compiler_params=params_vmem,
        name="energy_slopes",
    )(scalars, wg, own, ghost, src, dst, lists)


def backward(scalars, refs, wg, own, ghost, lists, received, kept):
    outs = [shape(8, 128), shape(8, 128), shape(64, BLOCKS, 128)]
    return pl.pallas_call(
        backward_kernel,
        out_shape=outs,
        in_specs=[smem] * 2 + [vmem] * (5 + len(kept)),
        out_specs=[vmem] * 3,
        scratch_shapes=[
            pltpu.VMEM((1, E), f32),
            pltpu.VMEM((C, A), f32),
            pltpu.VMEM((C, N), f32),
            pltpu.VMEM((C, K), f32),
            pltpu.VMEM((C, C), f32),
        ],
        compiler_params=params_vmem,
        name="weight_gradients",
    )(scalars, refs, wg, own, ghost, lists, received, *kept)


def to_blocks(x):
    two = x[:840].reshape(420, 2).T
    table = jnp.pad(two[:, :100], ((0, 0), (0, 28)))
    one = two[:, 100:164].reshape(1, 128)
    rest = jnp.pad(x[1864:], (0, 72)).reshape(1, 128)
    return jnp.concatenate(
        [table, one, two[:, 164:292], two[:, 292:420], x[840:1864].reshape(128, 8).T, rest], axis=0
    )


def from_blocks(y):
    two = jnp.concatenate([y[0:2, :100], y[2].reshape(2, 64), y[3:5], y[5:7]], axis=1)
    return jnp.concatenate([two.T.reshape(-1), y[7:15].T.reshape(-1), y[15, :56]])


def pack_own(positions, species, force_ref):
    return jnp.concatenate(
        [positions, species[None].astype(f32), force_ref, jnp.zeros((1, A), f32)], axis=0
    )


def pack_lists(send_left, send_right):
    return jnp.concatenate([send_right, send_left, jnp.full((64,), -1, jnp.int32)])[None]


def adam(params, moment_one, moment_two, grad):
    new_moment_one = 0.9 * moment_one + 0.1 * grad
    new_moment_two = 0.999 * moment_two + 0.001 * grad * grad
    corrected_one = new_moment_one / (1.0 - 0.9**STEP)
    corrected_two = new_moment_two / (1.0 - 0.999**STEP)
    new_params = params - 0.001 * (
        corrected_one / (jnp.sqrt(corrected_two) + 1e-08) + 0.01 * params
    )
    return new_params, new_moment_one, new_moment_two


def body(
    positions,
    species,
    counts,
    source,
    target,
    send_left,
    send_right,
    energy_ref,
    force_ref,
    stress_ref,
    params,
    moment_one,
    moment_two,
):
    shards = lax.axis_size("dp")
    slabs = lax.axis_size("graph")
    rank = lax.axis_index("graph")
    own = pack_own(positions[0, 0], species[0, 0], force_ref[0, 0])
    lists = pack_lists(send_left[0, 0], send_right[0, 0])
    outgoing = send(own, lists)
    lane = jnp.arange(128)[None]
    from_left = lax.ppermute(outgoing, "graph", [(i, (i + 1) % slabs) for i in range(slabs)])
    from_right = lax.ppermute(outgoing, "graph", [((i + 1) % slabs, i) for i in range(slabs)])
    blocks = jnp.broadcast_to(to_blocks(params)[None], (shards, BLOCKS, 128))
    wg = lax.all_to_all(blocks, "dp", 0, 0, tiled=True)
    ghost = jnp.where(lane < G, from_left, from_right)
    scalars = jnp.stack([counts[0, 0], rank, jnp.int32(slabs)]).astype(jnp.int32)
    refs = jnp.concatenate([energy_ref, stress_ref[0].reshape(-1)])
    message, *kept = forward(scalars, wg, own, ghost, source[0], target[0], lists)
    received = lax.all_to_all(message, "graph", 0, 0, tiled=True)
    forces, sums, grad_blocks = backward(scalars, refs, wg, own, ghost, lists, received, kept)
    volume = slabs * slab_width * cross_area
    within = jnp.sum(lax.all_to_all(grad_blocks, "dp", 0, 0, tiled=True), axis=0)
    wide = jnp.broadcast_to(within[None], (slabs, BLOCKS, 128))
    grad = from_blocks(jnp.sum(lax.all_to_all(wide, "graph", 0, 0, tiled=True), axis=0))
    new_params, new_moment_one, new_moment_two = adam(params, moment_one, moment_two, grad)
    return (
        new_params,
        new_moment_one,
        new_moment_two,
        forces[:3][None, None],
        sums[3, 9][None],
        (sums[3, :9] / volume).reshape(1, 3, 3),
    )


def solution(mesh):
    in_specs = (
        P("dp", "graph", None, None),
        P("dp", "graph", None),
        P("dp", "graph"),
        P("dp", "graph", None),
        P("dp", "graph", None),
        P("dp", "graph", None),
        P("dp", "graph", None),
        P("dp"),
        P("dp", "graph", None, None),
        P("dp", None, None),
        P("dp"),
        P("dp"),
        P("dp"),
    )
    out_specs = (
        P("dp"),
        P("dp"),
        P("dp"),
        P("dp", "graph", None, None),
        P("dp"),
        P("dp", None, None),
    )
    return jax.shard_map(body, mesh=mesh, in_specs=in_specs, out_specs=out_specs, check_vma=False)
```

```python
import functools
import jax
import jax.numpy as jnp
from jax import lax
from jax.experimental import pallas as pl
from jax.experimental.pallas import tpu as pltpu
from jax.sharding import PartitionSpec as P

C = 128
FF = 512
K = 64
NS = 100
A = 128
G = 32
DEG = 16
STEP = 100
E = A * DEG
N = A + 2 * G
EC = 1024
CHUNKS = E // EC
BLOCKS = 16
KEPT = [8, 8, C, C, C]

highest = lax.Precision.HIGHEST
cutoff = 6.0
slab_width = 20.0
cross_area = 36.0
force_weight = 10.0
stress_weight = 100.0
spread = 0.5 * ((K - 1) / cutoff) ** 2

f32 = jnp.float32
bf16 = jnp.bfloat16
NN = ((1,), (0,))
NT = ((1,), (1,))


def split(x):
    high = x.astype(bf16)
    return high, (x - high.astype(f32)).astype(bf16)


def mm(a, b, dims):
    return lax.dot_general(a, b, (dims, ((), ())), preferred_element_type=f32)


def stack(x):
    return jnp.concatenate(split(x), axis=0)


def fold_rows(x):
    half = x.shape[0] // 2
    return x[:half] + x[half:]


def fold(x):
    half = x.shape[1] // 2
    x = fold_rows(x)
    return x[:, :half] + x[:, half:]


def lhs(w):
    high, low = split(w)
    return jnp.concatenate(
        [jnp.concatenate([high, high], axis=1), jnp.concatenate([low, jnp.zeros_like(low)], axis=1)], axis=0
    )


def wdot(w, x):
    return fold_rows(mm(w, x, NN))


def wide(x):
    return jnp.concatenate(split(x), axis=1)


def twice(x):
    return jnp.concatenate([x, x], axis=0)


def exact(x):
    one = x.astype(bf16).astype(f32)
    two = (x - one).astype(bf16).astype(f32)
    return jnp.concatenate([one, two, x - one - two], axis=0).astype(bf16)


def whole(x):
    return x[0:8] + x[8:16] + x[16:24]


def full_dot(a, b, dims):
    return lax.dot_general(a, b, (dims, ((), ())), precision=highest, preferred_element_type=f32)


def iota(shape, dim):
    return lax.broadcasted_iota(jnp.int32, shape, dim)


def select_lists(lists):
    return (iota((A, 128), 0) == lists).astype(f32)


def place(pieces, stride, offset, first, last):
    lane = iota((8, 128), 1)
    row = iota((8, 128), 0)
    column = iota((128, 128), 0)
    slot = iota((128, 128), 1)
    lefts, rights = [], []
    for i in range(first, last + 1):
        chosen = [jnp.where(lane % stride == row, p[:, 128 * i : 128 * i + 128], 0.0) for p in pieces]
        lefts.append(jnp.concatenate(chosen, axis=0))
        rights.append((column // stride + (128 // stride) * i == slot + offset).astype(f32))
    return whole(
        mm(
            jnp.concatenate(lefts, axis=1).astype(bf16),
            jnp.concatenate(rights, axis=0).astype(bf16),
            NN,
        )
    )


def prepare_kernel(positions, species, force_ref, send_left, send_right, shard, own, lists, outgoing, blocks):
    own[...] = jnp.concatenate(
        [positions[...], species[...].astype(f32), force_ref[...], jnp.zeros((1, A), f32)], axis=0
    )
    lists[...] = jnp.concatenate(
        [send_right[...], send_left[...], jnp.full((1, 128 - 2 * G), -1, jnp.int32)], axis=1
    )
    outgoing[...] = full_dot(own[...], select_lists(lists[...]), NN)
    x = shard[...]
    one = x.astype(bf16).astype(f32)
    two = (x - one).astype(bf16).astype(f32)
    pieces = [one, two, x - one - two]
    table = place(pieces, 2, 0, 0, 1)
    radial = place(pieces, 2, 100, 1, 2)
    lane = iota((1, 128), 1)
    block = jnp.concatenate(
        [
            table[:2],
            jnp.where(lane < K, radial[:1], pltpu.roll(radial[1:2], K, 1)),
            place(pieces, 2, 164, 2, 4)[:2],
            place(pieces, 2, 292, 4, 6)[:2],
            place(pieces, 8, 105, 6, 14),
            jnp.where(lane < 56, pltpu.roll(x[:, 14 * 128 :], 56, 1), 0.0),
        ],
        axis=0,
    )
    for j in range(blocks.shape[0]):
        blocks[j] = block


def weight(wg, first):
    return jnp.concatenate([wg[:, first, :], wg[:, first + 1, :]], axis=0)


def update_weight_t(wg):
    return jnp.concatenate([wg[:, 7 + h, :] for h in range(8)], axis=0)


def readout_column(wg):
    block = wg[:, 15, :]
    return jnp.concatenate([block[:, h : h + 1] for h in range(8)], axis=0)


def radial_one_t(wg):
    block = wg[:, 2, :]
    return jnp.concatenate([block[:, :K], block[:, K:]], axis=0)


def silu_parts(a):
    sig = 0.5 * jnp.tanh(0.5 * a) + 0.5
    first = sig * (1.0 + a * (1.0 - sig))
    return sig, first


def silu_second(a, sig):
    return sig * (1.0 - sig) * (2.0 + a * (1.0 - 2.0 * sig))


def one_hots(s, t):
    s = jnp.where(s < G, s + A, jnp.where(s < G + A, s - G, s))
    hot_s = (iota((N, EC), 0) == s).astype(f32).astype(bf16)
    hot_t = (iota((A, EC), 0) == t).astype(f32).astype(bf16)
    return hot_s, hot_t


def forward_kernel(
    slabs, count_ref, scalars, wg, own, from_left, from_right, src, dst, lists,
    message, contrib_out, h_out, dn_out, dh_out, z_out, emb_out, *rest,
):
    large = len(KEPT)
    far, near = rest[:large], rest[large : 2 * large]
    src_hot, dst_hot, total, force_total, sems = rest[2 * large :]
    rows_out, vec_out, dfilt_out, q_out, filt_out = near
    copies = []

    count = count_ref[0, 0]
    rank = scalars[0]
    box = slab_width * slabs
    table_t = weight(wg, 0)
    one_t = lhs(radial_one_t(wg))
    two_t = lhs(weight(wg, 3))
    message_t = lhs(weight(wg, 5))
    update_f = update_weight_t(wg)
    update_t = lhs(update_f)
    update = lhs(update_f.T)
    readout = readout_column(wg)

    own_rows = own[...]
    lane = iota((8, 128), 1)
    row = iota((8, 128), 0)
    ghost_rows = jnp.where(lane < G, from_left[...], from_right[...])
    shift = jnp.where(lane < G, jnp.where(rank == 0, -box, 0.0), 0.0)
    shift = shift + jnp.where((lane >= G) & (lane < 2 * G), jnp.where(rank == slabs - 1, box, 0.0), 0.0)
    ghost_pos = ghost_rows + jnp.where(row == 0, shift, 0.0)
    ext = jnp.concatenate([own_rows, ghost_pos], axis=1)
    pieces = exact(jnp.where(iota((8, 256), 0) < 3, ext, 0.0))
    kinds = ext[3:4, :].astype(jnp.int32)
    kind_hot = (iota((128, 256), 0) == kinds).astype(f32)
    table_hi, table_rest = split(table_t)
    table_lo = (table_t - table_hi.astype(f32) - table_rest.astype(f32)).astype(bf16)
    kind_bf = kind_hot.astype(bf16)
    emb = mm(table_hi, kind_bf, NN) + mm(table_rest, kind_bf, NN) + mm(table_lo, kind_bf, NN)
    emb_out[...] = emb
    projected = stack(wdot(message_t, stack(emb)))[:, :N]
    total[...] = jnp.zeros_like(total)
    centers = iota((K, EC), 0).astype(f32) * (cutoff / (K - 1))

    for i in range(CHUNKS):
        at = pl.ds(i * EC, EC)
        t = dst[:, at]
        hot_s, hot_t = one_hots(src[:, at], t)
        src_hot[:, at] = hot_s
        dst_hot[:, at] = hot_t
        vec = whole(mm(pieces[:, :N], hot_s, NN) - mm(pieces[:, :A], hot_t, NN))
        vec_out[:, at] = vec
        square = jnp.sum(vec * vec, axis=0, keepdims=True)
        dist = jnp.sqrt(square)
        inverse = jnp.where(square > 0.0, 1.0 / jnp.where(square > 0.0, dist, 1.0), 0.0)
        ratio = jnp.minimum(dist / cutoff, 1.0)
        live = (t < count).astype(f32)
        inside = 1.0 - ratio * ratio
        gate = inside * inside * live
        dgate = inside * ratio * (-4.0 / cutoff) * live
        rows_out[0:1, at] = dist
        rows_out[1:2, at] = inverse
        rows_out[2:3, at] = gate
        rows_out[3:4, at] = dgate
        delta = dist - centers
        basis = jnp.exp(-spread * delta * delta)
        dbasis = (-2.0 * spread) * delta * basis
        a = wdot(one_t, stack(basis))
        da = wdot(one_t, stack(dbasis))
        sig, slope = silu_parts(a)
        f = wdot(two_t, stack(a * sig))
        df = wdot(two_t, stack(slope * da))
        filt = f * gate
        dfilt = df * gate + f * dgate
        q = fold_rows(mm(projected, hot_s, NN))
        filt_out[:, at] = filt
        dfilt_out[:, at] = dfilt
        q_out[:, at] = q
        total[...] += mm(stack(filt * q), hot_t, NT)
        for k in range(large):
            copy = pltpu.make_async_copy(near[k].at[:, at], far[k].at[:, at], sems.at[k, i])
            copy.start()
            copies.append(copy)

    hidden = emb[:, :A] + fold_rows(total[...]) * (1.0 / DEG)
    h_out[...] = hidden
    rms = lax.rsqrt(jnp.mean(hidden * hidden, axis=0, keepdims=True) + 1e-05)
    z = wdot(update_t, stack(hidden * rms))
    z_out[...] = z
    sig, slope = silu_parts(z)
    live_atom = (iota((1, A), 1) < count).astype(f32)
    weighted = readout * live_atom
    energy = jnp.sum(jnp.sum(weighted * (z * sig), axis=0, keepdims=True), axis=1, keepdims=True)
    dn = wdot(update, stack(weighted * slope))
    dn_out[...] = dn
    cube = rms * rms * rms * (1.0 / C)
    dh = rms * dn - hidden * (cube * jnp.sum(dn * hidden, axis=0, keepdims=True))
    dh_out[...] = dh
    dh_pieces = wide(dh * (1.0 / DEG))
    force_total[...] = jnp.zeros_like(force_total)

    stress = jnp.zeros((8, 8), f32)
    for i in range(CHUNKS):
        at = pl.ds(i * EC, EC)
        hot_s = src_hot[:, at]
        hot_t = dst_hot[:, at]
        back = mm(dh_pieces, twice(hot_t), NN)
        along = jnp.sum(back * (dfilt_out[:, at] * q_out[:, at]), axis=0, keepdims=True)
        vec = vec_out[:, at]
        slopes = vec * (along * rows_out[1:2, at])
        three = exact(slopes)
        force_total[:, :N] += mm(three, hot_s, NT)
        force_total[:, :A] -= mm(three, hot_t, NT)
        stress = stress + full_dot(slopes, vec, NT)

    contrib = whole(force_total[...])
    contrib_out[...] = contrib
    lists_hot = select_lists(lists[...])
    outgoing = full_dot(contrib[:, :A], lists_hot, NN) + pltpu.roll(contrib[:, A:], 64, 1)
    to_right = (lane < G) | (lane >= 96)
    sums = jnp.zeros((8, 128), f32)
    for i in range(3):
        for j in range(3):
            sums = sums + jnp.where(lane == 3 * i + j, stress[i : i + 1, j : j + 1], 0.0)
    sums = sums + jnp.where(lane == 9, energy, 0.0)
    right = lax.rem(rank + 1, slabs)
    left = lax.rem(rank + slabs - 1, slabs)
    for d in range(8):
        keep = (to_right & (right == d)) | (jnp.logical_not(to_right) & (left == d))
        message[d] = jnp.where(row == 3, sums, jnp.where(keep, outgoing, 0.0))[:4]
    for copy in copies:
        copy.wait()


def backward_kernel(
    slabs, count_ref, scalars, energy_ref, stress_ref, wg, own, from_left, from_right, src, dst, lists, received, contrib_in, h_in, dn_in, dh_in, z_in, emb_in, *rest,
):
    large = len(KEPT)
    far, near = rest[:large], rest[large + 4 : 2 * large + 4]
    forces_out, sums_out, keep, give = rest[large : large + 4]
    src_hot, dst_hot, grad, step_row, total, source_total, one_total, two_total, sems = rest[2 * large + 4 :]
    rows_in, vec_in, dfilt_in, q_in, filt_in = near
    copies = [pltpu.make_async_copy(far[k], near[k], sems.at[k]) for k in range(large)]
    for copy in copies:
        copy.start()

    count = count_ref[0, 0]
    core = scalars[1]
    volume = slab_width * cross_area * slabs
    scale = 2.0 / (slabs * A)
    one_t = lhs(radial_one_t(wg))
    two = lhs(weight(wg, 3).T)
    message_w = lhs(weight(wg, 5).T)
    update_f = update_weight_t(wg)
    update_t = lhs(update_f)
    update = lhs(update_f.T)
    readout = readout_column(wg)
    lists_hot = select_lists(lists[...])
    lane = iota((8, 128), 1)
    row = iota((8, 128), 0)
    ghost = jnp.where(lane < G, from_left[...], from_right[...])

    got = jnp.sum(received[...], axis=0)
    got = jnp.concatenate([got, jnp.zeros_like(got)], axis=0)
    moved = jnp.where(row < 3, got, 0.0)
    energy = got[3:4, 9:10]
    inner = jnp.where(lane < 2 * G, pltpu.roll(moved, 64, 1), 0.0)
    contrib = contrib_in[...]
    force_own = -(contrib[:, :A] + full_dot(inner, lists_hot, NT))
    force_ghost = -(contrib[:, A:] + jnp.where(lane < 2 * G, moved, 0.0))
    forces_out[...] = force_own
    sums_out[...] = got
    own_ref = jnp.concatenate([own[4:8], jnp.zeros((4, 128), f32)], axis=0)
    ghost_ref = jnp.concatenate([ghost[4:8], jnp.zeros((4, 128), f32)], axis=0)
    factor = force_weight * scale
    cot_own = jnp.where((lane < count) & (row < 3), factor * (force_own - own_ref), 0.0)
    cot_ghost = jnp.where((lane < 2 * G) & (row < 3), factor * (force_ghost - ghost_ref), 0.0)
    cot = exact(jnp.concatenate([cot_own, cot_ghost], axis=1))
    stress_cot = [
        [
            (2.0 * stress_weight / volume) * (got[3:4, 3 * i + j : 3 * i + j + 1] / volume - stress_ref[0, i, j])
            for j in range(3)
        ]
        for i in range(3)
    ]
    energy_cot = (energy - energy_ref[0]) * scale
    total[...] = jnp.zeros_like(total)

    for copy in copies[:2]:
        copy.wait()
    for i in range(CHUNKS):
        at = pl.ds(i * EC, EC)
        hot_s, hot_t = one_hots(src[:, at], dst[:, at])
        src_hot[:, at] = hot_s
        dst_hot[:, at] = hot_t
        vec = vec_in[:, at]
        delta = whole(mm(cot[:, :A], hot_t, NN) - mm(cot[:, :N], hot_s, NN))
        along = jnp.sum(vec * delta, axis=0, keepdims=True)
        for r in range(3):
            inner_row = sum(stress_cot[r][j] * vec[j : j + 1] for j in range(3))
            along = along + vec[r : r + 1] * inner_row
        step = along * rows_in[1:2, at]
        step_row[:, at] = step
    for copy in copies[2:4]:
        copy.wait()
    for i in range(CHUNKS):
        at = pl.ds(i * EC, EC)
        step = step_row[:, at]
        hot_t = dst_hot[:, at]
        total[...] += mm(stack(dfilt_in[:, at] * q_in[:, at] * step), hot_t, NT)

    hidden = h_in[...]
    dn = dn_in[...]
    dh = dh_in[...]
    z = z_in[...]
    moved_h = fold_rows(total[...]) * (1.0 / DEG)
    rms = lax.rsqrt(jnp.mean(hidden * hidden, axis=0, keepdims=True) + 1e-05)
    cube = rms * rms * rms
    cross = jnp.mean(hidden * moved_h, axis=0, keepdims=True)
    normed = hidden * rms
    moved_n = rms * moved_h - (cube * cross) * hidden
    moved_n2 = stack(moved_n)
    moved_z = wdot(update_t, moved_n2)
    sig, slope = silu_parts(z)
    live_atom = (iota((1, A), 1) < count).astype(f32)
    weighted = readout * live_atom
    z_bar = weighted * (energy_cot * slope + silu_second(z, sig) * moved_z)
    z_bar = stack(z_bar)
    update_grad = fold(
        mm(
            jnp.concatenate([z_bar, stack(weighted * slope)], axis=1),
            jnp.concatenate([stack(normed), moved_n2], axis=1),
            NT,
        )
    )
    readout_grad = jnp.sum(live_atom * (energy_cot * (z * sig) + slope * moved_z), axis=1, keepdims=True)
    n_bar = wdot(update, z_bar)
    dn_h = jnp.sum(dn * hidden, axis=0, keepdims=True) * (1.0 / C)
    mix = (jnp.sum(n_bar * hidden, axis=0, keepdims=True) + jnp.sum(dn * moved_h, axis=0, keepdims=True)) * (1.0 / C)
    h_bar = (
        rms * n_bar
        + hidden * (3.0 * cube * rms * rms * cross * dn_h - cube * mix)
        - moved_h * (cube * dn_h)
        - dn * (cube * cross)
    )
    for h in range(8):
        grad[:, 7 + h, :] = update_grad[64 * h : 64 * h + 64]
    lane64 = iota((64, 128), 1)
    block = jnp.zeros((64, 128), f32)
    for h in range(8):
        block = block + jnp.where(lane64 == h, readout_grad[64 * h : 64 * h + 64], 0.0)
    grad[:, 15, :] = block

    both_pieces = jnp.concatenate([wide(h_bar * (1.0 / DEG)), wide(dh * (1.0 / DEG))], axis=0)
    source_total[...] = jnp.zeros_like(source_total)
    one_total[...] = jnp.zeros_like(one_total)
    two_total[...] = jnp.zeros_like(two_total)
    centers = iota((K, EC), 0).astype(f32) * (cutoff / (K - 1))

    copies[4].wait()
    for i in range(CHUNKS):
        at = pl.ds(i * EC, EC)
        hot_s = src_hot[:, at]
        hot_t = dst_hot[:, at]
        step = step_row[:, at]
        gate = rows_in[2:3, at]
        dgate = rows_in[3:4, at]
        both = mm(both_pieces, twice(hot_t), NN)
        m_bar = both[:C]
        dm_bar = both[C:]
        q = q_in[:, at]
        source_total[...] += mm(
            stack(m_bar * filt_in[:, at] + dm_bar * (dfilt_in[:, at] * step)), hot_s, NT
        )
        dq = dm_bar * q
        f_bar = stack(m_bar * q * gate + dq * (dgate * step))
        df_bar = stack(dq * gate)
        s_bar = wdot(two, f_bar)
        ds_bar = wdot(two, df_bar)
        delta = rows_in[0:1, at] - centers
        basis = jnp.exp(-spread * delta * delta)
        moved_basis = (-2.0 * spread) * delta * basis * step
        basis = stack(basis)
        moved_basis = stack(moved_basis)
        a = wdot(one_t, basis)
        moved_a = wdot(one_t, moved_basis)
        sig, slope = silu_parts(a)
        two_total[...] += mm(f_bar, stack(a * sig), NT) + mm(df_bar, stack(slope * moved_a), NT)
        a_bar = stack(s_bar * slope + ds_bar * (silu_second(a, sig) * moved_a))
        da_bar = stack(ds_bar * slope)
        one_total[...] += mm(a_bar, basis, NT) + mm(da_bar, moved_basis, NT)

    one_grad = fold(one_total[...])
    grad[:, 2, :] = jnp.concatenate([one_grad[:64], one_grad[64:]], axis=1)
    two_grad = fold(two_total[...])
    grad[:, 3, :] = two_grad[:64]
    grad[:, 4, :] = two_grad[64:]
    p_bar = fold_rows(source_total[...])
    p_bar = jnp.concatenate([p_bar, jnp.zeros((C, 256 - N), f32)], axis=1)
    p_pieces = stack(p_bar)
    emb = emb_in[...]
    message_grad = fold(mm(p_pieces, stack(emb), NT))
    grad[:, 5, :] = message_grad[:64]
    grad[:, 6, :] = message_grad[64:]
    emb_bar = wdot(message_w, p_pieces)
    emb_bar = jnp.concatenate([emb_bar[:, :A] + h_bar, emb_bar[:, A:]], axis=1)
    kinds = jnp.concatenate([own[3:4], ghost[3:4]], axis=1).astype(jnp.int32)
    kind_hot = (iota((128, 256), 0) == kinds).astype(f32).astype(bf16)
    table_grad = fold_rows(mm(stack(emb_bar), kind_hot, NT))
    grad[:, 0, :] = table_grad[:64]
    grad[:, 1, :] = table_grad[64:]
    for j in range(32):
        keep[j] = grad[2 * j + core]
        give[j] = grad[2 * j + 1 - core]


vmem = pl.BlockSpec(memory_space=pltpu.VMEM)
smem = pl.BlockSpec(memory_space=pltpu.SMEM)
far = pl.BlockSpec(memory_space=pl.ANY)
params_vmem = pltpu.CompilerParams(vmem_limit_bytes=56 * 1024 * 1024)
edge_scratch = [pltpu.VMEM((rows, E), f32) for rows in KEPT]


def shape(*dims, dtype=jnp.float32):
    return jax.ShapeDtypeStruct(dims, dtype)


def prepare(positions, species, force_ref, send_left, send_right, shard, shards):
    return pl.pallas_call(
        prepare_kernel,
        out_shape=[shape(8, 128), shape(1, 128, dtype=jnp.int32), shape(8, 128), shape(shards, BLOCKS, 128)],
        in_specs=[vmem] * 6,
        out_specs=[vmem] * 4,
        compiler_params=params_vmem,
        name="prepare",
    )(positions, species, force_ref, send_left, send_right, shard)


def forward(slabs, counts, scalars, wg, own, from_left, from_right, src, dst, lists):
    outs = [
        shape(8, 4, 128), shape(8, 256), shape(C, A), shape(C, A), shape(C, A), shape(FF, A), shape(C, 256),
    ]
    return pl.pallas_call(
        functools.partial(forward_kernel, slabs),
        out_shape=outs + [shape(rows, E) for rows in KEPT],
        in_specs=[smem] * 2 + [vmem] * 7,
        out_specs=[vmem] * len(outs) + [far] * len(KEPT),
        scratch_shapes=edge_scratch
        + [
            pltpu.VMEM((N, E), bf16),
            pltpu.VMEM((A, E), bf16),
            pltpu.VMEM((2 * C, A), f32),
            pltpu.VMEM((24, 256), f32),
            pltpu.SemaphoreType.DMA((len(KEPT), CHUNKS)),
        ],
        compiler_params=params_vmem,
        name="energy_slopes",
    )(counts, scalars, wg, own, from_left, from_right, src, dst, lists)


def backward(slabs, counts, scalars, energy_ref, stress_ref, wg, own, from_left, from_right, src, dst, lists, received, kept):
    outs = [shape(8, 128), shape(8, 128), shape(32, BLOCKS, 128), shape(32, BLOCKS, 128)]
    return pl.pallas_call(
        functools.partial(backward_kernel, slabs),
        out_shape=outs,
        in_specs=[smem] * 4 + [vmem] * (8 + len(kept) - len(KEPT)) + [far] * len(KEPT),
        out_specs=[vmem] * 4,
        scratch_shapes=edge_scratch
        + [
            pltpu.VMEM((N, E), bf16),
            pltpu.VMEM((A, E), bf16),
            pltpu.VMEM((64, BLOCKS, 128), f32),
            pltpu.VMEM((1, E), f32),
            pltpu.VMEM((2 * C, A), f32),
            pltpu.VMEM((2 * C, N), f32),
            pltpu.VMEM((2 * C, 2 * K), f32),
            pltpu.VMEM((2 * C, 2 * C), f32),
            pltpu.SemaphoreType.DMA((len(KEPT),)),
        ],
        compiler_params=params_vmem,
        name="weight_gradients",
    )(counts, scalars, energy_ref, stress_ref, wg, own, from_left, from_right, src, dst, lists, received, *kept)


def from_blocks(y):
    two = jnp.concatenate([y[0:2, :100], y[2].reshape(2, 64), y[3:5], y[5:7]], axis=1)
    return jnp.concatenate([two.T.reshape(-1), y[7:15].T.reshape(-1), y[15, :56]])


def adam(params, moment_one, moment_two, grad):
    new_moment_one = 0.9 * moment_one + 0.1 * grad
    new_moment_two = 0.999 * moment_two + 0.001 * grad * grad
    corrected_one = new_moment_one / (1.0 - 0.9**STEP)
    corrected_two = new_moment_two / (1.0 - 0.999**STEP)
    new_params = params - 0.001 * (
        corrected_one / (jnp.sqrt(corrected_two) + 1e-08) + 0.01 * params
    )
    return new_params, new_moment_one, new_moment_two


def body(
    positions,
    species,
    counts,
    source,
    target,
    send_left,
    send_right,
    energy_ref,
    force_ref,
    stress_ref,
    params,
    moment_one,
    moment_two,
):
    shards = lax.axis_size("dp")
    slabs = lax.axis_size("graph")
    rank = lax.axis_index("graph")
    index = lax.axis_index("dp")
    core = index % 2
    scalars = jnp.stack([rank, core]).astype(jnp.int32)
    own, lists, outgoing, blocks = prepare(
        positions[0, 0], species[0], force_ref[0, 0], send_left[0], send_right[0], params[None], shards
    )
    wg = lax.all_to_all(blocks, "dp", 0, 0, tiled=True)
    from_left = lax.ppermute(outgoing, "graph", [(i, (i + 1) % slabs) for i in range(slabs)])
    from_right = lax.ppermute(outgoing, "graph", [((i + 1) % slabs, i) for i in range(slabs)])
    message, *kept = forward(
        slabs, counts, scalars, wg, own, from_left, from_right, source[0], target[0], lists
    )
    received = lax.all_to_all(message, "graph", 0, 0, tiled=True)
    forces, sums, keep, give = backward(
        slabs, counts, scalars, energy_ref, stress_ref, wg, own, from_left, from_right, source[0], target[0], lists, received, kept
    )
    volume = slabs * slab_width * cross_area
    pair = keep + lax.ppermute(give, "dp", [(i, i ^ 1) for i in range(shards)])
    chips = [list(range(c, shards, 2)) for c in range(2)]
    within = jnp.sum(
        lax.all_to_all(pair, "dp", 0, 0, tiled=True, axis_index_groups=chips), axis=0
    )
    copies = jnp.broadcast_to(within[None], (slabs, BLOCKS, 128))
    grad = from_blocks(jnp.sum(lax.all_to_all(copies, "graph", 0, 0, tiled=True), axis=0))
    new_params, new_moment_one, new_moment_two = adam(params, moment_one, moment_two, grad)
    return (
        new_params,
        new_moment_one,
        new_moment_two,
        forces[:3][None, None],
        sums[3, 9][None],
        (sums[3, :9] / volume).reshape(1, 3, 3),
    )


def solution(mesh):
    in_specs = (
        P("dp", "graph", None, None),
        P("dp", "graph", None),
        P("dp", "graph"),
        P("dp", "graph", None),
        P("dp", "graph", None),
        P("dp", "graph", None),
        P("dp", "graph", None),
        P("dp"),
        P("dp", "graph", None, None),
        P("dp", None, None),
        P("dp"),
        P("dp"),
        P("dp"),
    )
    out_specs = (
        P("dp"),
        P("dp"),
        P("dp"),
        P("dp", "graph", None, None),
        P("dp"),
        P("dp", None, None),
    )
    return jax.shard_map(body, mesh=mesh, in_specs=in_specs, out_specs=out_specs, check_vma=False)
```

```python
import functools
import jax
import jax.numpy as jnp
from jax import lax
from jax.experimental import pallas as pl
from jax.experimental.pallas import tpu as pltpu
from jax.sharding import PartitionSpec as P

C = 128
FF = 512
K = 64
NS = 100
A = 128
G = 32
DEG = 16
STEP = 100
E = A * DEG
N = A + 2 * G
EC = 1024
CHUNKS = E // EC
BLOCKS = 16
HIDDEN, DN, DH, EMB_OWN, EMB_GHOST = (slice(C * i, C * i + C) for i in range(5))
Z = slice(5 * C, 5 * C + FF)
OWN, GHOST, CONTRIB_OWN, CONTRIB_GHOST = (slice(9 * C + 8 * i, 9 * C + 8 * i + 8) for i in range(4))
KEPT = [(9 * C + 32, A), (8, E), (8, E), (C, E), (C, E)]

highest = lax.Precision.HIGHEST
cutoff = 6.0
slab_width = 20.0
cross_area = 36.0
force_weight = 10.0
stress_weight = 100.0
spread = 0.5 * ((K - 1) / cutoff) ** 2

f32 = jnp.float32
bf16 = jnp.bfloat16
NN = ((1,), (0,))
NT = ((1,), (1,))


def split(x):
    high = x.astype(bf16)
    return high, (x - high.astype(f32)).astype(bf16)


def mm(a, b, dims):
    return lax.dot_general(a, b, (dims, ((), ())), preferred_element_type=f32)


def stack(x):
    return jnp.concatenate(split(x), axis=0)


def fold_rows(x):
    half = x.shape[0] // 2
    return x[:half] + x[half:]


def fold(x):
    half = x.shape[1] // 2
    x = fold_rows(x)
    return x[:, :half] + x[:, half:]


def lhs(w):
    high, low = split(w)
    return jnp.concatenate(
        [jnp.concatenate([high, high], axis=1), jnp.concatenate([low, jnp.zeros_like(low)], axis=1)], axis=0
    )


def wdot(w, x):
    return fold_rows(mm(w, x, NN))


def wide(x):
    return jnp.concatenate(split(x), axis=1)


def twice(x):
    return jnp.concatenate([x, x], axis=0)


def exact(x):
    one = x.astype(bf16).astype(f32)
    two = (x - one).astype(bf16).astype(f32)
    return jnp.concatenate([one, two, x - one - two], axis=0).astype(bf16)


def whole(x):
    return x[0:8] + x[8:16] + x[16:24]


def full_dot(a, b, dims):
    return lax.dot_general(a, b, (dims, ((), ())), precision=highest, preferred_element_type=f32)


def iota(shape, dim):
    return lax.broadcasted_iota(jnp.int32, shape, dim)


def select_lists(send_left, send_right):
    lists = jnp.concatenate(
        [send_right[...], send_left[...], jnp.full((1, 128 - 2 * G), -1, jnp.int32)], axis=1
    )
    return (iota((A, 128), 0) == lists).astype(f32)


def pack_own(positions, species, force_ref):
    rows = [positions[i] for i in range(3)] + [species[...].astype(f32)]
    rows = rows + [force_ref[i] for i in range(3)] + [jnp.zeros((1, A), f32)]
    return jnp.concatenate(rows, axis=0)


def place(pieces, stride, offset, first, last):
    lane = iota((8, 128), 1)
    row = iota((8, 128), 0)
    column = iota((128, 128), 0)
    slot = iota((128, 128), 1)
    lefts, rights = [], []
    for i in range(first, last + 1):
        chosen = [jnp.where(lane % stride == row, p[:, 128 * i : 128 * i + 128], 0.0) for p in pieces]
        lefts.append(jnp.concatenate(chosen, axis=0))
        rights.append((column // stride + (128 // stride) * i == slot + offset).astype(f32))
    return whole(
        mm(
            jnp.concatenate(lefts, axis=1).astype(bf16),
            jnp.concatenate(rights, axis=0).astype(bf16),
            NN,
        )
    )


def prepare_kernel(positions, species, force_ref, send_left, send_right, shard, outgoing, blocks):
    own = pack_own(positions, species, force_ref)
    outgoing[...] = full_dot(own, select_lists(send_left, send_right), NN)
    x = shard[...].reshape(1, 1920)
    one = x.astype(bf16).astype(f32)
    two = (x - one).astype(bf16).astype(f32)
    pieces = [one, two, x - one - two]
    table = place(pieces, 2, 0, 0, 1)
    radial = place(pieces, 2, 100, 1, 2)
    lane = iota((1, 128), 1)
    block = jnp.concatenate(
        [
            table[:2],
            jnp.where(lane < K, radial[:1], pltpu.roll(radial[1:2], K, 1)),
            place(pieces, 2, 164, 2, 4)[:2],
            place(pieces, 2, 292, 4, 6)[:2],
            place(pieces, 8, 105, 6, 14),
            jnp.where(lane < 56, pltpu.roll(x[:, 14 * 128 :], 56, 1), 0.0),
        ],
        axis=0,
    )
    for j in range(blocks.shape[0]):
        blocks[j] = block


def weight(wg, first):
    return jnp.concatenate([wg[:, first, :], wg[:, first + 1, :]], axis=0)


def update_weight_t(wg):
    return jnp.concatenate([wg[:, 7 + h, :] for h in range(8)], axis=0)


def readout_column(wg):
    block = wg[:, 15, :]
    return jnp.concatenate([block[:, h : h + 1] for h in range(8)], axis=0)


def radial_one_t(wg):
    block = wg[:, 2, :]
    return jnp.concatenate([block[:, :K], block[:, K:]], axis=0)


def silu_parts(a):
    sig = 0.5 * jnp.tanh(0.5 * a) + 0.5
    first = sig * (1.0 + a * (1.0 - sig))
    return sig, first


def silu_second(a, sig):
    return sig * (1.0 - sig) * (2.0 + a * (1.0 - 2.0 * sig))


def one_hots(s, t):
    s = jnp.where(s < G, s + A, jnp.where(s < G + A, s - G, s))
    hot_s = (iota((N, EC), 0) == s).astype(f32).astype(bf16)
    hot_t = (iota((A, EC), 0) == t).astype(f32).astype(bf16)
    return hot_s, hot_t


def forward_kernel(
    slabs, count_ref, scalars, wg, positions, species, force_ref, first_ghost, second_ghost, src, dst,
    send_left, send_right, message, atoms, rows_out, vec_out, dfilt_out, q_out,
    src_hot, dst_hot, total, force_total,
):

    count = count_ref[0, 0]
    rank = scalars[0]
    box = slab_width * slabs
    table_t = weight(wg, 0)
    one_t = lhs(radial_one_t(wg))
    two_t = lhs(weight(wg, 3))
    message_t = lhs(weight(wg, 5))
    update_f = update_weight_t(wg)
    update_t = lhs(update_f)
    update = lhs(update_f.T)
    readout = readout_column(wg)

    own_rows = pack_own(positions, species, force_ref)
    lane = iota((8, 128), 1)
    row = iota((8, 128), 0)
    ghost_rows = jnp.where((lane < G) == (rank % 2 == 1), first_ghost[...], second_ghost[...])
    atoms[OWN] = own_rows
    atoms[GHOST] = ghost_rows
    shift = jnp.where(lane < G, jnp.where(rank == 0, -box, 0.0), 0.0)
    shift = shift + jnp.where((lane >= G) & (lane < 2 * G), jnp.where(rank == slabs - 1, box, 0.0), 0.0)
    ghost_pos = ghost_rows + jnp.where(row == 0, shift, 0.0)
    ext = jnp.concatenate([own_rows, ghost_pos], axis=1)
    pieces = exact(jnp.where(iota((8, 256), 0) < 3, ext, 0.0))
    kinds = ext[3:4, :].astype(jnp.int32)
    kind_hot = (iota((128, 256), 0) == kinds).astype(f32)
    table_hi, table_rest = split(table_t)
    table_lo = (table_t - table_hi.astype(f32) - table_rest.astype(f32)).astype(bf16)
    kind_bf = kind_hot.astype(bf16)
    emb = mm(table_hi, kind_bf, NN) + mm(table_rest, kind_bf, NN) + mm(table_lo, kind_bf, NN)
    atoms[EMB_OWN] = emb[:, :A]
    atoms[EMB_GHOST] = emb[:, A:]
    projected = stack(wdot(message_t, stack(emb)))[:, :N]
    total[...] = jnp.zeros_like(total)
    centers = iota((K, EC), 0).astype(f32) * (cutoff / (K - 1))

    for i in range(CHUNKS):
        at = pl.ds(i * EC, EC)
        t = dst[:, at]
        hot_s, hot_t = one_hots(src[:, at], t)
        src_hot[:, at] = hot_s
        dst_hot[:, at] = hot_t
        vec = whole(mm(pieces[:, :N], hot_s, NN) - mm(pieces[:, :A], hot_t, NN))
        vec_out[:, at] = vec
        square = jnp.sum(vec * vec, axis=0, keepdims=True)
        dist = jnp.sqrt(square)
        inverse = jnp.where(square > 0.0, 1.0 / jnp.where(square > 0.0, dist, 1.0), 0.0)
        ratio = jnp.minimum(dist / cutoff, 1.0)
        live = (t < count).astype(f32)
        inside = 1.0 - ratio * ratio
        gate = inside * inside * live
        dgate = inside * ratio * (-4.0 / cutoff) * live
        rows_out[0:1, at] = dist
        rows_out[1:2, at] = inverse
        rows_out[2:3, at] = gate
        rows_out[3:4, at] = dgate
        delta = dist - centers
        basis = jnp.exp(-spread * delta * delta)
        dbasis = (-2.0 * spread) * delta * basis
        a = wdot(one_t, stack(basis))
        da = wdot(one_t, stack(dbasis))
        sig, slope = silu_parts(a)
        f = wdot(two_t, stack(a * sig))
        df = wdot(two_t, stack(slope * da))
        filt = f * gate
        dfilt = df * gate + f * dgate
        q = fold_rows(mm(projected, hot_s, NN))
        dfilt_out[:, at] = dfilt
        q_out[:, at] = q
        total[...] += mm(stack(filt * q), hot_t, NT)

    hidden = emb[:, :A] + fold_rows(total[...]) * (1.0 / DEG)
    atoms[HIDDEN] = hidden
    rms = lax.rsqrt(jnp.mean(hidden * hidden, axis=0, keepdims=True) + 1e-05)
    z = wdot(update_t, stack(hidden * rms))
    atoms[Z] = z
    sig, slope = silu_parts(z)
    live_atom = (iota((1, A), 1) < count).astype(f32)
    weighted = readout * live_atom
    energy = jnp.sum(jnp.sum(weighted * (z * sig), axis=0, keepdims=True), axis=1, keepdims=True)
    dn = wdot(update, stack(weighted * slope))
    atoms[DN] = dn
    cube = rms * rms * rms * (1.0 / C)
    dh = rms * dn - hidden * (cube * jnp.sum(dn * hidden, axis=0, keepdims=True))
    atoms[DH] = dh
    dh_pieces = wide(dh * (1.0 / DEG))
    force_total[...] = jnp.zeros_like(force_total)

    stress = [jnp.zeros((8, 1), f32) for _ in range(3)]
    for i in range(CHUNKS):
        at = pl.ds(i * EC, EC)
        hot_s = src_hot[:, at]
        hot_t = dst_hot[:, at]
        back = mm(dh_pieces, twice(hot_t), NN)
        along = jnp.sum(back * (dfilt_out[:, at] * q_out[:, at]), axis=0, keepdims=True)
        vec = vec_out[:, at]
        slopes = vec * (along * rows_out[1:2, at])
        three = exact(slopes)
        force_total[:, :N] += mm(three, hot_s, NT)
        force_total[:, :A] -= mm(three, hot_t, NT)
        stress = [
            stress[j] + jnp.sum(slopes * vec[j : j + 1], axis=1, keepdims=True) for j in range(3)
        ]

    contrib = whole(force_total[...])
    atoms[CONTRIB_OWN] = contrib[:, :A]
    atoms[CONTRIB_GHOST] = contrib[:, A:]
    lists_hot = select_lists(send_left, send_right)
    outgoing = full_dot(contrib[:, :A], lists_hot, NN) + pltpu.roll(contrib[:, A:], 64, 1)
    to_right = (lane < G) | (lane >= 96)
    sums = jnp.zeros((8, 128), f32)
    for i in range(3):
        for j in range(3):
            sums = sums + jnp.where(lane == 3 * i + j, stress[j][i : i + 1], 0.0)
    sums = sums + jnp.where(lane == 9, energy, 0.0)
    right = lax.rem(rank + 1, slabs)
    left = lax.rem(rank + slabs - 1, slabs)
    for d in range(8):
        keep = (to_right & (right == d)) | (jnp.logical_not(to_right) & (left == d))
        message[d] = jnp.where(row == 3, sums, jnp.where(keep, outgoing, 0.0))[:4]


def backward_kernel(
    slabs, count_ref, scalars, energy_ref, stress_ref, wg, src, dst, send_left, send_right, received, atoms, rows_in, vec_in, dfilt_in, q_in,
    forces_out, sums_out, keep, give,
    src_hot, dst_hot, grad, step_row, total, source_total, one_total, two_total,
):

    count = count_ref[0, 0]
    core = scalars[1]
    volume = slab_width * cross_area * slabs
    scale = 2.0 / (slabs * A)
    one_t = lhs(radial_one_t(wg))
    two_f = weight(wg, 3)
    two_t = lhs(two_f)
    two = lhs(two_f.T)
    message_w = lhs(weight(wg, 5).T)
    update_f = update_weight_t(wg)
    update_t = lhs(update_f)
    update = lhs(update_f.T)
    readout = readout_column(wg)
    lists_hot = select_lists(send_left, send_right)
    lane = iota((8, 128), 1)
    row = iota((8, 128), 0)
    own = atoms[OWN]
    ghost = atoms[GHOST]

    got = jnp.sum(received[...], axis=0)
    got = jnp.concatenate([got, jnp.zeros_like(got)], axis=0)
    moved = jnp.where(row < 3, got, 0.0)
    energy = got[3:4, 9:10]
    inner = jnp.where(lane < 2 * G, pltpu.roll(moved, 64, 1), 0.0)
    force_own = -(atoms[CONTRIB_OWN] + full_dot(inner, lists_hot, NT))
    force_ghost = -(atoms[CONTRIB_GHOST] + jnp.where(lane < 2 * G, moved, 0.0))
    forces_out[...] = force_own
    sums_out[...] = got
    own_ref = jnp.concatenate([own[4:8], jnp.zeros((4, 128), f32)], axis=0)
    ghost_ref = jnp.concatenate([ghost[4:8], jnp.zeros((4, 128), f32)], axis=0)
    factor = force_weight * scale
    cot_own = jnp.where((lane < count) & (row < 3), factor * (force_own - own_ref), 0.0)
    cot_ghost = jnp.where((lane < 2 * G) & (row < 3), factor * (force_ghost - ghost_ref), 0.0)
    cot = exact(jnp.concatenate([cot_own, cot_ghost], axis=1))
    stress_cot = [
        [
            (2.0 * stress_weight / volume) * (got[3:4, 3 * i + j : 3 * i + j + 1] / volume - stress_ref[i, 0, j])
            for j in range(3)
        ]
        for i in range(3)
    ]
    energy_cot = (energy - energy_ref[0]) * scale
    total[...] = jnp.zeros_like(total)

    for i in range(CHUNKS):
        at = pl.ds(i * EC, EC)
        hot_s, hot_t = one_hots(src[:, at], dst[:, at])
        src_hot[:, at] = hot_s
        dst_hot[:, at] = hot_t
        vec = vec_in[:, at]
        delta = whole(mm(cot[:, :A], hot_t, NN) - mm(cot[:, :N], hot_s, NN))
        along = jnp.sum(vec * delta, axis=0, keepdims=True)
        for r in range(3):
            inner_row = sum(stress_cot[r][j] * vec[j : j + 1] for j in range(3))
            along = along + vec[r : r + 1] * inner_row
        step = along * rows_in[1:2, at]
        step_row[:, at] = step
        total[...] += mm(stack(dfilt_in[:, at] * q_in[:, at] * step), hot_t, NT)

    hidden = atoms[HIDDEN]
    dn = atoms[DN]
    dh = atoms[DH]
    z = atoms[Z]
    moved_h = fold_rows(total[...]) * (1.0 / DEG)
    rms = lax.rsqrt(jnp.mean(hidden * hidden, axis=0, keepdims=True) + 1e-05)
    cube = rms * rms * rms
    cross = jnp.mean(hidden * moved_h, axis=0, keepdims=True)
    normed = hidden * rms
    moved_n = rms * moved_h - (cube * cross) * hidden
    moved_n2 = stack(moved_n)
    moved_z = wdot(update_t, moved_n2)
    sig, slope = silu_parts(z)
    live_atom = (iota((1, A), 1) < count).astype(f32)
    weighted = readout * live_atom
    z_bar = weighted * (energy_cot * slope + silu_second(z, sig) * moved_z)
    z_bar = stack(z_bar)
    update_grad = fold(
        mm(
            jnp.concatenate([z_bar, stack(weighted * slope)], axis=1),
            jnp.concatenate([stack(normed), moved_n2], axis=1),
            NT,
        )
    )
    readout_grad = jnp.sum(live_atom * (energy_cot * (z * sig) + slope * moved_z), axis=1, keepdims=True)
    n_bar = wdot(update, z_bar)
    dn_h = jnp.sum(dn * hidden, axis=0, keepdims=True) * (1.0 / C)
    mix = (jnp.sum(n_bar * hidden, axis=0, keepdims=True) + jnp.sum(dn * moved_h, axis=0, keepdims=True)) * (1.0 / C)
    h_bar = (
        rms * n_bar
        + hidden * (3.0 * cube * rms * rms * cross * dn_h - cube * mix)
        - moved_h * (cube * dn_h)
        - dn * (cube * cross)
    )
    for h in range(8):
        grad[:, 7 + h, :] = update_grad[64 * h : 64 * h + 64]
    lane64 = iota((64, 128), 1)
    block = jnp.zeros((64, 128), f32)
    for h in range(8):
        block = block + jnp.where(lane64 == h, readout_grad[64 * h : 64 * h + 64], 0.0)
    grad[:, 15, :] = block

    both_pieces = jnp.concatenate([wide(h_bar * (1.0 / DEG)), wide(dh * (1.0 / DEG))], axis=0)
    source_total[...] = jnp.zeros_like(source_total)
    one_total[...] = jnp.zeros_like(one_total)
    two_total[...] = jnp.zeros_like(two_total)
    centers = iota((K, EC), 0).astype(f32) * (cutoff / (K - 1))

    for i in range(CHUNKS):
        at = pl.ds(i * EC, EC)
        hot_s = src_hot[:, at]
        hot_t = dst_hot[:, at]
        step = step_row[:, at]
        gate = rows_in[2:3, at]
        dgate = rows_in[3:4, at]
        both = mm(both_pieces, twice(hot_t), NN)
        m_bar = both[:C]
        dm_bar = both[C:]
        q = q_in[:, at]
        dq = dm_bar * q
        f_bar = stack(m_bar * q * gate + dq * (dgate * step))
        df_bar = stack(dq * gate)
        s_bar = wdot(two, f_bar)
        ds_bar = wdot(two, df_bar)
        delta = rows_in[0:1, at] - centers
        basis = jnp.exp(-spread * delta * delta)
        moved_basis = (-2.0 * spread) * delta * basis * step
        basis = stack(basis)
        moved_basis = stack(moved_basis)
        a = wdot(one_t, basis)
        moved_a = wdot(one_t, moved_basis)
        sig, slope = silu_parts(a)
        inner = stack(a * sig)
        filt = wdot(two_t, inner) * gate
        source_total[...] += mm(stack(m_bar * filt + dm_bar * (dfilt_in[:, at] * step)), hot_s, NT)
        two_total[...] += mm(f_bar, inner, NT) + mm(df_bar, stack(slope * moved_a), NT)
        a_bar = stack(s_bar * slope + ds_bar * (silu_second(a, sig) * moved_a))
        da_bar = stack(ds_bar * slope)
        one_total[...] += mm(a_bar, basis, NT) + mm(da_bar, moved_basis, NT)

    one_grad = fold(one_total[...])
    grad[:, 2, :] = jnp.concatenate([one_grad[:64], one_grad[64:]], axis=1)
    two_grad = fold(two_total[...])
    grad[:, 3, :] = two_grad[:64]
    grad[:, 4, :] = two_grad[64:]
    p_bar = fold_rows(source_total[...])
    p_bar = jnp.concatenate([p_bar, jnp.zeros((C, 256 - N), f32)], axis=1)
    p_pieces = stack(p_bar)
    emb = jnp.concatenate([atoms[EMB_OWN], atoms[EMB_GHOST]], axis=1)
    message_grad = fold(mm(p_pieces, stack(emb), NT))
    grad[:, 5, :] = message_grad[:64]
    grad[:, 6, :] = message_grad[64:]
    emb_bar = wdot(message_w, p_pieces)
    emb_bar = jnp.concatenate([emb_bar[:, :A] + h_bar, emb_bar[:, A:]], axis=1)
    kinds = jnp.concatenate([own[3:4], ghost[3:4]], axis=1).astype(jnp.int32)
    kind_hot = (iota((128, 256), 0) == kinds).astype(f32).astype(bf16)
    table_grad = fold_rows(mm(stack(emb_bar), kind_hot, NT))
    grad[:, 0, :] = table_grad[:64]
    grad[:, 1, :] = table_grad[64:]
    for j in range(32):
        keep[j] = grad[2 * j + core]
        give[j] = grad[2 * j + 1 - core]


vmem = pl.BlockSpec(memory_space=pltpu.VMEM)
smem = pl.BlockSpec(memory_space=pltpu.SMEM)
params_vmem = pltpu.CompilerParams(vmem_limit_bytes=32 * 1024 * 1024)


def shape(*dims, dtype=jnp.float32):
    return jax.ShapeDtypeStruct(dims, dtype)


def prepare(positions, species, force_ref, send_left, send_right, shard, shards):
    return pl.pallas_call(
        prepare_kernel,
        out_shape=[shape(8, 128), shape(shards, BLOCKS, 128)],
        in_specs=[vmem] * 6,
        out_specs=[vmem] * 2,
        compiler_params=params_vmem,
        name="prepare",
    )(positions, species, force_ref, send_left, send_right, shard)


def forward(slabs, counts, scalars, wg, *arrays):
    return pl.pallas_call(
        functools.partial(forward_kernel, slabs),
        out_shape=[shape(8, 4, 128)] + [shape(*dims) for dims in KEPT],
        in_specs=[smem] * 2 + [vmem] * (1 + len(arrays)),
        out_specs=[vmem] * (1 + len(KEPT)),
        scratch_shapes=[
            pltpu.VMEM((N, E), bf16),
            pltpu.VMEM((A, E), bf16),
            pltpu.VMEM((2 * C, A), f32),
            pltpu.VMEM((24, 256), f32),
        ],
        compiler_params=params_vmem,
        name="energy_slopes",
    )(counts, scalars, wg, *arrays)


def backward(slabs, counts, scalars, energy_ref, stress_ref, *arrays):
    outs = [shape(8, 128), shape(8, 128), shape(32, BLOCKS, 128), shape(32, BLOCKS, 128)]
    return pl.pallas_call(
        functools.partial(backward_kernel, slabs),
        out_shape=outs,
        in_specs=[smem] * 4 + [vmem] * len(arrays),
        out_specs=[vmem] * 4,
        scratch_shapes=[
            pltpu.VMEM((N, E), bf16),
            pltpu.VMEM((A, E), bf16),
            pltpu.VMEM((64, BLOCKS, 128), f32),
            pltpu.VMEM((1, E), f32),
            pltpu.VMEM((2 * C, A), f32),
            pltpu.VMEM((2 * C, N), f32),
            pltpu.VMEM((2 * C, 2 * K), f32),
            pltpu.VMEM((2 * C, 2 * C), f32),
        ],
        compiler_params=params_vmem,
        name="weight_gradients",
    )(counts, scalars, energy_ref, stress_ref, *arrays)


def from_blocks(y):
    two = jnp.concatenate([y[0:2, :100], y[2].reshape(2, 64), y[3:5], y[5:7]], axis=1)
    return jnp.concatenate([two.T.reshape(-1), y[7:15].T.reshape(-1), y[15, :56]])


def adam(params, moment_one, moment_two, grad):
    new_moment_one = 0.9 * moment_one + 0.1 * grad
    new_moment_two = 0.999 * moment_two + 0.001 * grad * grad
    corrected_one = new_moment_one / (1.0 - 0.9**STEP)
    corrected_two = new_moment_two / (1.0 - 0.999**STEP)
    new_params = params - 0.001 * (
        corrected_one / (jnp.sqrt(corrected_two) + 1e-08) + 0.01 * params
    )
    return new_params, new_moment_one, new_moment_two


def body(
    positions,
    species,
    counts,
    source,
    target,
    send_left,
    send_right,
    energy_ref,
    force_ref,
    stress_ref,
    params,
    moment_one,
    moment_two,
):
    shards = lax.axis_size("dp")
    slabs = lax.axis_size("graph")
    rank = lax.axis_index("graph")
    index = lax.axis_index("dp")
    core = index % 2
    scalars = jnp.stack([rank, core]).astype(jnp.int32)
    atoms = (positions.reshape(3, 1, A), species[0], force_ref.reshape(3, 1, A))
    lists = (send_left[0], send_right[0])
    outgoing, blocks = prepare(*atoms, *lists, params, shards)
    wg = lax.all_to_all(blocks, "dp", 0, 0, tiled=True)
    first = lax.ppermute(outgoing, "graph", [(i, i ^ 1) for i in range(slabs)])
    second = lax.ppermute(
        outgoing, "graph", [(i, (i + (1 if i % 2 else slabs - 1)) % slabs) for i in range(slabs)]
    )
    message, *kept = forward(
        slabs, counts, scalars, wg, *atoms, first, second, source[0], target[0], *lists
    )
    received = lax.all_to_all(message, "graph", 0, 0, tiled=True)
    forces, sums, keep, give = backward(
        slabs, counts, scalars, energy_ref, stress_ref.reshape(3, 1, 3), wg, source[0], target[0], *lists, received, *kept
    )
    volume = slabs * slab_width * cross_area
    pair = keep + lax.ppermute(give, "dp", [(i, i ^ 1) for i in range(shards)])
    chips = [list(range(c, shards, 2)) for c in range(2)]
    within = jnp.sum(
        lax.all_to_all(pair, "dp", 0, 0, tiled=True, axis_index_groups=chips), axis=0
    )
    copies = jnp.broadcast_to(within[None], (slabs, BLOCKS, 128))
    grad = from_blocks(jnp.sum(lax.all_to_all(copies, "graph", 0, 0, tiled=True), axis=0))
    new_params, new_moment_one, new_moment_two = adam(params, moment_one, moment_two, grad)
    return (
        new_params,
        new_moment_one,
        new_moment_two,
        forces[:3][None, None],
        sums[3, 9][None],
        (sums[3, :9] / volume).reshape(1, 3, 3),
    )


def solution(mesh):
    in_specs = (
        P("dp", "graph", None, None),
        P("dp", "graph", None),
        P("dp", "graph"),
        P("dp", "graph", None),
        P("dp", "graph", None),
        P("dp", "graph", None),
        P("dp", "graph", None),
        P("dp"),
        P("dp", "graph", None, None),
        P("dp", None, None),
        P("dp"),
        P("dp"),
        P("dp"),
    )
    out_specs = (
        P("dp"),
        P("dp"),
        P("dp"),
        P("dp", "graph", None, None),
        P("dp"),
        P("dp", None, None),
    )
    return jax.shard_map(body, mesh=mesh, in_specs=in_specs, out_specs=out_specs, check_vma=False)
```

```python
import functools
import jax
import jax.numpy as jnp
from jax import lax
from jax.experimental import pallas as pl
from jax.experimental.pallas import tpu as pltpu
from jax.sharding import PartitionSpec as P

C = 128
FF = 512
K = 64
NS = 100
A = 128
G = 32
DEG = 16
STEP = 100
E = A * DEG
N = A + 2 * G
EC = 1024
CHUNKS = E // EC
BLOCKS = 16
HIDDEN, DN, DH, EMB_OWN, EMB_GHOST = (slice(C * i, C * i + C) for i in range(5))
Z = slice(5 * C, 5 * C + FF)
GHOST, CONTRIB_OWN, CONTRIB_GHOST = (slice(9 * C + 8 * i, 9 * C + 8 * i + 8) for i in range(3))
OWN = slice(9 * C + 24, 9 * C + 40)
KEPT = [(9 * C + 40, A), (8, E), (8, E), (C, E), (C, E)]

highest = lax.Precision.HIGHEST
cutoff = 6.0
slab_width = 20.0
cross_area = 36.0
force_weight = 10.0
stress_weight = 100.0
spread = 0.5 * ((K - 1) / cutoff) ** 2

f32 = jnp.float32
bf16 = jnp.bfloat16
NN = ((1,), (0,))
NT = ((1,), (1,))


def split(x):
    high = x.astype(bf16)
    return high, (x - high.astype(f32)).astype(bf16)


def mm(a, b, dims):
    return lax.dot_general(a, b, (dims, ((), ())), preferred_element_type=f32)


def stack(x):
    return jnp.concatenate(split(x), axis=0)


def fold_rows(x):
    half = x.shape[0] // 2
    return x[:half] + x[half:]


def fold(x):
    half = x.shape[1] // 2
    x = fold_rows(x)
    return x[:, :half] + x[:, half:]


def lhs(w):
    high, low = split(w)
    return jnp.concatenate(
        [jnp.concatenate([high, high], axis=1), jnp.concatenate([low, jnp.zeros_like(low)], axis=1)], axis=0
    )


def wdot(w, x):
    return fold_rows(mm(w, x, NN))


def lhs_deep(w):
    high, low = split(w)
    return jnp.concatenate([high, high, low], axis=1)


def deep(pair):
    return jnp.concatenate([pair, pair[: pair.shape[0] // 2]], axis=0)


def wide(x):
    return jnp.concatenate(split(x), axis=1)


def twice(x):
    return jnp.concatenate([x, x], axis=0)


def exact(x):
    one = x.astype(bf16).astype(f32)
    two = (x - one).astype(bf16).astype(f32)
    return jnp.concatenate([one, two, x - one - two], axis=0).astype(bf16)


def whole(x):
    return x[0:8] + x[8:16] + x[16:24]


def full_dot(a, b, dims):
    return lax.dot_general(a, b, (dims, ((), ())), precision=highest, preferred_element_type=f32)


def iota(shape, dim):
    return lax.broadcasted_iota(jnp.int32, shape, dim)


def select_lists(own):
    return (iota((A, 128), 0) == own[8:9].astype(jnp.int32)).astype(f32)


def pack_own(positions, species, force_ref, send_left, send_right, stress_ref):
    lane = iota((1, A), 1)
    refs = jnp.zeros((1, A), f32)
    for i in range(3):
        for j in range(3):
            refs = refs + jnp.where(lane == 3 * i + j, stress_ref[i][:, j : j + 1], 0.0)
    rows = [positions[i] for i in range(3)] + [species[...].astype(f32)]
    lists = jnp.concatenate(
        [send_right[...], send_left[...], jnp.full((1, 128 - 2 * G), -1, jnp.int32)], axis=1
    )
    rows = rows + [force_ref[i] for i in range(3)] + [refs, lists.astype(f32), jnp.zeros((7, A), f32)]
    return jnp.concatenate(rows, axis=0)


def place(pieces, stride, offset, first, last):
    lane = iota((8, 128), 1)
    row = iota((8, 128), 0)
    column = iota((128, 128), 0)
    slot = iota((128, 128), 1)
    lefts, rights = [], []
    for i in range(first, last + 1):
        chosen = [jnp.where(lane % stride == row, p[:, 128 * i : 128 * i + 128], 0.0) for p in pieces]
        lefts.append(jnp.concatenate(chosen, axis=0))
        rights.append((column // stride + (128 // stride) * i == slot + offset).astype(f32))
    return whole(
        mm(
            jnp.concatenate(lefts, axis=1).astype(bf16),
            jnp.concatenate(rights, axis=0).astype(bf16),
            NN,
        )
    )


def prepare_kernel(
    positions, species, force_ref, send_left, send_right, stress_ref, shard, own_out, outgoing, blocks
):
    own = pack_own(positions, species, force_ref, send_left, send_right, stress_ref)
    own_out[...] = own
    outgoing[...] = full_dot(own[:8], select_lists(own), NN)
    x = shard[...].reshape(1, 1920)
    one = x.astype(bf16).astype(f32)
    two = (x - one).astype(bf16).astype(f32)
    pieces = [one, two, x - one - two]
    table = place(pieces, 2, 0, 0, 1)
    radial = place(pieces, 2, 100, 1, 2)
    lane = iota((1, 128), 1)
    block = jnp.concatenate(
        [
            table[:2],
            jnp.where(lane < K, radial[:1], pltpu.roll(radial[1:2], K, 1)),
            place(pieces, 2, 164, 2, 4)[:2],
            place(pieces, 2, 292, 4, 6)[:2],
            place(pieces, 8, 105, 6, 14),
            jnp.where(lane < 56, pltpu.roll(x[:, 14 * 128 :], 56, 1), 0.0),
        ],
        axis=0,
    )
    for j in range(blocks.shape[0]):
        blocks[j] = block


def weight(wg, first):
    return jnp.concatenate([wg[:, first, :], wg[:, first + 1, :]], axis=0)


def update_weight_t(wg):
    return jnp.concatenate([wg[:, 7 + h, :] for h in range(8)], axis=0)


def readout_column(wg):
    block = wg[:, 15, :]
    return jnp.concatenate([block[:, h : h + 1] for h in range(8)], axis=0)


def radial_one_t(wg):
    block = wg[:, 2, :]
    return jnp.concatenate([block[:, :K], block[:, K:]], axis=0)


def silu_parts(a):
    t = jnp.tanh(0.5 * a)
    sig = 0.5 * t + 0.5
    peak = 0.25 - 0.25 * (t * t)
    return sig, sig + a * peak, peak * (2.0 - a * t)


def one_hots(s, t):
    s = jnp.where(s < G, s + A, jnp.where(s < G + A, s - G, s))
    hot_s = (iota((N, EC), 0) == s).astype(f32).astype(bf16)
    hot_t = (iota((A, EC), 0) == t).astype(f32).astype(bf16)
    return hot_s, hot_t


def forward_kernel(
    slabs, count_ref, scalars, wg, own, first_ghost, second_ghost, src, dst,
    message, atoms, rows_out, vec_out, dfilt_out, q_out,
    src_hot, dst_hot, total, force_total,
):

    count = count_ref[0, 0]
    rank = scalars[0]
    box = slab_width * slabs
    table_t = weight(wg, 0)
    one_t = lhs_deep(radial_one_t(wg))
    two_t = lhs(weight(wg, 3))
    message_t = lhs(weight(wg, 5))
    update_f = update_weight_t(wg)
    update_t = lhs(update_f)
    update = lhs(update_f.T)
    readout = readout_column(wg)

    own = own[...]
    own_rows = own[:8]
    lane = iota((8, 128), 1)
    row = iota((8, 128), 0)
    ghost_rows = jnp.where((lane < G) == (rank % 2 == 1), first_ghost[...], second_ghost[...])
    atoms[OWN] = own
    atoms[GHOST] = ghost_rows
    shift = jnp.where(lane < G, jnp.where(rank == 0, -box, 0.0), 0.0)
    shift = shift + jnp.where((lane >= G) & (lane < 2 * G), jnp.where(rank == slabs - 1, box, 0.0), 0.0)
    ghost_pos = ghost_rows + jnp.where(row == 0, shift, 0.0)
    ext = jnp.concatenate([own_rows, ghost_pos], axis=1)
    pieces = exact(jnp.where(iota((8, 256), 0) < 3, ext, 0.0))
    kinds = ext[3:4, :].astype(jnp.int32)
    kind_hot = (iota((128, 256), 0) == kinds).astype(f32)
    table_hi, table_rest = split(table_t)
    table_lo = (table_t - table_hi.astype(f32) - table_rest.astype(f32)).astype(bf16)
    kind_bf = kind_hot.astype(bf16)
    emb = mm(table_hi, kind_bf, NN) + mm(table_rest, kind_bf, NN) + mm(table_lo, kind_bf, NN)
    atoms[EMB_OWN] = emb[:, :A]
    atoms[EMB_GHOST] = emb[:, A:]
    projected = stack(wdot(message_t, stack(emb)))[:, :N]
    total[...] = jnp.zeros_like(total)
    centers = iota((K, EC), 0).astype(f32) * (cutoff / (K - 1))

    for i in range(CHUNKS):
        at = pl.ds(i * EC, EC)
        t = dst[:, at]
        hot_s, hot_t = one_hots(src[:, at], t)
        src_hot[:, at] = hot_s
        dst_hot[:, at] = hot_t
        vec = whole(mm(pieces[:, :N], hot_s, NN) - mm(pieces[:, :A], hot_t, NN))
        vec_out[:, at] = vec
        square = jnp.sum(vec * vec, axis=0, keepdims=True)
        dist = jnp.sqrt(square)
        inverse = jnp.where(square > 0.0, 1.0 / jnp.where(square > 0.0, dist, 1.0), 0.0)
        ratio = jnp.minimum(dist / cutoff, 1.0)
        live = (t < count).astype(f32)
        inside = 1.0 - ratio * ratio
        gate = inside * inside * live
        dgate = inside * ratio * (-4.0 / cutoff) * live
        rows_out[0:1, at] = dist
        rows_out[1:2, at] = inverse
        rows_out[2:3, at] = gate
        rows_out[3:4, at] = dgate
        delta = dist - centers
        basis = jnp.exp(-spread * delta * delta)
        dbasis = (-2.0 * spread) * delta * basis
        a = mm(one_t, deep(stack(basis)), NN)
        da = mm(one_t, deep(stack(dbasis)), NN)
        sig, slope, second = silu_parts(a)
        f = wdot(two_t, stack(a * sig))
        df = wdot(two_t, stack(slope * da))
        filt = f * gate
        dfilt = df * gate + f * dgate
        q = fold_rows(mm(projected, hot_s, NN))
        dfilt_out[:, at] = dfilt
        q_out[:, at] = q
        total[...] += mm(stack(filt * q), hot_t, NT)

    hidden = emb[:, :A] + fold_rows(total[...]) * (1.0 / DEG)
    atoms[HIDDEN] = hidden
    rms = lax.rsqrt(jnp.mean(hidden * hidden, axis=0, keepdims=True) + 1e-05)
    z = wdot(update_t, stack(hidden * rms))
    atoms[Z] = z
    sig, slope, second = silu_parts(z)
    live_atom = (iota((1, A), 1) < count).astype(f32)
    weighted = readout * live_atom
    energy = jnp.sum(jnp.sum(weighted * (z * sig), axis=0, keepdims=True), axis=1, keepdims=True)
    dn = wdot(update, stack(weighted * slope))
    atoms[DN] = dn
    cube = rms * rms * rms * (1.0 / C)
    dh = rms * dn - hidden * (cube * jnp.sum(dn * hidden, axis=0, keepdims=True))
    atoms[DH] = dh
    dh_pieces = wide(dh * (1.0 / DEG))
    force_total[...] = jnp.zeros_like(force_total)

    stress = [jnp.zeros((8, 1), f32) for _ in range(3)]
    for i in range(CHUNKS):
        at = pl.ds(i * EC, EC)
        hot_s = src_hot[:, at]
        hot_t = dst_hot[:, at]
        back = mm(dh_pieces, twice(hot_t), NN)
        along = jnp.sum(back * (dfilt_out[:, at] * q_out[:, at]), axis=0, keepdims=True)
        vec = vec_out[:, at]
        slopes = vec * (along * rows_out[1:2, at])
        three = exact(slopes)
        force_total[:, :N] += mm(three, hot_s, NT)
        force_total[:, :A] -= mm(three, hot_t, NT)
        stress = [
            stress[j] + jnp.sum(slopes * vec[j : j + 1], axis=1, keepdims=True) for j in range(3)
        ]

    contrib = whole(force_total[...])
    atoms[CONTRIB_OWN] = contrib[:, :A]
    atoms[CONTRIB_GHOST] = contrib[:, A:]
    lists_hot = select_lists(own)
    outgoing = full_dot(contrib[:, :A], lists_hot, NN) + pltpu.roll(contrib[:, A:], 64, 1)
    to_right = (lane < G) | (lane >= 96)
    sums = jnp.zeros((8, 128), f32)
    for i in range(3):
        for j in range(3):
            sums = sums + jnp.where(lane == 3 * i + j, stress[j][i : i + 1], 0.0)
    sums = sums + jnp.where(lane == 9, energy, 0.0)
    right = lax.rem(rank + 1, slabs)
    left = lax.rem(rank + slabs - 1, slabs)
    for d in range(8):
        keep = (to_right & (right == d)) | (jnp.logical_not(to_right) & (left == d))
        message[d] = jnp.where(row == 3, sums, jnp.where(keep, outgoing, 0.0))[:4]


def backward_kernel(
    slabs, count_ref, scalars, energy_ref, wg, src, dst, received, atoms, rows_in, vec_in, dfilt_in, q_in,
    forces_out, sums_out, keep, give,
    src_hot, dst_hot, grad, step_row, total, source_total, one_total, two_total,
):

    count = count_ref[0, 0]
    core = scalars[1]
    volume = slab_width * cross_area * slabs
    scale = 2.0 / (slabs * A)
    one_t = lhs_deep(radial_one_t(wg))
    two_f = weight(wg, 3)
    two_t = lhs(two_f)
    two = lhs(two_f.T)
    message_w = lhs(weight(wg, 5).T)
    update_f = update_weight_t(wg)
    update_t = lhs(update_f)
    update = lhs(update_f.T)
    readout = readout_column(wg)
    own = atoms[OWN]
    lists_hot = select_lists(own)
    lane = iota((8, 128), 1)
    row = iota((8, 128), 0)
    ghost = atoms[GHOST]

    got = jnp.sum(received[...], axis=0)
    got = jnp.concatenate([got, jnp.zeros_like(got)], axis=0)
    moved = jnp.where(row < 3, got, 0.0)
    energy = got[3:4, 9:10]
    inner = jnp.where(lane < 2 * G, pltpu.roll(moved, 64, 1), 0.0)
    force_own = -(atoms[CONTRIB_OWN] + full_dot(inner, lists_hot, NT))
    force_ghost = -(atoms[CONTRIB_GHOST] + jnp.where(lane < 2 * G, moved, 0.0))
    forces_out[...] = force_own
    sums_out[...] = got
    own_ref = jnp.concatenate([own[4:8], jnp.zeros((4, 128), f32)], axis=0)
    ghost_ref = jnp.concatenate([ghost[4:8], jnp.zeros((4, 128), f32)], axis=0)
    factor = force_weight * scale
    cot_own = jnp.where((lane < count) & (row < 3), factor * (force_own - own_ref), 0.0)
    cot_ghost = jnp.where((lane < 2 * G) & (row < 3), factor * (force_ghost - ghost_ref), 0.0)
    cot = exact(jnp.concatenate([cot_own, cot_ghost], axis=1))
    stress_row = (2.0 * stress_weight / volume) * (got[3:4] / volume - own[7:8])
    stress_cot = [[stress_row[:, 3 * i + j : 3 * i + j + 1] for j in range(3)] for i in range(3)]
    energy_cot = (energy - energy_ref[0]) * scale
    total[...] = jnp.zeros_like(total)

    for i in range(CHUNKS):
        at = pl.ds(i * EC, EC)
        hot_s, hot_t = one_hots(src[:, at], dst[:, at])
        src_hot[:, at] = hot_s
        dst_hot[:, at] = hot_t
        vec = vec_in[:, at]
        delta = whole(mm(cot[:, :A], hot_t, NN) - mm(cot[:, :N], hot_s, NN))
        along = jnp.sum(vec * delta, axis=0, keepdims=True)
        for r in range(3):
            inner_row = sum(stress_cot[r][j] * vec[j : j + 1] for j in range(3))
            along = along + vec[r : r + 1] * inner_row
        step = along * rows_in[1:2, at]
        step_row[:, at] = step
        total[...] += mm(stack(dfilt_in[:, at] * q_in[:, at] * step), hot_t, NT)

    hidden = atoms[HIDDEN]
    dn = atoms[DN]
    dh = atoms[DH]
    z = atoms[Z]
    moved_h = fold_rows(total[...]) * (1.0 / DEG)
    rms = lax.rsqrt(jnp.mean(hidden * hidden, axis=0, keepdims=True) + 1e-05)
    cube = rms * rms * rms
    cross = jnp.mean(hidden * moved_h, axis=0, keepdims=True)
    normed = hidden * rms
    moved_n = rms * moved_h - (cube * cross) * hidden
    moved_n2 = stack(moved_n)
    moved_z = wdot(update_t, moved_n2)
    sig, slope, second = silu_parts(z)
    live_atom = (iota((1, A), 1) < count).astype(f32)
    weighted = readout * live_atom
    z_bar = weighted * (energy_cot * slope + second * moved_z)
    z_bar = stack(z_bar)
    update_grad = fold(
        mm(
            jnp.concatenate([z_bar, stack(weighted * slope)], axis=1),
            jnp.concatenate([stack(normed), moved_n2], axis=1),
            NT,
        )
    )
    readout_grad = jnp.sum(live_atom * (energy_cot * (z * sig) + slope * moved_z), axis=1, keepdims=True)
    n_bar = wdot(update, z_bar)
    dn_h = jnp.sum(dn * hidden, axis=0, keepdims=True) * (1.0 / C)
    mix = (jnp.sum(n_bar * hidden, axis=0, keepdims=True) + jnp.sum(dn * moved_h, axis=0, keepdims=True)) * (1.0 / C)
    h_bar = (
        rms * n_bar
        + hidden * (3.0 * cube * rms * rms * cross * dn_h - cube * mix)
        - moved_h * (cube * dn_h)
        - dn * (cube * cross)
    )
    for h in range(8):
        grad[:, 7 + h, :] = update_grad[64 * h : 64 * h + 64]
    lane64 = iota((64, 128), 1)
    block = jnp.zeros((64, 128), f32)
    for h in range(8):
        block = block + jnp.where(lane64 == h, readout_grad[64 * h : 64 * h + 64], 0.0)
    grad[:, 15, :] = block

    both_pieces = jnp.concatenate([wide(h_bar * (1.0 / DEG)), wide(dh * (1.0 / DEG))], axis=0)
    source_total[...] = jnp.zeros_like(source_total)
    one_total[...] = jnp.zeros_like(one_total)
    two_total[...] = jnp.zeros_like(two_total)
    centers = iota((K, EC), 0).astype(f32) * (cutoff / (K - 1))

    for i in range(CHUNKS):
        at = pl.ds(i * EC, EC)
        hot_s = src_hot[:, at]
        hot_t = dst_hot[:, at]
        step = step_row[:, at]
        gate = rows_in[2:3, at]
        dgate = rows_in[3:4, at]
        both = mm(both_pieces, twice(hot_t), NN)
        m_bar = both[:C]
        dm_bar = both[C:]
        q = q_in[:, at]
        dq = dm_bar * q
        f_bar = stack(m_bar * q * gate + dq * (dgate * step))
        df_bar = stack(dq * gate)
        s_bar = wdot(two, f_bar)
        ds_bar = wdot(two, df_bar)
        delta = rows_in[0:1, at] - centers
        basis = jnp.exp(-spread * delta * delta)
        moved_basis = (-2.0 * spread) * delta * basis * step
        basis = stack(basis)
        moved_basis = stack(moved_basis)
        a = mm(one_t, deep(basis), NN)
        moved_a = mm(one_t, deep(moved_basis), NN)
        sig, slope, second = silu_parts(a)
        inner = stack(a * sig)
        filt = wdot(two_t, inner) * gate
        source_total[...] += mm(stack(m_bar * filt + dm_bar * (dfilt_in[:, at] * step)), hot_s, NT)
        two_total[...] += mm(f_bar, inner, NT) + mm(df_bar, stack(slope * moved_a), NT)
        a_bar = stack(s_bar * slope + ds_bar * (second * moved_a))
        da_bar = stack(ds_bar * slope)
        one_total[...] += mm(a_bar, basis, NT) + mm(da_bar, moved_basis, NT)

    one_grad = fold(one_total[...])
    grad[:, 2, :] = jnp.concatenate([one_grad[:64], one_grad[64:]], axis=1)
    two_grad = fold(two_total[...])
    grad[:, 3, :] = two_grad[:64]
    grad[:, 4, :] = two_grad[64:]
    p_bar = fold_rows(source_total[...])
    p_bar = jnp.concatenate([p_bar, jnp.zeros((C, 256 - N), f32)], axis=1)
    p_pieces = stack(p_bar)
    emb = jnp.concatenate([atoms[EMB_OWN], atoms[EMB_GHOST]], axis=1)
    message_grad = fold(mm(p_pieces, stack(emb), NT))
    grad[:, 5, :] = message_grad[:64]
    grad[:, 6, :] = message_grad[64:]
    emb_bar = wdot(message_w, p_pieces)
    emb_bar = jnp.concatenate([emb_bar[:, :A] + h_bar, emb_bar[:, A:]], axis=1)
    kinds = jnp.concatenate([own[3:4], ghost[3:4]], axis=1).astype(jnp.int32)
    kind_hot = (iota((128, 256), 0) == kinds).astype(f32).astype(bf16)
    table_grad = fold_rows(mm(stack(emb_bar), kind_hot, NT))
    grad[:, 0, :] = table_grad[:64]
    grad[:, 1, :] = table_grad[64:]
    for j in range(32):
        keep[j] = grad[2 * j + core]
        give[j] = grad[2 * j + 1 - core]


vmem = pl.BlockSpec(memory_space=pltpu.VMEM)
smem = pl.BlockSpec(memory_space=pltpu.SMEM)
params_vmem = pltpu.CompilerParams(vmem_limit_bytes=32 * 1024 * 1024)


def shape(*dims, dtype=jnp.float32):
    return jax.ShapeDtypeStruct(dims, dtype)


def prepare(shards, *arrays):
    return pl.pallas_call(
        prepare_kernel,
        out_shape=[shape(16, 128), shape(8, 128), shape(shards, BLOCKS, 128)],
        in_specs=[vmem] * len(arrays),
        out_specs=[vmem] * 3,
        compiler_params=pltpu.CompilerParams(vmem_limit_bytes=60 * 1024 * 1024),
        name="prepare",
    )(*arrays)


def forward(slabs, counts, scalars, wg, *arrays):
    return pl.pallas_call(
        functools.partial(forward_kernel, slabs),
        out_shape=[shape(8, 4, 128)] + [shape(*dims) for dims in KEPT],
        in_specs=[smem] * 2 + [vmem] * (1 + len(arrays)),
        out_specs=[vmem] * (1 + len(KEPT)),
        scratch_shapes=[
            pltpu.VMEM((N, E), bf16),
            pltpu.VMEM((A, E), bf16),
            pltpu.VMEM((2 * C, A), f32),
            pltpu.VMEM((24, 256), f32),
        ],
        compiler_params=params_vmem,
        name="energy_slopes",
    )(counts, scalars, wg, *arrays)


def backward(slabs, counts, scalars, energy_ref, *arrays):
    outs = [shape(8, 128), shape(8, 128), shape(32, BLOCKS, 128), shape(32, BLOCKS, 128)]
    return pl.pallas_call(
        functools.partial(backward_kernel, slabs),
        out_shape=outs,
        in_specs=[smem] * 3 + [vmem] * len(arrays),
        out_specs=[vmem] * 4,
        scratch_shapes=[
            pltpu.VMEM((N, E), bf16),
            pltpu.VMEM((A, E), bf16),
            pltpu.VMEM((64, BLOCKS, 128), f32),
            pltpu.VMEM((1, E), f32),
            pltpu.VMEM((2 * C, A), f32),
            pltpu.VMEM((2 * C, N), f32),
            pltpu.VMEM((2 * C, 2 * K), f32),
            pltpu.VMEM((2 * C, 2 * C), f32),
        ],
        compiler_params=params_vmem,
        name="weight_gradients",
    )(counts, scalars, energy_ref, *arrays)


def from_blocks(y):
    two = jnp.concatenate([y[0:2, :100], y[2].reshape(2, 64), y[3:5], y[5:7]], axis=1)
    return jnp.concatenate([two.T.reshape(-1), y[7:15].T.reshape(-1), y[15, :56]])


def decay(params, moment_one, moment_two):
    return params - (0.001 * 0.01) * params, 0.9 * moment_one, 0.999 * moment_two


def adam(params, moment_one, moment_two, grad):
    new_moment_one = moment_one + 0.1 * grad
    new_moment_two = moment_two + 0.001 * grad * grad
    corrected_one = new_moment_one / (1.0 - 0.9**STEP)
    corrected_two = new_moment_two / (1.0 - 0.999**STEP)
    new_params = params - 0.001 * (corrected_one / (jnp.sqrt(corrected_two) + 1e-08))
    return new_params, new_moment_one, new_moment_two


def body(
    positions,
    species,
    counts,
    source,
    target,
    send_left,
    send_right,
    energy_ref,
    force_ref,
    stress_ref,
    params,
    moment_one,
    moment_two,
):
    shards = lax.axis_size("dp")
    slabs = lax.axis_size("graph")
    rank = lax.axis_index("graph")
    index = lax.axis_index("dp")
    core = index % 2
    scalars = jnp.stack([rank, core]).astype(jnp.int32)
    own, outgoing, blocks = prepare(
        shards,
        positions.reshape(3, 1, A),
        species[0],
        force_ref.reshape(3, 1, A),
        send_left[0],
        send_right[0],
        stress_ref.reshape(3, 1, 3),
        params,
    )
    wg = lax.all_to_all(blocks, "dp", 0, 0, tiled=True)
    first = lax.ppermute(outgoing, "graph", [(i, i ^ 1) for i in range(slabs)])
    second = lax.ppermute(
        outgoing, "graph", [(i, (i + (1 if i % 2 else slabs - 1)) % slabs) for i in range(slabs)]
    )
    message, *kept = forward(
        slabs, counts, scalars, wg, own, first, second, source[0], target[0]
    )
    received = lax.all_to_all(message, "graph", 0, 0, tiled=True)
    forces, sums, keep, give = backward(
        slabs, counts, scalars, energy_ref, wg, source[0], target[0], received, *kept
    )
    volume = slabs * slab_width * cross_area
    decayed = lax.optimization_barrier(decay(params, moment_one, moment_two))
    pair = keep + lax.ppermute(give, "dp", [(i, i ^ 1) for i in range(shards)])
    chips = [list(range(c, shards, 2)) for c in range(2)]
    within = jnp.sum(
        lax.all_to_all(pair, "dp", 0, 0, tiled=True, axis_index_groups=chips), axis=0
    )
    copies = jnp.broadcast_to(within[None], (slabs, BLOCKS, 128))
    grad = from_blocks(jnp.sum(lax.all_to_all(copies, "graph", 0, 0, tiled=True), axis=0))
    new_params, new_moment_one, new_moment_two = adam(*decayed, grad)
    return (
        new_params,
        new_moment_one,
        new_moment_two,
        forces[:3][None, None],
        sums[3, 9][None],
        (sums[3, :9] / volume).reshape(1, 3, 3),
    )


def solution(mesh):
    in_specs = (
        P("dp", "graph", None, None),
        P("dp", "graph", None),
        P("dp", "graph"),
        P("dp", "graph", None),
        P("dp", "graph", None),
        P("dp", "graph", None),
        P("dp", "graph", None),
        P("dp"),
        P("dp", "graph", None, None),
        P("dp", None, None),
        P("dp"),
        P("dp"),
        P("dp"),
    )
    out_specs = (
        P("dp"),
        P("dp"),
        P("dp"),
        P("dp", "graph", None, None),
        P("dp"),
        P("dp", None, None),
    )
    return jax.shard_map(body, mesh=mesh, in_specs=in_specs, out_specs=out_specs, check_vma=False)
```

```python
import functools
import jax
import jax.numpy as jnp
from jax import lax
from jax.experimental import pallas as pl
from jax.experimental.pallas import tpu as pltpu
from jax.sharding import PartitionSpec as P

C = 128
FF = 512
K = 64
NS = 100
A = 128
G = 32
DEG = 16
STEP = 100
E = A * DEG
N = A + 2 * G
EC = 1024
CHUNKS = E // EC
BLOCKS = 16
HIDDEN, DN, DH, EMB_OWN, EMB_GHOST = (slice(C * i, C * i + C) for i in range(5))
Z = slice(5 * C, 5 * C + FF)
GHOST, CONTRIB_OWN, CONTRIB_GHOST = (slice(9 * C + 8 * i, 9 * C + 8 * i + 8) for i in range(3))
OWN = slice(9 * C + 24, 9 * C + 40)
KEPT = [(9 * C + 40, A), (8, E), (8, E), (C, E), (C, E)]

highest = lax.Precision.HIGHEST
cutoff = 6.0
slab_width = 20.0
cross_area = 36.0
force_weight = 10.0
stress_weight = 100.0
spread = 0.5 * ((K - 1) / cutoff) ** 2

f32 = jnp.float32
bf16 = jnp.bfloat16
NN = ((1,), (0,))
NT = ((1,), (1,))


def split(x):
    high = x.astype(bf16)
    return high, (x - high.astype(f32)).astype(bf16)


def mm(a, b, dims):
    return lax.dot_general(a, b, (dims, ((), ())), preferred_element_type=f32)


def stack(x):
    return jnp.concatenate(split(x), axis=0)


def fold_rows(x):
    half = x.shape[0] // 2
    return x[:half] + x[half:]


def fold(x):
    half = x.shape[1] // 2
    x = fold_rows(x)
    return x[:, :half] + x[:, half:]


def lhs(w):
    high, low = split(w)
    return jnp.concatenate(
        [jnp.concatenate([high, high], axis=1), jnp.concatenate([low, jnp.zeros_like(low)], axis=1)], axis=0
    )


def wdot(w, x):
    return fold_rows(mm(w, x, NN))


def lhs_deep(w):
    high, low = split(w)
    return jnp.concatenate([high, high, low], axis=1)


def deep(pair):
    return jnp.concatenate([pair, pair[: pair.shape[0] // 2]], axis=0)


def wide(x):
    return jnp.concatenate(split(x), axis=1)


def twice(x):
    return jnp.concatenate([x, x], axis=0)


def exact(x):
    one = x.astype(bf16).astype(f32)
    two = (x - one).astype(bf16).astype(f32)
    return jnp.concatenate([one, two, x - one - two], axis=0).astype(bf16)


def whole(x):
    return x[0:8] + x[8:16] + x[16:24]


def full_dot(a, b, dims):
    return lax.dot_general(a, b, (dims, ((), ())), precision=highest, preferred_element_type=f32)


def iota(shape, dim):
    return lax.broadcasted_iota(jnp.int32, shape, dim)


def select_lists(own):
    return (iota((A, 128), 0) == own[8:9].astype(jnp.int32)).astype(f32)


def pack_own(positions, species, force_ref, send_left, send_right, stress_ref):
    lane = iota((1, A), 1)
    refs = jnp.zeros((1, A), f32)
    for i in range(3):
        for j in range(3):
            refs = refs + jnp.where(lane == 3 * i + j, stress_ref[i][:, j : j + 1], 0.0)
    rows = [positions[i] for i in range(3)] + [species[...].astype(f32)]
    lists = jnp.concatenate(
        [send_right[...], send_left[...], jnp.full((1, 128 - 2 * G), -1, jnp.int32)], axis=1
    )
    rows = rows + [force_ref[i] for i in range(3)] + [refs, lists.astype(f32), jnp.zeros((7, A), f32)]
    return jnp.concatenate(rows, axis=0)


def place(pieces, stride, offset, first, last):
    lane = iota((8, 128), 1)
    row = iota((8, 128), 0)
    column = iota((128, 128), 0)
    slot = iota((128, 128), 1)
    lefts, rights = [], []
    for i in range(first, last + 1):
        chosen = [jnp.where(lane % stride == row, p[:, 128 * i : 128 * i + 128], 0.0) for p in pieces]
        lefts.append(jnp.concatenate(chosen, axis=0))
        rights.append((column // stride + (128 // stride) * i == slot + offset).astype(f32))
    return whole(
        mm(
            jnp.concatenate(lefts, axis=1).astype(bf16),
            jnp.concatenate(rights, axis=0).astype(bf16),
            NN,
        )
    )


def prepare_kernel(
    positions, species, force_ref, send_left, send_right, stress_ref, shard, own_out, outgoing, blocks
):
    own = pack_own(positions, species, force_ref, send_left, send_right, stress_ref)
    own_out[...] = own
    outgoing[...] = full_dot(own[:8], select_lists(own), NN)
    x = shard[...].reshape(1, 1920)
    one = x.astype(bf16).astype(f32)
    two = (x - one).astype(bf16).astype(f32)
    pieces = [one, two, x - one - two]
    table = place(pieces, 2, 0, 0, 1)
    radial = place(pieces, 2, 100, 1, 2)
    lane = iota((1, 128), 1)
    block = jnp.concatenate(
        [
            table[:2],
            jnp.where(lane < K, radial[:1], pltpu.roll(radial[1:2], K, 1)),
            place(pieces, 2, 164, 2, 4)[:2],
            place(pieces, 2, 292, 4, 6)[:2],
            place(pieces, 8, 105, 6, 14),
            jnp.where(lane < 56, pltpu.roll(x[:, 14 * 128 :], 56, 1), 0.0),
        ],
        axis=0,
    )
    for j in range(blocks.shape[0]):
        blocks[j] = block


def weight(wg, first):
    return jnp.concatenate([wg[:, first, :], wg[:, first + 1, :]], axis=0)


def update_weight_t(wg):
    return jnp.concatenate([wg[:, 7 + h, :] for h in range(8)], axis=0)


def readout_column(wg):
    block = wg[:, 15, :]
    return jnp.concatenate([block[:, h : h + 1] for h in range(8)], axis=0)


def radial_one_t(wg):
    block = wg[:, 2, :]
    return jnp.concatenate([block[:, :K], block[:, K:]], axis=0)


def silu_parts(a):
    t = jnp.tanh(0.5 * a)
    sig = 0.5 * t + 0.5
    peak = 0.25 - 0.25 * (t * t)
    return sig, sig + a * peak, peak * (2.0 - a * t)


def one_hots(s, t):
    s = jnp.where(s < G, s + A, jnp.where(s < G + A, s - G, s))
    hot_s = (iota((N, EC), 0) == s).astype(f32).astype(bf16)
    hot_t = (iota((A, EC), 0) == t).astype(f32).astype(bf16)
    return hot_s, hot_t


def forward_kernel(
    slabs, count_ref, scalars, energy_ref, wg, own, first_ghost, second_ghost, src, dst,
    message, atoms, rows_out, vec_out, dfilt_out, q_out,
    src_hot, dst_hot, total, force_total,
):

    count = count_ref[0, 0]
    rank = scalars[0]
    box = slab_width * slabs
    table_t = weight(wg, 0)
    one_t = lhs_deep(radial_one_t(wg))
    two_t = lhs(weight(wg, 3))
    message_t = lhs(weight(wg, 5))
    update_f = update_weight_t(wg)
    update_t = lhs(update_f)
    update = lhs(update_f.T)
    readout = readout_column(wg)

    own = own[...]
    own_rows = own[:8]
    lane = iota((8, 128), 1)
    row = iota((8, 128), 0)
    ghost_rows = jnp.where((lane < G) == (rank % 2 == 1), first_ghost[...], second_ghost[...])
    atoms[OWN] = jnp.where((iota(own.shape, 0) == 7) & (iota(own.shape, 1) == 9), energy_ref[0], own)
    atoms[GHOST] = ghost_rows
    shift = jnp.where(lane < G, jnp.where(rank == 0, -box, 0.0), 0.0)
    shift = shift + jnp.where((lane >= G) & (lane < 2 * G), jnp.where(rank == slabs - 1, box, 0.0), 0.0)
    ghost_pos = ghost_rows + jnp.where(row == 0, shift, 0.0)
    ext = jnp.concatenate([own_rows, ghost_pos], axis=1)
    pieces = exact(jnp.where(iota((8, 256), 0) < 3, ext, 0.0))
    kinds = ext[3:4, :].astype(jnp.int32)
    kind_hot = (iota((128, 256), 0) == kinds).astype(f32)
    table_hi, table_rest = split(table_t)
    table_lo = (table_t - table_hi.astype(f32) - table_rest.astype(f32)).astype(bf16)
    kind_bf = kind_hot.astype(bf16)
    emb = mm(table_hi, kind_bf, NN) + mm(table_rest, kind_bf, NN) + mm(table_lo, kind_bf, NN)
    atoms[EMB_OWN] = emb[:, :A]
    atoms[EMB_GHOST] = emb[:, A:]
    projected = stack(wdot(message_t, stack(emb)))[:, :N]
    total[...] = jnp.zeros_like(total)
    centers = iota((K, EC), 0).astype(f32) * (cutoff / (K - 1))

    for i in range(CHUNKS):
        at = pl.ds(i * EC, EC)
        t = dst[:, at]
        hot_s, hot_t = one_hots(src[:, at], t)
        src_hot[:, at] = hot_s
        dst_hot[:, at] = hot_t
        vec = whole(mm(pieces[:, :N], hot_s, NN) - mm(pieces[:, :A], hot_t, NN))
        vec_out[:, at] = vec
        square = jnp.sum(vec * vec, axis=0, keepdims=True)
        dist = jnp.sqrt(square)
        inverse = jnp.where(square > 0.0, 1.0 / jnp.where(square > 0.0, dist, 1.0), 0.0)
        ratio = jnp.minimum(dist / cutoff, 1.0)
        live = (t < count).astype(f32)
        inside = 1.0 - ratio * ratio
        gate = inside * inside * live
        dgate = inside * ratio * (-4.0 / cutoff) * live
        rows_out[0:1, at] = dist
        rows_out[1:2, at] = inverse
        rows_out[2:3, at] = gate
        rows_out[3:4, at] = dgate
        delta = dist - centers
        basis = jnp.exp(-spread * delta * delta)
        dbasis = (-2.0 * spread) * delta * basis
        a = mm(one_t, deep(stack(basis)), NN)
        da = mm(one_t, deep(stack(dbasis)), NN)
        sig, slope, second = silu_parts(a)
        f = wdot(two_t, stack(a * sig))
        df = wdot(two_t, stack(slope * da))
        filt = f * gate
        dfilt = df * gate + f * dgate
        q = fold_rows(mm(projected, hot_s, NN))
        dfilt_out[:, at] = dfilt
        q_out[:, at] = q
        total[...] += mm(stack(filt * q), hot_t, NT)

    hidden = emb[:, :A] + fold_rows(total[...]) * (1.0 / DEG)
    atoms[HIDDEN] = hidden
    rms = lax.rsqrt(jnp.mean(hidden * hidden, axis=0, keepdims=True) + 1e-05)
    z = wdot(update_t, stack(hidden * rms))
    atoms[Z] = z
    sig, slope, second = silu_parts(z)
    live_atom = (iota((1, A), 1) < count).astype(f32)
    weighted = readout * live_atom
    energy = jnp.sum(jnp.sum(weighted * (z * sig), axis=0, keepdims=True), axis=1, keepdims=True)
    dn = wdot(update, stack(weighted * slope))
    atoms[DN] = dn
    cube = rms * rms * rms * (1.0 / C)
    dh = rms * dn - hidden * (cube * jnp.sum(dn * hidden, axis=0, keepdims=True))
    atoms[DH] = dh
    dh_pieces = wide(dh * (1.0 / DEG))
    force_total[...] = jnp.zeros_like(force_total)

    stress = [jnp.zeros((8, 1), f32) for _ in range(3)]
    for i in range(CHUNKS):
        at = pl.ds(i * EC, EC)
        hot_s = src_hot[:, at]
        hot_t = dst_hot[:, at]
        back = mm(dh_pieces, twice(hot_t), NN)
        along = jnp.sum(back * (dfilt_out[:, at] * q_out[:, at]), axis=0, keepdims=True)
        vec = vec_out[:, at]
        slopes = vec * (along * rows_out[1:2, at])
        three = exact(slopes)
        force_total[:, :N] += mm(three, hot_s, NT)
        force_total[:, :A] -= mm(three, hot_t, NT)
        stress = [
            stress[j] + jnp.sum(slopes * vec[j : j + 1], axis=1, keepdims=True) for j in range(3)
        ]

    contrib = whole(force_total[...])
    atoms[CONTRIB_OWN] = contrib[:, :A]
    atoms[CONTRIB_GHOST] = contrib[:, A:]
    lists_hot = select_lists(own)
    outgoing = full_dot(contrib[:, :A], lists_hot, NN) + pltpu.roll(contrib[:, A:], 64, 1)
    to_right = (lane < G) | (lane >= 96)
    sums = jnp.zeros((8, 128), f32)
    for i in range(3):
        for j in range(3):
            sums = sums + jnp.where(lane == 3 * i + j, stress[j][i : i + 1], 0.0)
    sums = sums + jnp.where(lane == 9, energy, 0.0)
    right = lax.rem(rank + 1, slabs)
    left = lax.rem(rank + slabs - 1, slabs)
    for d in range(8):
        keep = (to_right & (right == d)) | (jnp.logical_not(to_right) & (left == d))
        message[d] = jnp.where(row == 3, sums, jnp.where(keep, outgoing, 0.0))[:4]


def backward_kernel(
    slabs, count_ref, scalars, wg, src, dst, received, atoms, rows_in, vec_in, dfilt_in, q_in,
    forces_out, energy_out, stress_out, keep, give,
    src_hot, dst_hot, grad, step_row, total, source_total, one_total, two_total,
):

    count = count_ref[0, 0]
    core = scalars[1]
    volume = slab_width * cross_area * slabs
    scale = 2.0 / (slabs * A)
    one_t = lhs_deep(radial_one_t(wg))
    two_f = weight(wg, 3)
    two_t = lhs(two_f)
    two = lhs(two_f.T)
    message_w = lhs(weight(wg, 5).T)
    update_f = update_weight_t(wg)
    update_t = lhs(update_f)
    update = lhs(update_f.T)
    readout = readout_column(wg)
    own = atoms[OWN]
    lists_hot = select_lists(own)
    lane = iota((8, 128), 1)
    row = iota((8, 128), 0)
    ghost = atoms[GHOST]

    got = jnp.sum(received[...], axis=0)
    got = jnp.concatenate([got, jnp.zeros_like(got)], axis=0)
    moved = jnp.where(row < 3, got, 0.0)
    energy = got[3:4, 9:10]
    inner = jnp.where(lane < 2 * G, pltpu.roll(moved, 64, 1), 0.0)
    force_own = -(atoms[CONTRIB_OWN] + full_dot(inner, lists_hot, NT))
    force_ghost = -(atoms[CONTRIB_GHOST] + jnp.where(lane < 2 * G, moved, 0.0))
    for i in range(3):
        forces_out[i] = force_own[i : i + 1]
        stress_out[i] = got[3:4, 3 * i : 3 * i + 3] / volume
    energy_out[...] = energy
    own_ref = jnp.concatenate([own[4:8], jnp.zeros((4, 128), f32)], axis=0)
    ghost_ref = jnp.concatenate([ghost[4:8], jnp.zeros((4, 128), f32)], axis=0)
    factor = force_weight * scale
    cot_own = jnp.where((lane < count) & (row < 3), factor * (force_own - own_ref), 0.0)
    cot_ghost = jnp.where((lane < 2 * G) & (row < 3), factor * (force_ghost - ghost_ref), 0.0)
    cot = exact(jnp.concatenate([cot_own, cot_ghost], axis=1))
    stress_row = (2.0 * stress_weight / volume) * (got[3:4] / volume - own[7:8])
    stress_cot = [[stress_row[:, 3 * i + j : 3 * i + j + 1] for j in range(3)] for i in range(3)]
    energy_cot = (energy - own[7:8, 9:10]) * scale
    total[...] = jnp.zeros_like(total)

    for i in range(CHUNKS):
        at = pl.ds(i * EC, EC)
        hot_s, hot_t = one_hots(src[:, at], dst[:, at])
        src_hot[:, at] = hot_s
        dst_hot[:, at] = hot_t
        vec = vec_in[:, at]
        delta = whole(mm(cot[:, :A], hot_t, NN) - mm(cot[:, :N], hot_s, NN))
        along = jnp.sum(vec * delta, axis=0, keepdims=True)
        for r in range(3):
            inner_row = sum(stress_cot[r][j] * vec[j : j + 1] for j in range(3))
            along = along + vec[r : r + 1] * inner_row
        step = along * rows_in[1:2, at]
        step_row[:, at] = step
        total[...] += mm(stack(dfilt_in[:, at] * q_in[:, at] * step), hot_t, NT)

    hidden = atoms[HIDDEN]
    dn = atoms[DN]
    dh = atoms[DH]
    z = atoms[Z]
    moved_h = fold_rows(total[...]) * (1.0 / DEG)
    rms = lax.rsqrt(jnp.mean(hidden * hidden, axis=0, keepdims=True) + 1e-05)
    cube = rms * rms * rms
    cross = jnp.mean(hidden * moved_h, axis=0, keepdims=True)
    normed = hidden * rms
    moved_n = rms * moved_h - (cube * cross) * hidden
    moved_n2 = stack(moved_n)
    moved_z = wdot(update_t, moved_n2)
    sig, slope, second = silu_parts(z)
    live_atom = (iota((1, A), 1) < count).astype(f32)
    weighted = readout * live_atom
    z_bar = weighted * (energy_cot * slope + second * moved_z)
    z_bar = stack(z_bar)
    update_grad = fold(
        mm(
            jnp.concatenate([z_bar, stack(weighted * slope)], axis=1),
            jnp.concatenate([stack(normed), moved_n2], axis=1),
            NT,
        )
    )
    readout_grad = jnp.sum(live_atom * (energy_cot * (z * sig) + slope * moved_z), axis=1, keepdims=True)
    n_bar = wdot(update, z_bar)
    dn_h = jnp.sum(dn * hidden, axis=0, keepdims=True) * (1.0 / C)
    mix = (jnp.sum(n_bar * hidden, axis=0, keepdims=True) + jnp.sum(dn * moved_h, axis=0, keepdims=True)) * (1.0 / C)
    h_bar = (
        rms * n_bar
        + hidden * (3.0 * cube * rms * rms * cross * dn_h - cube * mix)
        - moved_h * (cube * dn_h)
        - dn * (cube * cross)
    )
    for h in range(8):
        grad[:, 7 + h, :] = update_grad[64 * h : 64 * h + 64]
    lane64 = iota((64, 128), 1)
    block = jnp.zeros((64, 128), f32)
    for h in range(8):
        block = block + jnp.where(lane64 == h, readout_grad[64 * h : 64 * h + 64], 0.0)
    grad[:, 15, :] = block

    both_pieces = jnp.concatenate([wide(h_bar * (1.0 / DEG)), wide(dh * (1.0 / DEG))], axis=0)
    source_total[...] = jnp.zeros_like(source_total)
    one_total[...] = jnp.zeros_like(one_total)
    two_total[...] = jnp.zeros_like(two_total)
    centers = iota((K, EC), 0).astype(f32) * (cutoff / (K - 1))

    for i in range(CHUNKS):
        at = pl.ds(i * EC, EC)
        hot_s = src_hot[:, at]
        hot_t = dst_hot[:, at]
        step = step_row[:, at]
        gate = rows_in[2:3, at]
        dgate = rows_in[3:4, at]
        both = mm(both_pieces, twice(hot_t), NN)
        m_bar = both[:C]
        dm_bar = both[C:]
        q = q_in[:, at]
        dq = dm_bar * q
        f_bar = stack(m_bar * q * gate + dq * (dgate * step))
        df_bar = stack(dq * gate)
        s_bar = wdot(two, f_bar)
        ds_bar = wdot(two, df_bar)
        delta = rows_in[0:1, at] - centers
        basis = jnp.exp(-spread * delta * delta)
        moved_basis = (-2.0 * spread) * delta * basis * step
        basis = stack(basis)
        moved_basis = stack(moved_basis)
        a = mm(one_t, deep(basis), NN)
        moved_a = mm(one_t, deep(moved_basis), NN)
        sig, slope, second = silu_parts(a)
        inner = stack(a * sig)
        filt = wdot(two_t, inner) * gate
        source_total[...] += mm(stack(m_bar * filt + dm_bar * (dfilt_in[:, at] * step)), hot_s, NT)
        two_total[...] += mm(f_bar, inner, NT) + mm(df_bar, stack(slope * moved_a), NT)
        a_bar = stack(s_bar * slope + ds_bar * (second * moved_a))
        da_bar = stack(ds_bar * slope)
        one_total[...] += mm(a_bar, basis, NT) + mm(da_bar, moved_basis, NT)

    one_grad = fold(one_total[...])
    grad[:, 2, :] = jnp.concatenate([one_grad[:64], one_grad[64:]], axis=1)
    two_grad = fold(two_total[...])
    grad[:, 3, :] = two_grad[:64]
    grad[:, 4, :] = two_grad[64:]
    p_bar = fold_rows(source_total[...])
    p_bar = jnp.concatenate([p_bar, jnp.zeros((C, 256 - N), f32)], axis=1)
    p_pieces = stack(p_bar)
    emb = jnp.concatenate([atoms[EMB_OWN], atoms[EMB_GHOST]], axis=1)
    message_grad = fold(mm(p_pieces, stack(emb), NT))
    grad[:, 5, :] = message_grad[:64]
    grad[:, 6, :] = message_grad[64:]
    emb_bar = wdot(message_w, p_pieces)
    emb_bar = jnp.concatenate([emb_bar[:, :A] + h_bar, emb_bar[:, A:]], axis=1)
    kinds = jnp.concatenate([own[3:4], ghost[3:4]], axis=1).astype(jnp.int32)
    kind_hot = (iota((128, 256), 0) == kinds).astype(f32).astype(bf16)
    table_grad = fold_rows(mm(stack(emb_bar), kind_hot, NT))
    grad[:, 0, :] = table_grad[:64]
    grad[:, 1, :] = table_grad[64:]
    for j in range(32):
        keep[j] = grad[2 * j + core]
        give[j] = grad[2 * j + 1 - core]


vmem = pl.BlockSpec(memory_space=pltpu.VMEM)
smem = pl.BlockSpec(memory_space=pltpu.SMEM)
params_vmem = pltpu.CompilerParams(vmem_limit_bytes=32 * 1024 * 1024)


def shape(*dims, dtype=jnp.float32):
    return jax.ShapeDtypeStruct(dims, dtype)


def prepare(shards, *arrays):
    return pl.pallas_call(
        prepare_kernel,
        out_shape=[shape(16, 128), shape(8, 128), shape(shards, BLOCKS, 128)],
        in_specs=[vmem] * len(arrays),
        out_specs=[vmem] * 3,
        compiler_params=pltpu.CompilerParams(vmem_limit_bytes=60 * 1024 * 1024),
        name="prepare",
    )(*arrays)


def forward(slabs, counts, scalars, energy_ref, *arrays):
    return pl.pallas_call(
        functools.partial(forward_kernel, slabs),
        out_shape=[shape(8, 4, 128)] + [shape(*dims) for dims in KEPT],
        in_specs=[smem] * 3 + [vmem] * len(arrays),
        out_specs=[vmem] * (1 + len(KEPT)),
        scratch_shapes=[
            pltpu.VMEM((N, E), bf16),
            pltpu.VMEM((A, E), bf16),
            pltpu.VMEM((2 * C, A), f32),
            pltpu.VMEM((24, 256), f32),
        ],
        compiler_params=params_vmem,
        name="energy_slopes",
    )(counts, scalars, energy_ref, *arrays)


def backward(slabs, counts, scalars, *arrays):
    outs = [shape(3, 1, A), shape(1, 1), shape(3, 1, 3), shape(32, BLOCKS, 128), shape(32, BLOCKS, 128)]
    return pl.pallas_call(
        functools.partial(backward_kernel, slabs),
        out_shape=outs,
        in_specs=[smem] * 2 + [vmem] * len(arrays),
        out_specs=[vmem] * len(outs),
        scratch_shapes=[
            pltpu.VMEM((N, E), bf16),
            pltpu.VMEM((A, E), bf16),
            pltpu.VMEM((64, BLOCKS, 128), f32),
            pltpu.VMEM((1, E), f32),
            pltpu.VMEM((2 * C, A), f32),
            pltpu.VMEM((2 * C, N), f32),
            pltpu.VMEM((2 * C, 2 * K), f32),
            pltpu.VMEM((2 * C, 2 * C), f32),
        ],
        compiler_params=params_vmem,
        name="weight_gradients",
    )(counts, scalars, *arrays)


def from_blocks(y):
    two = jnp.concatenate([y[0:2, :100], y[2].reshape(2, 64), y[3:5], y[5:7]], axis=1)
    return jnp.concatenate([two.T.reshape(-1), y[7:15].T.reshape(-1), y[15, :56]])


def decay(params, moment_one, moment_two):
    return params - (0.001 * 0.01) * params, 0.9 * moment_one, 0.999 * moment_two


def adam(params, moment_one, moment_two, grad):
    new_moment_one = moment_one + 0.1 * grad
    new_moment_two = moment_two + 0.001 * grad * grad
    corrected_one = new_moment_one / (1.0 - 0.9**STEP)
    corrected_two = new_moment_two / (1.0 - 0.999**STEP)
    new_params = params - 0.001 * (corrected_one / (jnp.sqrt(corrected_two) + 1e-08))
    return new_params, new_moment_one, new_moment_two


def body(
    positions,
    species,
    counts,
    source,
    target,
    send_left,
    send_right,
    energy_ref,
    force_ref,
    stress_ref,
    params,
    moment_one,
    moment_two,
):
    shards = lax.axis_size("dp")
    slabs = lax.axis_size("graph")
    rank = lax.axis_index("graph")
    index = lax.axis_index("dp")
    core = index % 2
    scalars = jnp.stack([rank, core]).astype(jnp.int32)
    own, outgoing, blocks = prepare(
        shards,
        positions.reshape(3, 1, A),
        species[0],
        force_ref.reshape(3, 1, A),
        send_left[0],
        send_right[0],
        stress_ref.reshape(3, 1, 3),
        params,
    )
    wg = lax.all_to_all(blocks, "dp", 0, 0, tiled=True)
    first = lax.ppermute(outgoing, "graph", [(i, i ^ 1) for i in range(slabs)])
    second = lax.ppermute(
        outgoing, "graph", [(i, (i + (1 if i % 2 else slabs - 1)) % slabs) for i in range(slabs)]
    )
    wg, decayed = lax.optimization_barrier((wg, decay(params, moment_one, moment_two)))
    message, *kept = forward(
        slabs, counts, scalars, energy_ref, wg, own, first, second, source[0], target[0]
    )
    received = lax.all_to_all(message, "graph", 0, 0, tiled=True)
    forces, energy, stress, keep, give = backward(
        slabs, counts, scalars, wg, source[0], target[0], received, *kept
    )
    pair = keep + lax.ppermute(give, "dp", [(i, i ^ 1) for i in range(shards)])
    chips = [list(range(c, shards, 2)) for c in range(2)]
    within = jnp.sum(
        lax.all_to_all(pair, "dp", 0, 0, tiled=True, axis_index_groups=chips), axis=0
    )
    copies = jnp.broadcast_to(within[None], (slabs, BLOCKS, 128))
    grad = from_blocks(jnp.sum(lax.all_to_all(copies, "graph", 0, 0, tiled=True), axis=0))
    new_params, new_moment_one, new_moment_two = adam(*decayed, grad)
    return (
        new_params,
        new_moment_one,
        new_moment_two,
        forces.reshape(1, 1, 3, A),
        energy.reshape(1),
        stress.reshape(1, 3, 3),
    )


def solution(mesh):
    in_specs = (
        P("dp", "graph", None, None),
        P("dp", "graph", None),
        P("dp", "graph"),
        P("dp", "graph", None),
        P("dp", "graph", None),
        P("dp", "graph", None),
        P("dp", "graph", None),
        P("dp"),
        P("dp", "graph", None, None),
        P("dp", None, None),
        P("dp"),
        P("dp"),
        P("dp"),
    )
    out_specs = (
        P("dp"),
        P("dp"),
        P("dp"),
        P("dp", "graph", None, None),
        P("dp"),
        P("dp", None, None),
    )
    return jax.shard_map(body, mesh=mesh, in_specs=in_specs, out_specs=out_specs, check_vma=False)
```

```python
import functools
import jax
import jax.numpy as jnp
from jax import lax
from jax.experimental import pallas as pl
from jax.experimental.pallas import tpu as pltpu
from jax.sharding import PartitionSpec as P

C = 128
FF = 512
K = 64
NS = 100
A = 128
G = 32
DEG = 16
STEP = 100
E = A * DEG
N = A + 2 * G
EC = 1024
CHUNKS = E // EC
BLOCKS = 16
HIDDEN, DN, DH, EMB_OWN, EMB_GHOST = (slice(C * i, C * i + C) for i in range(5))
Z = slice(5 * C, 5 * C + FF)
GHOST, CONTRIB_OWN, CONTRIB_GHOST = (slice(9 * C + 8 * i, 9 * C + 8 * i + 8) for i in range(3))
OWN = slice(9 * C + 24, 9 * C + 40)
KEPT = [(9 * C + 40, A), (8, E), (8, E), (C, E), (C, E)]

highest = lax.Precision.HIGHEST
cutoff = 6.0
slab_width = 20.0
cross_area = 36.0
force_weight = 10.0
stress_weight = 100.0
spread = 0.5 * ((K - 1) / cutoff) ** 2

f32 = jnp.float32
bf16 = jnp.bfloat16
NN = ((1,), (0,))
NT = ((1,), (1,))


def split(x):
    high = x.astype(bf16)
    return high, (x - high.astype(f32)).astype(bf16)


def mm(a, b, dims):
    return lax.dot_general(a, b, (dims, ((), ())), preferred_element_type=f32)


def stack(x):
    return jnp.concatenate(split(x), axis=0)


def fold_rows(x):
    half = x.shape[0] // 2
    return x[:half] + x[half:]


def fold(x):
    half = x.shape[1] // 2
    x = fold_rows(x)
    return x[:, :half] + x[:, half:]


def lhs(w):
    high, low = split(w)
    return jnp.concatenate(
        [jnp.concatenate([high, high], axis=1), jnp.concatenate([low, jnp.zeros_like(low)], axis=1)], axis=0
    )


def wdot(w, x):
    return fold_rows(mm(w, x, NN))


def lhs_deep(w):
    high, low = split(w)
    return jnp.concatenate([high, high, low], axis=1)


def deep(pair):
    return jnp.concatenate([pair, pair[: pair.shape[0] // 2]], axis=0)


def wide(x):
    return jnp.concatenate(split(x), axis=1)


def twice(x):
    return jnp.concatenate([x, x], axis=0)


def exact(x):
    one = x.astype(bf16).astype(f32)
    two = (x - one).astype(bf16).astype(f32)
    return jnp.concatenate([one, two, x - one - two], axis=0).astype(bf16)


def whole(x):
    return x[0:8] + x[8:16] + x[16:24]


def full_dot(a, b, dims):
    return lax.dot_general(a, b, (dims, ((), ())), precision=highest, preferred_element_type=f32)


def iota(shape, dim):
    return lax.broadcasted_iota(jnp.int32, shape, dim)


def select_lists(own):
    return (iota((A, 128), 0) == own[8:9].astype(jnp.int32)).astype(f32)


def pack_own(positions, species, force_ref, send_left, send_right, stress_ref):
    lane = iota((1, A), 1)
    refs = jnp.zeros((1, A), f32)
    for i in range(3):
        for j in range(3):
            refs = refs + jnp.where(lane == 3 * i + j, stress_ref[i][:, j : j + 1], 0.0)
    rows = [positions[i] for i in range(3)] + [species[...].astype(f32)]
    lists = jnp.concatenate(
        [send_right[...], send_left[...], jnp.full((1, 128 - 2 * G), -1, jnp.int32)], axis=1
    )
    rows = rows + [force_ref[i] for i in range(3)] + [refs, lists.astype(f32), jnp.zeros((7, A), f32)]
    return jnp.concatenate(rows, axis=0)


def place(pieces, stride, offset, first, last):
    lane = iota((8, 128), 1)
    row = iota((8, 128), 0)
    column = iota((128, 128), 0)
    slot = iota((128, 128), 1)
    lefts, rights = [], []
    for i in range(first, last + 1):
        chosen = [jnp.where(lane % stride == row, p[:, 128 * i : 128 * i + 128], 0.0) for p in pieces]
        lefts.append(jnp.concatenate(chosen, axis=0))
        rights.append((column // stride + (128 // stride) * i == slot + offset).astype(f32))
    return whole(
        mm(
            jnp.concatenate(lefts, axis=1).astype(bf16),
            jnp.concatenate(rights, axis=0).astype(bf16),
            NN,
        )
    )


def prepare_kernel(
    positions, species, force_ref, send_left, send_right, stress_ref, shard, own_out, outgoing, blocks
):
    own = pack_own(positions, species, force_ref, send_left, send_right, stress_ref)
    own_out[...] = own
    outgoing[...] = full_dot(own[:8], select_lists(own), NN)
    x = shard[...].reshape(1, 1920)
    one = x.astype(bf16).astype(f32)
    two = (x - one).astype(bf16).astype(f32)
    pieces = [one, two, x - one - two]
    table = place(pieces, 2, 0, 0, 1)
    radial = place(pieces, 2, 100, 1, 2)
    lane = iota((1, 128), 1)
    block = jnp.concatenate(
        [
            table[:2],
            jnp.where(lane < K, radial[:1], pltpu.roll(radial[1:2], K, 1)),
            place(pieces, 2, 164, 2, 4)[:2],
            place(pieces, 2, 292, 4, 6)[:2],
            place(pieces, 8, 105, 6, 14),
            jnp.where(lane < 56, pltpu.roll(x[:, 14 * 128 :], 56, 1), 0.0),
        ],
        axis=0,
    )
    for j in range(blocks.shape[0]):
        blocks[j] = block


def weight(wg, first):
    return jnp.concatenate([wg[:, first, :], wg[:, first + 1, :]], axis=0)


def update_weight_t(wg):
    return jnp.concatenate([wg[:, 7 + h, :] for h in range(8)], axis=0)


def readout_column(wg):
    block = wg[:, 15, :]
    return jnp.concatenate([block[:, h : h + 1] for h in range(8)], axis=0)


def radial_one_t(wg):
    block = wg[:, 2, :]
    return jnp.concatenate([block[:, :K], block[:, K:]], axis=0)


def silu_parts(a):
    t = jnp.tanh(0.5 * a)
    sig = 0.5 * t + 0.5
    peak = 0.25 - 0.25 * (t * t)
    return sig, sig + a * peak, peak * (2.0 - a * t)


def one_hots(s, t):
    s = jnp.where(s < G, s + A, jnp.where(s < G + A, s - G, s))
    hot_s = (iota((N, EC), 0) == s).astype(f32).astype(bf16)
    hot_t = (iota((A, EC), 0) == t).astype(f32).astype(bf16)
    return hot_s, hot_t


def hot_kernel(src, dst, src_hot, dst_hot):
    for i in range(CHUNKS):
        at = pl.ds(i * EC, EC)
        src_hot[:, at], dst_hot[:, at] = one_hots(src[:, at], dst[:, at])


def forward_kernel(
    slabs, count_ref, scalars, energy_ref, wg, own, first_ghost, second_ghost, dst, src_hot, dst_hot,
    message, atoms, rows_out, vec_out, dfilt_out, q_out,
    total, force_total,
):

    count = count_ref[0, 0]
    rank = scalars[0]
    box = slab_width * slabs
    table_t = weight(wg, 0)
    one_t = lhs_deep(radial_one_t(wg))
    two_t = lhs(weight(wg, 3))
    message_t = lhs(weight(wg, 5))
    update_f = update_weight_t(wg)
    update_t = lhs(update_f)
    update = lhs(update_f.T)
    readout = readout_column(wg)

    own = own[...]
    own_rows = own[:8]
    lane = iota((8, 128), 1)
    row = iota((8, 128), 0)
    ghost_rows = jnp.where((lane < G) == (rank % 2 == 1), first_ghost[...], second_ghost[...])
    atoms[OWN] = jnp.where((iota(own.shape, 0) == 7) & (iota(own.shape, 1) == 9), energy_ref[0], own)
    atoms[GHOST] = ghost_rows
    shift = jnp.where(lane < G, jnp.where(rank == 0, -box, 0.0), 0.0)
    shift = shift + jnp.where((lane >= G) & (lane < 2 * G), jnp.where(rank == slabs - 1, box, 0.0), 0.0)
    ghost_pos = ghost_rows + jnp.where(row == 0, shift, 0.0)
    ext = jnp.concatenate([own_rows, ghost_pos], axis=1)
    pieces = exact(jnp.where(iota((8, 256), 0) < 3, ext, 0.0))
    kinds = ext[3:4, :].astype(jnp.int32)
    kind_hot = (iota((128, 256), 0) == kinds).astype(f32)
    table_hi, table_rest = split(table_t)
    table_lo = (table_t - table_hi.astype(f32) - table_rest.astype(f32)).astype(bf16)
    kind_bf = kind_hot.astype(bf16)
    emb = mm(table_hi, kind_bf, NN) + mm(table_rest, kind_bf, NN) + mm(table_lo, kind_bf, NN)
    atoms[EMB_OWN] = emb[:, :A]
    atoms[EMB_GHOST] = emb[:, A:]
    projected = stack(wdot(message_t, stack(emb)))[:, :N]
    total[...] = jnp.zeros_like(total)
    centers = iota((K, EC), 0).astype(f32) * (cutoff / (K - 1))

    for i in range(CHUNKS):
        at = pl.ds(i * EC, EC)
        t = dst[:, at]
        hot_s = src_hot[:, at]
        hot_t = dst_hot[:, at]
        vec = whole(mm(pieces[:, :N], hot_s, NN) - mm(pieces[:, :A], hot_t, NN))
        vec_out[:, at] = vec
        square = jnp.sum(vec * vec, axis=0, keepdims=True)
        dist = jnp.sqrt(square)
        inverse = jnp.where(square > 0.0, 1.0 / jnp.where(square > 0.0, dist, 1.0), 0.0)
        ratio = jnp.minimum(dist / cutoff, 1.0)
        live = (t < count).astype(f32)
        inside = 1.0 - ratio * ratio
        gate = inside * inside * live
        dgate = inside * ratio * (-4.0 / cutoff) * live
        rows_out[0:1, at] = dist
        rows_out[1:2, at] = inverse
        rows_out[2:3, at] = gate
        rows_out[3:4, at] = dgate
        delta = dist - centers
        basis = jnp.exp(-spread * delta * delta)
        dbasis = (-2.0 * spread) * delta * basis
        a = mm(one_t, deep(stack(basis)), NN)
        da = mm(one_t, deep(stack(dbasis)), NN)
        sig, slope, second = silu_parts(a)
        f = wdot(two_t, stack(a * sig))
        df = wdot(two_t, stack(slope * da))
        filt = f * gate
        dfilt = df * gate + f * dgate
        q = fold_rows(mm(projected, hot_s, NN))
        dfilt_out[:, at] = dfilt
        q_out[:, at] = q
        total[...] += mm(stack(filt * q), hot_t, NT)

    hidden = emb[:, :A] + fold_rows(total[...]) * (1.0 / DEG)
    atoms[HIDDEN] = hidden
    rms = lax.rsqrt(jnp.mean(hidden * hidden, axis=0, keepdims=True) + 1e-05)
    z = wdot(update_t, stack(hidden * rms))
    atoms[Z] = z
    sig, slope, second = silu_parts(z)
    live_atom = (iota((1, A), 1) < count).astype(f32)
    weighted = readout * live_atom
    energy = jnp.sum(jnp.sum(weighted * (z * sig), axis=0, keepdims=True), axis=1, keepdims=True)
    dn = wdot(update, stack(weighted * slope))
    atoms[DN] = dn
    cube = rms * rms * rms * (1.0 / C)
    dh = rms * dn - hidden * (cube * jnp.sum(dn * hidden, axis=0, keepdims=True))
    atoms[DH] = dh
    dh_pieces = wide(dh * (1.0 / DEG))
    force_total[...] = jnp.zeros_like(force_total)

    stress = [jnp.zeros((8, 1), f32) for _ in range(3)]
    for i in range(CHUNKS):
        at = pl.ds(i * EC, EC)
        hot_s = src_hot[:, at]
        hot_t = dst_hot[:, at]
        back = mm(dh_pieces, twice(hot_t), NN)
        along = jnp.sum(back * (dfilt_out[:, at] * q_out[:, at]), axis=0, keepdims=True)
        vec = vec_out[:, at]
        slopes = vec * (along * rows_out[1:2, at])
        three = exact(slopes)
        force_total[:, :N] += mm(three, hot_s, NT)
        force_total[:, :A] -= mm(three, hot_t, NT)
        stress = [
            stress[j] + jnp.sum(slopes * vec[j : j + 1], axis=1, keepdims=True) for j in range(3)
        ]

    contrib = whole(force_total[...])
    atoms[CONTRIB_OWN] = contrib[:, :A]
    atoms[CONTRIB_GHOST] = contrib[:, A:]
    lists_hot = select_lists(own)
    outgoing = full_dot(contrib[:, :A], lists_hot, NN) + pltpu.roll(contrib[:, A:], 64, 1)
    to_right = (lane < G) | (lane >= 96)
    sums = jnp.zeros((8, 128), f32)
    for i in range(3):
        for j in range(3):
            sums = sums + jnp.where(lane == 3 * i + j, stress[j][i : i + 1], 0.0)
    sums = sums + jnp.where(lane == 9, energy, 0.0)
    right = lax.rem(rank + 1, slabs)
    left = lax.rem(rank + slabs - 1, slabs)
    for d in range(8):
        keep = (to_right & (right == d)) | (jnp.logical_not(to_right) & (left == d))
        message[d] = jnp.where(row == 3, sums, jnp.where(keep, outgoing, 0.0))[:4]


def backward_kernel(
    slabs, count_ref, scalars, wg, src, dst, received, atoms, rows_in, vec_in, dfilt_in, q_in,
    forces_far, energy_far, stress_far, keep, give, forces_out, energy_out, stress_out, sems,
    src_hot, dst_hot, grad, step_row, total, source_total, one_total, two_total,
):

    count = count_ref[0, 0]
    core = scalars[1]
    volume = slab_width * cross_area * slabs
    scale = 2.0 / (slabs * A)
    one_t = lhs_deep(radial_one_t(wg))
    two_f = weight(wg, 3)
    two_t = lhs(two_f)
    two = lhs(two_f.T)
    message_w = lhs(weight(wg, 5).T)
    update_f = update_weight_t(wg)
    update_t = lhs(update_f)
    update = lhs(update_f.T)
    readout = readout_column(wg)
    own = atoms[OWN]
    lists_hot = select_lists(own)
    lane = iota((8, 128), 1)
    row = iota((8, 128), 0)
    ghost = atoms[GHOST]

    got = jnp.sum(received[...], axis=0)
    got = jnp.concatenate([got, jnp.zeros_like(got)], axis=0)
    moved = jnp.where(row < 3, got, 0.0)
    energy = got[3:4, 9:10]
    inner = jnp.where(lane < 2 * G, pltpu.roll(moved, 64, 1), 0.0)
    force_own = -(atoms[CONTRIB_OWN] + full_dot(inner, lists_hot, NT))
    force_ghost = -(atoms[CONTRIB_GHOST] + jnp.where(lane < 2 * G, moved, 0.0))
    for i in range(3):
        forces_out[i] = force_own[i : i + 1]
        stress_out[i] = got[3:4, 3 * i : 3 * i + 3] / volume
    energy_out[...] = energy
    results = ((forces_out, forces_far), (energy_out, energy_far), (stress_out, stress_far))
    copies = [pltpu.make_async_copy(near, far, sems.at[k]) for k, (near, far) in enumerate(results)]
    for copy in copies:
        copy.start()
    own_ref = jnp.concatenate([own[4:8], jnp.zeros((4, 128), f32)], axis=0)
    ghost_ref = jnp.concatenate([ghost[4:8], jnp.zeros((4, 128), f32)], axis=0)
    factor = force_weight * scale
    cot_own = jnp.where((lane < count) & (row < 3), factor * (force_own - own_ref), 0.0)
    cot_ghost = jnp.where((lane < 2 * G) & (row < 3), factor * (force_ghost - ghost_ref), 0.0)
    cot = exact(jnp.concatenate([cot_own, cot_ghost], axis=1))
    stress_row = (2.0 * stress_weight / volume) * (got[3:4] / volume - own[7:8])
    stress_cot = [[stress_row[:, 3 * i + j : 3 * i + j + 1] for j in range(3)] for i in range(3)]
    energy_cot = (energy - own[7:8, 9:10]) * scale
    total[...] = jnp.zeros_like(total)

    for i in range(CHUNKS):
        at = pl.ds(i * EC, EC)
        hot_s, hot_t = one_hots(src[:, at], dst[:, at])
        src_hot[:, at] = hot_s
        dst_hot[:, at] = hot_t
        vec = vec_in[:, at]
        delta = whole(mm(cot[:, :A], hot_t, NN) - mm(cot[:, :N], hot_s, NN))
        along = jnp.sum(vec * delta, axis=0, keepdims=True)
        for r in range(3):
            inner_row = sum(stress_cot[r][j] * vec[j : j + 1] for j in range(3))
            along = along + vec[r : r + 1] * inner_row
        step = along * rows_in[1:2, at]
        step_row[:, at] = step
        total[...] += mm(stack(dfilt_in[:, at] * q_in[:, at] * step), hot_t, NT)

    hidden = atoms[HIDDEN]
    dn = atoms[DN]
    dh = atoms[DH]
    z = atoms[Z]
    moved_h = fold_rows(total[...]) * (1.0 / DEG)
    rms = lax.rsqrt(jnp.mean(hidden * hidden, axis=0, keepdims=True) + 1e-05)
    cube = rms * rms * rms
    cross = jnp.mean(hidden * moved_h, axis=0, keepdims=True)
    normed = hidden * rms
    moved_n = rms * moved_h - (cube * cross) * hidden
    moved_n2 = stack(moved_n)
    moved_z = wdot(update_t, moved_n2)
    sig, slope, second = silu_parts(z)
    live_atom = (iota((1, A), 1) < count).astype(f32)
    weighted = readout * live_atom
    z_bar = weighted * (energy_cot * slope + second * moved_z)
    z_bar = stack(z_bar)
    update_grad = fold(
        mm(
            jnp.concatenate([z_bar, stack(weighted * slope)], axis=1),
            jnp.concatenate([stack(normed), moved_n2], axis=1),
            NT,
        )
    )
    readout_grad = jnp.sum(live_atom * (energy_cot * (z * sig) + slope * moved_z), axis=1, keepdims=True)
    n_bar = wdot(update, z_bar)
    dn_h = jnp.sum(dn * hidden, axis=0, keepdims=True) * (1.0 / C)
    mix = (jnp.sum(n_bar * hidden, axis=0, keepdims=True) + jnp.sum(dn * moved_h, axis=0, keepdims=True)) * (1.0 / C)
    h_bar = (
        rms * n_bar
        + hidden * (3.0 * cube * rms * rms * cross * dn_h - cube * mix)
        - moved_h * (cube * dn_h)
        - dn * (cube * cross)
    )
    for h in range(8):
        grad[:, 7 + h, :] = update_grad[64 * h : 64 * h + 64]
    lane64 = iota((64, 128), 1)
    block = jnp.zeros((64, 128), f32)
    for h in range(8):
        block = block + jnp.where(lane64 == h, readout_grad[64 * h : 64 * h + 64], 0.0)
    grad[:, 15, :] = block

    both_pieces = jnp.concatenate([wide(h_bar * (1.0 / DEG)), wide(dh * (1.0 / DEG))], axis=0)
    source_total[...] = jnp.zeros_like(source_total)
    one_total[...] = jnp.zeros_like(one_total)
    two_total[...] = jnp.zeros_like(two_total)
    centers = iota((K, EC), 0).astype(f32) * (cutoff / (K - 1))

    for i in range(CHUNKS):
        at = pl.ds(i * EC, EC)
        hot_s = src_hot[:, at]
        hot_t = dst_hot[:, at]
        step = step_row[:, at]
        gate = rows_in[2:3, at]
        dgate = rows_in[3:4, at]
        both = mm(both_pieces, twice(hot_t), NN)
        m_bar = both[:C]
        dm_bar = both[C:]
        q = q_in[:, at]
        dq = dm_bar * q
        f_bar = stack(m_bar * q * gate + dq * (dgate * step))
        df_bar = stack(dq * gate)
        s_bar = wdot(two, f_bar)
        ds_bar = wdot(two, df_bar)
        delta = rows_in[0:1, at] - centers
        basis = jnp.exp(-spread * delta * delta)
        moved_basis = (-2.0 * spread) * delta * basis * step
        basis = stack(basis)
        moved_basis = stack(moved_basis)
        a = mm(one_t, deep(basis), NN)
        moved_a = mm(one_t, deep(moved_basis), NN)
        sig, slope, second = silu_parts(a)
        inner = stack(a * sig)
        filt = wdot(two_t, inner) * gate
        source_total[...] += mm(stack(m_bar * filt + dm_bar * (dfilt_in[:, at] * step)), hot_s, NT)
        two_total[...] += mm(f_bar, inner, NT) + mm(df_bar, stack(slope * moved_a), NT)
        a_bar = stack(s_bar * slope + ds_bar * (second * moved_a))
        da_bar = stack(ds_bar * slope)
        one_total[...] += mm(a_bar, basis, NT) + mm(da_bar, moved_basis, NT)

    one_grad = fold(one_total[...])
    grad[:, 2, :] = jnp.concatenate([one_grad[:64], one_grad[64:]], axis=1)
    two_grad = fold(two_total[...])
    grad[:, 3, :] = two_grad[:64]
    grad[:, 4, :] = two_grad[64:]
    p_bar = fold_rows(source_total[...])
    p_bar = jnp.concatenate([p_bar, jnp.zeros((C, 256 - N), f32)], axis=1)
    p_pieces = stack(p_bar)
    emb = jnp.concatenate([atoms[EMB_OWN], atoms[EMB_GHOST]], axis=1)
    message_grad = fold(mm(p_pieces, stack(emb), NT))
    grad[:, 5, :] = message_grad[:64]
    grad[:, 6, :] = message_grad[64:]
    emb_bar = wdot(message_w, p_pieces)
    emb_bar = jnp.concatenate([emb_bar[:, :A] + h_bar, emb_bar[:, A:]], axis=1)
    kinds = jnp.concatenate([own[3:4], ghost[3:4]], axis=1).astype(jnp.int32)
    kind_hot = (iota((128, 256), 0) == kinds).astype(f32).astype(bf16)
    table_grad = fold_rows(mm(stack(emb_bar), kind_hot, NT))
    grad[:, 0, :] = table_grad[:64]
    grad[:, 1, :] = table_grad[64:]
    for j in range(32):
        keep[j] = grad[2 * j + core]
        give[j] = grad[2 * j + 1 - core]
    for copy in copies:
        copy.wait()


vmem = pl.BlockSpec(memory_space=pltpu.VMEM)
smem = pl.BlockSpec(memory_space=pltpu.SMEM)
far = pl.BlockSpec(memory_space=pl.ANY)
params_vmem = pltpu.CompilerParams(vmem_limit_bytes=32 * 1024 * 1024)


def shape(*dims, dtype=jnp.float32):
    return jax.ShapeDtypeStruct(dims, dtype)


def prepare(shards, *arrays):
    return pl.pallas_call(
        prepare_kernel,
        out_shape=[shape(16, 128), shape(8, 128), shape(shards, BLOCKS, 128)],
        in_specs=[vmem] * len(arrays),
        out_specs=[vmem] * 3,
        compiler_params=pltpu.CompilerParams(vmem_limit_bytes=60 * 1024 * 1024),
        name="prepare",
    )(*arrays)


def edge_hots(src, dst):
    return pl.pallas_call(
        hot_kernel,
        out_shape=[shape(N, E, dtype=bf16), shape(A, E, dtype=bf16)],
        in_specs=[vmem] * 2,
        out_specs=[vmem] * 2,
        compiler_params=params_vmem,
        name="edge_hots",
    )(src, dst)


def forward(slabs, counts, scalars, energy_ref, *arrays):
    return pl.pallas_call(
        functools.partial(forward_kernel, slabs),
        out_shape=[shape(8, 4, 128)] + [shape(*dims) for dims in KEPT],
        in_specs=[smem] * 3 + [vmem] * len(arrays),
        out_specs=[vmem] * (1 + len(KEPT)),
        scratch_shapes=[
            pltpu.VMEM((2 * C, A), f32),
            pltpu.VMEM((24, 256), f32),
        ],
        compiler_params=params_vmem,
        name="energy_slopes",
    )(counts, scalars, energy_ref, *arrays)


def backward(slabs, counts, scalars, *arrays):
    outs = [shape(3, 1, A), shape(1, 1), shape(3, 1, 3), shape(32, BLOCKS, 128), shape(32, BLOCKS, 128)]
    return pl.pallas_call(
        functools.partial(backward_kernel, slabs),
        out_shape=outs,
        in_specs=[smem] * 2 + [vmem] * len(arrays),
        out_specs=[far] * 3 + [vmem] * 2,
        scratch_shapes=[pltpu.VMEM(out.shape, f32) for out in outs[:3]]
        + [
            pltpu.SemaphoreType.DMA((3,)),
            pltpu.VMEM((N, E), bf16),
            pltpu.VMEM((A, E), bf16),
            pltpu.VMEM((64, BLOCKS, 128), f32),
            pltpu.VMEM((1, E), f32),
            pltpu.VMEM((2 * C, A), f32),
            pltpu.VMEM((2 * C, N), f32),
            pltpu.VMEM((2 * C, 2 * K), f32),
            pltpu.VMEM((2 * C, 2 * C), f32),
        ],
        compiler_params=params_vmem,
        name="weight_gradients",
    )(counts, scalars, *arrays)


def from_blocks(y):
    two = jnp.concatenate([y[0:2, :100], y[2].reshape(2, 64), y[3:5], y[5:7]], axis=1)
    return jnp.concatenate([two.T.reshape(-1), y[7:15].T.reshape(-1), y[15, :56]])


def decay(params, moment_one, moment_two):
    return params - (0.001 * 0.01) * params, 0.9 * moment_one, 0.999 * moment_two


def adam(params, moment_one, moment_two, grad):
    new_moment_one = moment_one + 0.1 * grad
    new_moment_two = moment_two + 0.001 * grad * grad
    corrected_one = new_moment_one / (1.0 - 0.9**STEP)
    corrected_two = new_moment_two / (1.0 - 0.999**STEP)
    new_params = params - 0.001 * (corrected_one / (jnp.sqrt(corrected_two) + 1e-08))
    return new_params, new_moment_one, new_moment_two


def body(
    positions,
    species,
    counts,
    source,
    target,
    send_left,
    send_right,
    energy_ref,
    force_ref,
    stress_ref,
    params,
    moment_one,
    moment_two,
):
    shards = lax.axis_size("dp")
    slabs = lax.axis_size("graph")
    rank = lax.axis_index("graph")
    index = lax.axis_index("dp")
    core = index % 2
    scalars = jnp.stack([rank, core]).astype(jnp.int32)
    own, outgoing, blocks = prepare(
        shards,
        positions.reshape(3, 1, A),
        species[0],
        force_ref.reshape(3, 1, A),
        send_left[0],
        send_right[0],
        stress_ref.reshape(3, 1, 3),
        params,
    )
    wg = lax.all_to_all(blocks, "dp", 0, 0, tiled=True)
    first = lax.ppermute(outgoing, "graph", [(i, i ^ 1) for i in range(slabs)])
    second = lax.ppermute(
        outgoing, "graph", [(i, (i + (1 if i % 2 else slabs - 1)) % slabs) for i in range(slabs)]
    )
    wg, decayed, hots = lax.optimization_barrier(
        (wg, decay(params, moment_one, moment_two), edge_hots(source[0], target[0]))
    )
    message, *kept = forward(
        slabs, counts, scalars, energy_ref, wg, own, first, second, target[0], *hots
    )
    received = lax.all_to_all(message, "graph", 0, 0, tiled=True)
    forces, energy, stress, keep, give = backward(
        slabs, counts, scalars, wg, source[0], target[0], received, *kept
    )
    pair = keep + lax.ppermute(give, "dp", [(i, i ^ 1) for i in range(shards)])
    chips = [list(range(c, shards, 2)) for c in range(2)]
    within = jnp.sum(
        lax.all_to_all(pair, "dp", 0, 0, tiled=True, axis_index_groups=chips), axis=0
    )
    copies = jnp.broadcast_to(within[None], (slabs, BLOCKS, 128))
    grad = from_blocks(jnp.sum(lax.all_to_all(copies, "graph", 0, 0, tiled=True), axis=0))
    new_params, new_moment_one, new_moment_two = adam(*decayed, grad)
    return (
        new_params,
        new_moment_one,
        new_moment_two,
        forces.reshape(1, 1, 3, A),
        energy.reshape(1),
        stress.reshape(1, 3, 3),
    )


def solution(mesh):
    in_specs = (
        P("dp", "graph", None, None),
        P("dp", "graph", None),
        P("dp", "graph"),
        P("dp", "graph", None),
        P("dp", "graph", None),
        P("dp", "graph", None),
        P("dp", "graph", None),
        P("dp"),
        P("dp", "graph", None, None),
        P("dp", None, None),
        P("dp"),
        P("dp"),
        P("dp"),
    )
    out_specs = (
        P("dp"),
        P("dp"),
        P("dp"),
        P("dp", "graph", None, None),
        P("dp"),
        P("dp", None, None),
    )
    return jax.shard_map(body, mesh=mesh, in_specs=in_specs, out_specs=out_specs, check_vma=False)
```

```python
import functools
import jax
import jax.numpy as jnp
from jax import lax
from jax.experimental import pallas as pl
from jax.experimental.pallas import tpu as pltpu
from jax.sharding import PartitionSpec as P

C = 128
FF = 512
K = 64
NS = 100
A = 128
G = 32
DEG = 16
STEP = 100
E = A * DEG
N = A + 2 * G
EC = 1024
CHUNKS = E // EC
BLOCKS = 16
HIDDEN, DN, DH, EMB_OWN, EMB_GHOST = (slice(C * i, C * i + C) for i in range(5))
Z = slice(5 * C, 5 * C + FF)
GHOST, CONTRIB_OWN, CONTRIB_GHOST = (slice(9 * C + 8 * i, 9 * C + 8 * i + 8) for i in range(3))
OWN = slice(9 * C + 24, 9 * C + 40)
KEPT = [(9 * C + 40, A), (8, E), (8, E), (C, E), (C, E)]

highest = lax.Precision.HIGHEST
cutoff = 6.0
slab_width = 20.0
cross_area = 36.0
force_weight = 10.0
stress_weight = 100.0
spread = 0.5 * ((K - 1) / cutoff) ** 2

f32 = jnp.float32
bf16 = jnp.bfloat16
NN = ((1,), (0,))
NT = ((1,), (1,))


def split(x):
    high = x.astype(bf16)
    return high, (x - high.astype(f32)).astype(bf16)


def mm(a, b, dims):
    return lax.dot_general(a, b, (dims, ((), ())), preferred_element_type=f32)


def stack(x):
    return jnp.concatenate(split(x), axis=0)


def fold_rows(x):
    half = x.shape[0] // 2
    return x[:half] + x[half:]


def fold(x):
    half = x.shape[1] // 2
    x = fold_rows(x)
    return x[:, :half] + x[:, half:]


def lhs(w):
    high, low = split(w)
    return jnp.concatenate(
        [jnp.concatenate([high, high], axis=1), jnp.concatenate([low, jnp.zeros_like(low)], axis=1)], axis=0
    )


def wdot(w, x):
    return fold_rows(mm(w, x, NN))


def lhs_deep(w):
    high, low = split(w)
    return jnp.concatenate([high, high, low], axis=1)


def deep(pair):
    return jnp.concatenate([pair, pair[: pair.shape[0] // 2]], axis=0)


def wide(x):
    return jnp.concatenate(split(x), axis=1)


def twice(x):
    return jnp.concatenate([x, x], axis=0)


def exact(x):
    one = x.astype(bf16).astype(f32)
    two = (x - one).astype(bf16).astype(f32)
    return jnp.concatenate([one, two, x - one - two], axis=0).astype(bf16)


def whole(x):
    return x[0:8] + x[8:16] + x[16:24]


def full_dot(a, b, dims):
    return lax.dot_general(a, b, (dims, ((), ())), precision=highest, preferred_element_type=f32)


def iota(shape, dim):
    return lax.broadcasted_iota(jnp.int32, shape, dim)


def select_lists(own):
    return (iota((A, 128), 0) == own[8:9].astype(jnp.int32)).astype(f32)


def pack_own(positions, species, force_ref, send_left, send_right, stress_ref):
    lane = iota((1, A), 1)
    refs = jnp.zeros((1, A), f32)
    for i in range(3):
        for j in range(3):
            refs = refs + jnp.where(lane == 3 * i + j, stress_ref[i][:, j : j + 1], 0.0)
    rows = [positions[i] for i in range(3)] + [species[...].astype(f32)]
    lists = jnp.concatenate(
        [send_right[...], send_left[...], jnp.full((1, 128 - 2 * G), -1, jnp.int32)], axis=1
    )
    rows = rows + [force_ref[i] for i in range(3)] + [refs, lists.astype(f32), jnp.zeros((7, A), f32)]
    return jnp.concatenate(rows, axis=0)


def place(pieces, stride, offset, first, last):
    lane = iota((8, 128), 1)
    row = iota((8, 128), 0)
    column = iota((128, 128), 0)
    slot = iota((128, 128), 1)
    lefts, rights = [], []
    for i in range(first, last + 1):
        chosen = [jnp.where(lane % stride == row, p[:, 128 * i : 128 * i + 128], 0.0) for p in pieces]
        lefts.append(jnp.concatenate(chosen, axis=0))
        rights.append((column // stride + (128 // stride) * i == slot + offset).astype(f32))
    return whole(
        mm(
            jnp.concatenate(lefts, axis=1).astype(bf16),
            jnp.concatenate(rights, axis=0).astype(bf16),
            NN,
        )
    )


def prepare_kernel(
    positions, species, force_ref, send_left, send_right, stress_ref, shard, own_out, outgoing, blocks
):
    own = pack_own(positions, species, force_ref, send_left, send_right, stress_ref)
    own_out[...] = own
    outgoing[...] = full_dot(own[:8], select_lists(own), NN)
    x = shard[...].reshape(1, 1920)
    one = x.astype(bf16).astype(f32)
    two = (x - one).astype(bf16).astype(f32)
    pieces = [one, two, x - one - two]
    table = place(pieces, 2, 0, 0, 1)
    radial = place(pieces, 2, 100, 1, 2)
    lane = iota((1, 128), 1)
    block = jnp.concatenate(
        [
            table[:2],
            jnp.where(lane < K, radial[:1], pltpu.roll(radial[1:2], K, 1)),
            place(pieces, 2, 164, 2, 4)[:2],
            place(pieces, 2, 292, 4, 6)[:2],
            place(pieces, 8, 105, 6, 14),
            jnp.where(lane < 56, pltpu.roll(x[:, 14 * 128 :], 56, 1), 0.0),
        ],
        axis=0,
    )
    for j in range(blocks.shape[0]):
        blocks[j] = block


def weight(wg, first):
    return jnp.concatenate([wg[:, first, :], wg[:, first + 1, :]], axis=0)


def update_weight_t(wg):
    return jnp.concatenate([wg[:, 7 + h, :] for h in range(8)], axis=0)


def readout_column(wg):
    block = wg[:, 15, :]
    return jnp.concatenate([block[:, h : h + 1] for h in range(8)], axis=0)


def radial_one_t(wg):
    block = wg[:, 2, :]
    return jnp.concatenate([block[:, :K], block[:, K:]], axis=0)


def silu_parts(a):
    t = jnp.tanh(0.5 * a)
    sig = 0.5 * t + 0.5
    peak = 0.25 - 0.25 * (t * t)
    return sig, sig + a * peak, peak * (2.0 - a * t)


def one_hots(s, t):
    s = jnp.where(s < G, s + A, jnp.where(s < G + A, s - G, s))
    hot_s = (iota((N, EC), 0) == s).astype(f32).astype(bf16)
    hot_t = (iota((A, EC), 0) == t).astype(f32).astype(bf16)
    return hot_s, hot_t


def hot_kernel(src, dst, src_hot, dst_hot):
    for i in range(CHUNKS):
        at = pl.ds(i * EC, EC)
        src_hot[:, at], dst_hot[:, at] = one_hots(src[:, at], dst[:, at])


def forward_kernel(
    slabs, count_ref, scalars, energy_ref, wg, own, first_ghost, second_ghost, dst, src_hot, dst_hot,
    message, atoms, rows_out, vec_out, dfilt_out, q_out,
    total, force_total,
):

    count = count_ref[0, 0]
    rank = scalars[0]
    box = slab_width * slabs
    table_t = weight(wg, 0)
    one_t = lhs_deep(radial_one_t(wg))
    two_t = lhs(weight(wg, 3))
    message_t = lhs(weight(wg, 5))
    update_f = update_weight_t(wg)
    update_t = lhs(update_f)
    update = lhs(update_f.T)
    readout = readout_column(wg)

    own = own[...]
    own_rows = own[:8]
    lane = iota((8, 128), 1)
    row = iota((8, 128), 0)
    ghost_rows = jnp.where((lane < G) == (rank % 2 == 1), first_ghost[...], second_ghost[...])
    atoms[OWN] = jnp.where((iota(own.shape, 0) == 7) & (iota(own.shape, 1) == 9), energy_ref[0], own)
    atoms[GHOST] = ghost_rows
    shift = jnp.where(lane < G, jnp.where(rank == 0, -box, 0.0), 0.0)
    shift = shift + jnp.where((lane >= G) & (lane < 2 * G), jnp.where(rank == slabs - 1, box, 0.0), 0.0)
    ghost_pos = ghost_rows + jnp.where(row == 0, shift, 0.0)
    ext = jnp.concatenate([own_rows, ghost_pos], axis=1)
    pieces = exact(jnp.where(iota((8, 256), 0) < 3, ext, 0.0))
    kinds = ext[3:4, :].astype(jnp.int32)
    kind_hot = (iota((128, 256), 0) == kinds).astype(f32)
    table_hi, table_rest = split(table_t)
    table_lo = (table_t - table_hi.astype(f32) - table_rest.astype(f32)).astype(bf16)
    kind_bf = kind_hot.astype(bf16)
    emb = mm(table_hi, kind_bf, NN) + mm(table_rest, kind_bf, NN) + mm(table_lo, kind_bf, NN)
    atoms[EMB_OWN] = emb[:, :A]
    atoms[EMB_GHOST] = emb[:, A:]
    projected = stack(wdot(message_t, stack(emb)))[:, :N]
    total[...] = jnp.zeros_like(total)
    centers = iota((K, EC), 0).astype(f32) * (cutoff / (K - 1))

    for i in range(CHUNKS):
        at = pl.ds(i * EC, EC)
        t = dst[:, at]
        hot_s = src_hot[:, at]
        hot_t = dst_hot[:, at]
        vec = whole(mm(pieces[:, :N], hot_s, NN) - mm(pieces[:, :A], hot_t, NN))
        vec_out[:, at] = vec
        square = jnp.sum(vec * vec, axis=0, keepdims=True)
        dist = jnp.sqrt(square)
        inverse = jnp.where(square > 0.0, 1.0 / jnp.where(square > 0.0, dist, 1.0), 0.0)
        ratio = jnp.minimum(dist / cutoff, 1.0)
        live = (t < count).astype(f32)
        inside = 1.0 - ratio * ratio
        gate = inside * inside * live
        dgate = inside * ratio * (-4.0 / cutoff) * live
        rows_out[0:1, at] = dist
        rows_out[1:2, at] = inverse
        rows_out[2:3, at] = gate
        rows_out[3:4, at] = dgate
        delta = dist - centers
        basis = jnp.exp(-spread * delta * delta)
        dbasis = (-2.0 * spread) * delta * basis
        a = mm(one_t, deep(stack(basis)), NN)
        da = mm(one_t, deep(stack(dbasis)), NN)
        sig, slope, second = silu_parts(a)
        f = wdot(two_t, stack(a * sig))
        df = wdot(two_t, stack(slope * da))
        filt = f * gate
        dfilt = df * gate + f * dgate
        q = fold_rows(mm(projected, hot_s, NN))
        dfilt_out[:, at] = dfilt
        q_out[:, at] = q
        total[...] += mm(stack(filt * q), hot_t, NT)

    hidden = emb[:, :A] + fold_rows(total[...]) * (1.0 / DEG)
    atoms[HIDDEN] = hidden
    rms = lax.rsqrt(jnp.mean(hidden * hidden, axis=0, keepdims=True) + 1e-05)
    z = wdot(update_t, stack(hidden * rms))
    atoms[Z] = z
    sig, slope, second = silu_parts(z)
    live_atom = (iota((1, A), 1) < count).astype(f32)
    weighted = readout * live_atom
    energy = jnp.sum(jnp.sum(weighted * (z * sig), axis=0, keepdims=True), axis=1, keepdims=True)
    dn = wdot(update, stack(weighted * slope))
    atoms[DN] = dn
    cube = rms * rms * rms * (1.0 / C)
    dh = rms * dn - hidden * (cube * jnp.sum(dn * hidden, axis=0, keepdims=True))
    atoms[DH] = dh
    dh_pieces = wide(dh * (1.0 / DEG))
    force_total[...] = jnp.zeros_like(force_total)

    stress = [jnp.zeros((8, 1), f32) for _ in range(3)]
    for i in range(CHUNKS):
        at = pl.ds(i * EC, EC)
        hot_s = src_hot[:, at]
        hot_t = dst_hot[:, at]
        back = mm(dh_pieces, twice(hot_t), NN)
        along = jnp.sum(back * (dfilt_out[:, at] * q_out[:, at]), axis=0, keepdims=True)
        vec = vec_out[:, at]
        slopes = vec * (along * rows_out[1:2, at])
        three = exact(slopes)
        force_total[:, :N] += mm(three, hot_s, NT)
        force_total[:, :A] -= mm(three, hot_t, NT)
        stress = [
            stress[j] + jnp.sum(slopes * vec[j : j + 1], axis=1, keepdims=True) for j in range(3)
        ]

    contrib = whole(force_total[...])
    atoms[CONTRIB_OWN] = contrib[:, :A]
    atoms[CONTRIB_GHOST] = contrib[:, A:]
    lists_hot = select_lists(own)
    outgoing = full_dot(contrib[:, :A], lists_hot, NN) + pltpu.roll(contrib[:, A:], 64, 1)
    to_right = (lane < G) | (lane >= 96)
    sums = jnp.zeros((8, 128), f32)
    for i in range(3):
        for j in range(3):
            sums = sums + jnp.where(lane == 3 * i + j, stress[j][i : i + 1], 0.0)
    sums = sums + jnp.where(lane == 9, energy, 0.0)
    right = lax.rem(rank + 1, slabs)
    left = lax.rem(rank + slabs - 1, slabs)
    for d in range(8):
        keep = (to_right & (right == d)) | (jnp.logical_not(to_right) & (left == d))
        message[d] = jnp.where(row == 3, sums, jnp.where(keep, outgoing, 0.0))[:4]


def backward_kernel(
    slabs, count_ref, scalars, wg, src, dst, received, atoms, rows_in, vec_in, dfilt_in, q_in,
    forces_far, energy_far, stress_far, keep, give, forces_out, energy_out, stress_out, sems,
    src_hot, dst_hot, grad, step_row, total, source_total, one_total, two_total,
):

    count = count_ref[0, 0]
    core = scalars[1]
    volume = slab_width * cross_area * slabs
    scale = 2.0 / (slabs * A)
    one_t = lhs_deep(radial_one_t(wg))
    two_f = weight(wg, 3)
    two_t = lhs(two_f)
    two = lhs(two_f.T)
    message_w = lhs(weight(wg, 5).T)
    update_f = update_weight_t(wg)
    update_t = lhs(update_f)
    update = lhs(update_f.T)
    readout = readout_column(wg)
    own = atoms[OWN]
    lists_hot = select_lists(own)
    lane = iota((8, 128), 1)
    row = iota((8, 128), 0)
    ghost = atoms[GHOST]

    got = jnp.sum(received[...], axis=0)
    got = jnp.concatenate([got, jnp.zeros_like(got)], axis=0)
    moved = jnp.where(row < 3, got, 0.0)
    energy = got[3:4, 9:10]
    inner = jnp.where(lane < 2 * G, pltpu.roll(moved, 64, 1), 0.0)
    force_own = -(atoms[CONTRIB_OWN] + full_dot(inner, lists_hot, NT))
    force_ghost = -(atoms[CONTRIB_GHOST] + jnp.where(lane < 2 * G, moved, 0.0))
    for i in range(3):
        forces_out[i] = force_own[i : i + 1]
        stress_out[i] = got[3:4, 3 * i : 3 * i + 3] / volume
    energy_out[...] = energy
    results = ((forces_out, forces_far), (energy_out, energy_far), (stress_out, stress_far))
    copies = [pltpu.make_async_copy(near, far, sems.at[k]) for k, (near, far) in enumerate(results)]
    for copy in copies:
        copy.start()
    own_ref = jnp.concatenate([own[4:8], jnp.zeros((4, 128), f32)], axis=0)
    ghost_ref = jnp.concatenate([ghost[4:8], jnp.zeros((4, 128), f32)], axis=0)
    factor = force_weight * scale
    cot_own = jnp.where((lane < count) & (row < 3), factor * (force_own - own_ref), 0.0)
    cot_ghost = jnp.where((lane < 2 * G) & (row < 3), factor * (force_ghost - ghost_ref), 0.0)
    cot = exact(jnp.concatenate([cot_own, cot_ghost], axis=1))
    stress_row = (2.0 * stress_weight / volume) * (got[3:4] / volume - own[7:8])
    stress_cot = [[stress_row[:, 3 * i + j : 3 * i + j + 1] for j in range(3)] for i in range(3)]
    energy_cot = (energy - own[7:8, 9:10]) * scale
    total[...] = jnp.zeros_like(total)

    for i in range(CHUNKS):
        at = pl.ds(i * EC, EC)
        hot_s, hot_t = one_hots(src[:, at], dst[:, at])
        src_hot[:, at] = hot_s
        dst_hot[:, at] = hot_t
        vec = vec_in[:, at]
        delta = whole(mm(cot[:, :A], hot_t, NN) - mm(cot[:, :N], hot_s, NN))
        along = jnp.sum(vec * delta, axis=0, keepdims=True)
        for r in range(3):
            inner_row = sum(stress_cot[r][j] * vec[j : j + 1] for j in range(3))
            along = along + vec[r : r + 1] * inner_row
        step = along * rows_in[1:2, at]
        step_row[:, at] = step
        total[...] += mm(stack(dfilt_in[:, at] * q_in[:, at] * step), hot_t, NT)

    hidden = atoms[HIDDEN]
    dn = atoms[DN]
    dh = atoms[DH]
    z = atoms[Z]
    moved_h = fold_rows(total[...]) * (1.0 / DEG)
    rms = lax.rsqrt(jnp.mean(hidden * hidden, axis=0, keepdims=True) + 1e-05)
    cube = rms * rms * rms
    cross = jnp.mean(hidden * moved_h, axis=0, keepdims=True)
    normed = hidden * rms
    moved_n = rms * moved_h - (cube * cross) * hidden
    moved_n2 = stack(moved_n)
    moved_z = wdot(update_t, moved_n2)
    sig, slope, second = silu_parts(z)
    live_atom = (iota((1, A), 1) < count).astype(f32)
    weighted = readout * live_atom
    z_bar = weighted * (energy_cot * slope + second * moved_z)
    z_bar = stack(z_bar)
    update_grad = fold(
        mm(
            jnp.concatenate([z_bar, stack(weighted * slope)], axis=1),
            jnp.concatenate([stack(normed), moved_n2], axis=1),
            NT,
        )
    )
    readout_grad = jnp.sum(live_atom * (energy_cot * (z * sig) + slope * moved_z), axis=1, keepdims=True)
    n_bar = wdot(update, z_bar)
    dn_h = jnp.sum(dn * hidden, axis=0, keepdims=True) * (1.0 / C)
    mix = (jnp.sum(n_bar * hidden, axis=0, keepdims=True) + jnp.sum(dn * moved_h, axis=0, keepdims=True)) * (1.0 / C)
    h_bar = (
        rms * n_bar
        + hidden * (3.0 * cube * rms * rms * cross * dn_h - cube * mix)
        - moved_h * (cube * dn_h)
        - dn * (cube * cross)
    )
    for h in range(8):
        grad[:, 7 + h, :] = update_grad[64 * h : 64 * h + 64]
    lane64 = iota((64, 128), 1)
    block = jnp.zeros((64, 128), f32)
    for h in range(8):
        block = block + jnp.where(lane64 == h, readout_grad[64 * h : 64 * h + 64], 0.0)
    grad[:, 15, :] = block

    both_pieces = jnp.concatenate([wide(h_bar * (1.0 / DEG)), wide(dh * (1.0 / DEG))], axis=0)
    source_total[...] = jnp.zeros_like(source_total)
    one_total[...] = jnp.zeros_like(one_total)
    two_total[...] = jnp.zeros_like(two_total)
    centers = iota((K, EC), 0).astype(f32) * (cutoff / (K - 1))

    for i in range(CHUNKS):
        at = pl.ds(i * EC, EC)
        hot_s = src_hot[:, at]
        hot_t = dst_hot[:, at]
        step = step_row[:, at]
        gate = rows_in[2:3, at]
        dgate = rows_in[3:4, at]
        both = mm(both_pieces, twice(hot_t), NN)
        m_bar = both[:C]
        dm_bar = both[C:]
        q = q_in[:, at]
        dq = dm_bar * q
        f_bar = stack(m_bar * q * gate + dq * (dgate * step))
        df_bar = stack(dq * gate)
        s_bar = wdot(two, f_bar)
        ds_bar = wdot(two, df_bar)
        delta = rows_in[0:1, at] - centers
        basis = jnp.exp(-spread * delta * delta)
        moved_basis = (-2.0 * spread) * delta * basis * step
        basis = stack(basis)
        moved_basis = stack(moved_basis)
        a = mm(one_t, deep(basis), NN)
        moved_a = mm(one_t, deep(moved_basis), NN)
        sig, slope, second = silu_parts(a)
        inner = stack(a * sig)
        filt = wdot(two_t, inner) * gate
        source_total[...] += mm(stack(m_bar * filt + dm_bar * (dfilt_in[:, at] * step)), hot_s, NT)
        two_total[...] += mm(
            jnp.concatenate([f_bar, df_bar], axis=1),
            jnp.concatenate([inner, stack(slope * moved_a)], axis=1),
            NT,
        )
        a_bar = stack(s_bar * slope + ds_bar * (second * moved_a))
        da_bar = stack(ds_bar * slope)
        one_total[...] += mm(
            jnp.concatenate([a_bar, da_bar], axis=1),
            jnp.concatenate([basis, moved_basis], axis=1),
            NT,
        )

    one_grad = fold(one_total[...])
    grad[:, 2, :] = jnp.concatenate([one_grad[:64], one_grad[64:]], axis=1)
    two_grad = fold(two_total[...])
    grad[:, 3, :] = two_grad[:64]
    grad[:, 4, :] = two_grad[64:]
    p_bar = fold_rows(source_total[...])
    p_bar = jnp.concatenate([p_bar, jnp.zeros((C, 256 - N), f32)], axis=1)
    p_pieces = stack(p_bar)
    emb = jnp.concatenate([atoms[EMB_OWN], atoms[EMB_GHOST]], axis=1)
    message_grad = fold(mm(p_pieces, stack(emb), NT))
    grad[:, 5, :] = message_grad[:64]
    grad[:, 6, :] = message_grad[64:]
    emb_bar = wdot(message_w, p_pieces)
    emb_bar = jnp.concatenate([emb_bar[:, :A] + h_bar, emb_bar[:, A:]], axis=1)
    kinds = jnp.concatenate([own[3:4], ghost[3:4]], axis=1).astype(jnp.int32)
    kind_hot = (iota((128, 256), 0) == kinds).astype(f32).astype(bf16)
    table_grad = fold_rows(mm(stack(emb_bar), kind_hot, NT))
    grad[:, 0, :] = table_grad[:64]
    grad[:, 1, :] = table_grad[64:]
    for j in range(32):
        keep[j] = grad[2 * j + core]
        give[j] = grad[2 * j + 1 - core]
    for copy in copies:
        copy.wait()


vmem = pl.BlockSpec(memory_space=pltpu.VMEM)
smem = pl.BlockSpec(memory_space=pltpu.SMEM)
far = pl.BlockSpec(memory_space=pl.ANY)
params_vmem = pltpu.CompilerParams(vmem_limit_bytes=32 * 1024 * 1024)


def shape(*dims, dtype=jnp.float32):
    return jax.ShapeDtypeStruct(dims, dtype)


def prepare(shards, *arrays):
    return pl.pallas_call(
        prepare_kernel,
        out_shape=[shape(16, 128), shape(8, 128), shape(shards, BLOCKS, 128)],
        in_specs=[vmem] * len(arrays),
        out_specs=[vmem] * 3,
        compiler_params=pltpu.CompilerParams(vmem_limit_bytes=60 * 1024 * 1024),
        name="prepare",
    )(*arrays)


def edge_hots(src, dst):
    return pl.pallas_call(
        hot_kernel,
        out_shape=[shape(N, E, dtype=bf16), shape(A, E, dtype=bf16)],
        in_specs=[vmem] * 2,
        out_specs=[vmem] * 2,
        compiler_params=params_vmem,
        name="edge_hots",
    )(src, dst)


def forward(slabs, counts, scalars, energy_ref, *arrays):
    return pl.pallas_call(
        functools.partial(forward_kernel, slabs),
        out_shape=[shape(8, 4, 128)] + [shape(*dims) for dims in KEPT],
        in_specs=[smem] * 3 + [vmem] * len(arrays),
        out_specs=[vmem] * (1 + len(KEPT)),
        scratch_shapes=[
            pltpu.VMEM((2 * C, A), f32),
            pltpu.VMEM((24, 256), f32),
        ],
        compiler_params=params_vmem,
        name="energy_slopes",
    )(counts, scalars, energy_ref, *arrays)


def backward(slabs, counts, scalars, *arrays):
    outs = [shape(3, 1, A), shape(1, 1), shape(3, 1, 3), shape(32, BLOCKS, 128), shape(32, BLOCKS, 128)]
    return pl.pallas_call(
        functools.partial(backward_kernel, slabs),
        out_shape=outs,
        in_specs=[smem] * 2 + [vmem] * len(arrays),
        out_specs=[far] * 3 + [vmem] * 2,
        scratch_shapes=[pltpu.VMEM(out.shape, f32) for out in outs[:3]]
        + [
            pltpu.SemaphoreType.DMA((3,)),
            pltpu.VMEM((N, E), bf16),
            pltpu.VMEM((A, E), bf16),
            pltpu.VMEM((64, BLOCKS, 128), f32),
            pltpu.VMEM((1, E), f32),
            pltpu.VMEM((2 * C, A), f32),
            pltpu.VMEM((2 * C, N), f32),
            pltpu.VMEM((2 * C, 2 * K), f32),
            pltpu.VMEM((2 * C, 2 * C), f32),
        ],
        compiler_params=params_vmem,
        name="weight_gradients",
    )(counts, scalars, *arrays)


def from_blocks(y):
    two = jnp.concatenate([y[0:2, :100], y[2].reshape(2, 64), y[3:5], y[5:7]], axis=1)
    return jnp.concatenate([two.T.reshape(-1), y[7:15].T.reshape(-1), y[15, :56]])


def decay(params, moment_one, moment_two):
    return params - (0.001 * 0.01) * params, 0.9 * moment_one, 0.999 * moment_two


def adam(params, moment_one, moment_two, grad):
    new_moment_one = moment_one + 0.1 * grad
    new_moment_two = moment_two + 0.001 * grad * grad
    corrected_one = new_moment_one / (1.0 - 0.9**STEP)
    corrected_two = new_moment_two / (1.0 - 0.999**STEP)
    new_params = params - 0.001 * (corrected_one / (jnp.sqrt(corrected_two) + 1e-08))
    return new_params, new_moment_one, new_moment_two


def body(
    positions,
    species,
    counts,
    source,
    target,
    send_left,
    send_right,
    energy_ref,
    force_ref,
    stress_ref,
    params,
    moment_one,
    moment_two,
):
    shards = lax.axis_size("dp")
    slabs = lax.axis_size("graph")
    rank = lax.axis_index("graph")
    index = lax.axis_index("dp")
    core = index % 2
    scalars = jnp.stack([rank, core]).astype(jnp.int32)
    own, outgoing, blocks = prepare(
        shards,
        positions.reshape(3, 1, A),
        species[0],
        force_ref.reshape(3, 1, A),
        send_left[0],
        send_right[0],
        stress_ref.reshape(3, 1, 3),
        params,
    )
    wg = lax.all_to_all(blocks, "dp", 0, 0, tiled=True)
    first = lax.ppermute(outgoing, "graph", [(i, i ^ 1) for i in range(slabs)])
    second = lax.ppermute(
        outgoing, "graph", [(i, (i + (1 if i % 2 else slabs - 1)) % slabs) for i in range(slabs)]
    )
    wg, decayed, hots = lax.optimization_barrier(
        (wg, decay(params, moment_one, moment_two), edge_hots(source[0], target[0]))
    )
    message, *kept = forward(
        slabs, counts, scalars, energy_ref, wg, own, first, second, target[0], *hots
    )
    received = lax.all_to_all(message, "graph", 0, 0, tiled=True)
    forces, energy, stress, keep, give = backward(
        slabs, counts, scalars, wg, source[0], target[0], received, *kept
    )
    pair = keep + lax.ppermute(give, "dp", [(i, i ^ 1) for i in range(shards)])
    chips = [list(range(c, shards, 2)) for c in range(2)]
    within = jnp.sum(
        lax.all_to_all(pair, "dp", 0, 0, tiled=True, axis_index_groups=chips), axis=0
    )
    copies = jnp.broadcast_to(within[None], (slabs, BLOCKS, 128))
    grad = from_blocks(jnp.sum(lax.all_to_all(copies, "graph", 0, 0, tiled=True), axis=0))
    new_params, new_moment_one, new_moment_two = adam(*decayed, grad)
    return (
        new_params,
        new_moment_one,
        new_moment_two,
        forces.reshape(1, 1, 3, A),
        energy.reshape(1),
        stress.reshape(1, 3, 3),
    )


def solution(mesh):
    in_specs = (
        P("dp", "graph", None, None),
        P("dp", "graph", None),
        P("dp", "graph"),
        P("dp", "graph", None),
        P("dp", "graph", None),
        P("dp", "graph", None),
        P("dp", "graph", None),
        P("dp"),
        P("dp", "graph", None, None),
        P("dp", None, None),
        P("dp"),
        P("dp"),
        P("dp"),
    )
    out_specs = (
        P("dp"),
        P("dp"),
        P("dp"),
        P("dp", "graph", None, None),
        P("dp"),
        P("dp", None, None),
    )
    return jax.shard_map(body, mesh=mesh, in_specs=in_specs, out_specs=out_specs, check_vma=False)
```
